32 devices in a mesh: parts: 2 (over y), band: 4 (over z), feat: 4 (over x, core).
Axes of the slice: x: 2, y: 2, z: 4, core: 2. Of those that a mesh axis runs over, the one named last changes fastest.
Arguments:
- x_grid: bfloat16 [4096, 474], P(('parts', 'band')), parts along dimension 0, may hold values from -6 to 6
- mesh_pos: float32 [3, 2048], P(None, 'band'), may hold values from -4 to 4
- pos_weight: float32 [3, 512], replicated, may hold values from -3.5 to 3.5
- embed_in: bfloat16 [474, 512], P(None, 'feat'), may hold values from -0.25 to 0.25
- pair_in: bfloat16 [8, 1024, 512], P(None, None, 'feat'), may hold values from -0.1875 to 0.1875
- pair_out: bfloat16 [9, 512, 512], P(None, 'feat'), may hold values from -0.25 to 0.25
- hidden_bias: float32 [9, 512], P(None, 'feat'), may hold values from -1 to 1
- norm_gain: float32 [9, 512], replicated, may hold values from 0.1 to 1.9
- norm_shift: float32 [9, 512], replicated, may hold values from -3 to 3
- head: bfloat16 [512, 227], replicated, may hold values from -0.25 to 0.25
- g2m_take: int32 [4, 4, 256], P('band'), may hold values from 0 to 511, as said below
- g2m_from: int32 [4096], P('band'), may hold values from 0 to 1023, as said below
- g2m_to: int32 [4096], P('band'), may hold values from 0 to 511, as said below
- m2m_take: int32 [4, 4, 512], P('band'), may hold values from 0 to 511, as said below
- m2m_from: int32 [8192], P('band'), may hold values from 0 to 2047, as said below
- m2m_to: int32 [8192], P('band'), may hold values from 0 to 511, as said below
- m2g_take: int32 [4, 4, 384], P('band'), may hold values from 0 to 511, as said below
- m2g_from: int32 [6144], P('band'), may hold values from 0 to 1535, as said below
Outputs:
- forecast: float32 [4096, 227], P(('parts', 'band', 'feat')), parts along dimension 0
The draws below stay inside these ranges and needn't reach their ends.
There are 2 independent parts, one for each index of `parts`. The reference program is written for one: setup_inputs(seed, part) draws one part's arguments, and reference() takes and returns one part's arrays. A program takes and returns all parts, laid end to end along the dimension named above; an argument that names none is the same for every part. Nothing has to cross between parts.
Inputs may be any that keep to these rules, and one draw needn't show every extreme that they name: `g2m_take`: every value names a row of the sending device; a slot may repeat a row. `m2m_take`: every value names a node of the sending partition; a slot may repeat a node. `m2g_take`: every value names a node of the sending partition; a slot may repeat a node. `g2m_from`: A slot index on the receiving device, source device major (256 slots per source). From each source the device's edges name exactly the slots below a count for that pair, which lies between half of 256 (rounded up) and 256; one receiving device has the full count from every source. The remaining slots are unused, though their take entries are valid rows. `m2m_from`: as for g2m_from, with 512 slots per source. `m2g_from`: as for g2m_from, with 384 slots per source. `g2m_to`: on each device, edges k * 128 * 2 to (k + 1) * 128 * 2 - 1 go to nodes of receiver block k (nodes k * 128 to (k + 1) * 128 - 1), in non-decreasing order; every node receives at least one edge. `m2m_to`: on each device, edges k * 128 * 4 to (k + 1) * 128 * 4 - 1 go to nodes of receiver block k, in non-decreasing order; every node receives at least one edge.
All inputs are finite; a program needn't handle non-finite values.
Results may differ from the reference program's by a relative error of at most 0.017.
Values may be sent and summed in bfloat16 or wider, within the bound.
No kernel may reach another device: no remote copies, remote signals or barrier semaphores. Data moves between devices by JAX's collectives and lax.ppermute only.
A program may use at most 64 MiB of HBM per device.

```python
import jax
import jax.numpy as jnp
from jax import lax

L = 512
HID = 512
F_IN = 474
F_OUT = 227
GD = 512
MD = 512
LAYERS = 2
NODE_BLK = 128
G2M_DEG = 2
M2M_DEG = 4
MLPS = 8
NG = 2048
NM = 2048
E1 = 1024
E2 = 2048
E3 = 1536
CAP1 = 256
CAP2 = 512
CAP3 = 384
N_BAND = 4


def shuffle_row(row_key, row_values):
    return jax.random.permutation(row_key, row_values)


def route_tables(key, salt, capacity, source_rows, edge_count):
    key = jax.random.fold_in(key, salt)
    take_key, count_key, full_key, pick_key, order_key = jax.random.split(key, 5)
    bands = N_BAND
    take_rows = jax.random.randint(take_key, (bands, bands, capacity), 0, source_rows, dtype=jnp.int32)
    take_rows = take_rows.at[0, 0, 0].set(0)
    take_rows = take_rows.at[bands - 1, bands - 1, capacity - 1].set(source_rows - 1)
    counts = jax.random.randint(count_key, (bands, bands), (capacity + 1) // 2, capacity + 1, dtype=jnp.int32)
    full_dest = jax.random.randint(full_key, (), 0, bands, dtype=jnp.int32)
    column = jnp.arange(bands, dtype=jnp.int32)
    counts = jnp.where(column[None, :] == full_dest, capacity, counts)
    slots = jnp.arange(bands * capacity, dtype=jnp.int32)
    live = slots[None, :] % capacity < counts.T[:, slots // capacity]
    ranking = jnp.argsort(1 - live.astype(jnp.int32), axis=1, stable=True).astype(jnp.int32)
    live_count = jnp.sum(live.astype(jnp.int32), axis=1)
    edge_ids = jnp.arange(edge_count, dtype=jnp.int32)
    extra = jax.random.randint(pick_key, (bands, edge_count), 0, live_count[:, None], dtype=jnp.int32)
    picks = jnp.where(edge_ids[None, :] < live_count[:, None], edge_ids[None, :], extra)
    senders = jnp.take_along_axis(ranking, picks, axis=1)
    order_keys = jax.random.split(order_key, bands)
    shuffled = jax.vmap(shuffle_row)(order_keys, senders)
    return (take_rows, shuffled.reshape(-1).astype(jnp.int32))


def receiver_table(key, degree):
    bands = N_BAND
    blocks = MD // NODE_BLK
    base = jnp.broadcast_to(jnp.arange(NODE_BLK, dtype=jnp.int32), (bands, blocks, NODE_BLK))
    extra = jax.random.randint(key, (bands, blocks, (degree - 1) * NODE_BLK), 0, NODE_BLK, dtype=jnp.int32)
    within = jnp.sort(jnp.concatenate([base, extra], axis=2), axis=2)
    offsets = (jnp.arange(blocks, dtype=jnp.int32) * NODE_BLK)[None, :, None]
    return (within + offsets).reshape(-1).astype(jnp.int32)


def draw_g2m_take(key, part):
    return route_tables(key, 11, CAP1, GD, E1)[0]


def draw_g2m_from(key, part):
    return route_tables(key, 11, CAP1, GD, E1)[1]


def draw_m2m_take(key, part):
    return route_tables(key, 12, CAP2, MD, E2)[0]


def draw_m2m_from(key, part):
    return route_tables(key, 12, CAP2, MD, E2)[1]


def draw_m2g_take(key, part):
    return route_tables(key, 13, CAP3, MD, E3)[0]


def draw_m2g_from(key, part):
    return route_tables(key, 13, CAP3, MD, E3)[1]


def draw_g2m_to(key, part):
    key = jax.random.fold_in(key, 21)
    return receiver_table(key, G2M_DEG)


def draw_m2m_to(key, part):
    key = jax.random.fold_in(key, 22)
    return receiver_table(key, M2M_DEG)


def block_scale(own_key, dims, shards, smallest, high):
    loudness, own = 1.0, jax.random.fold_in(own_key, 6)
    for position, parts in shards:
        steps = jnp.exp(jax.random.uniform(jax.random.fold_in(own, position), (parts,), jnp.float32, smallest / len(shards), high / len(shards)))
        loudness = loudness * jnp.repeat(steps, dims[position] // parts).reshape([-1 if axis == position else 1 for axis in range(len(dims))])
    return loudness


def bell_draw(rng, dims, deviation, reach, pieces=(), kind=jnp.bfloat16):
    drawn = jax.random.normal(rng, dims, jnp.float32) * deviation
    if len(pieces) > 0:
        drawn = block_scale(rng, dims, pieces, -0.22, 0.18) * drawn
    return jnp.clip(drawn, min=-reach, max=reach).astype(kind)


def setup_inputs(seed: int = 0, part: int = 0) -> dict:
    streams_of = jax.random.split(jax.random.key(seed), 19)
    part_splits = jax.random.split(jax.random.fold_in(streams_of[18], part), 19)
    x_grid = bell_draw(part_splits[0], (NG, F_IN), 1.0, 6.0, ((0, 4),))
    mesh_pos = bell_draw(streams_of[1], (3, NM), 1.0, 4.0, ((1, 4),), jnp.float32)
    pos_weight = bell_draw(streams_of[2], (3, L), 3 ** -0.5, 3.5, (), jnp.float32)
    embed_in = bell_draw(streams_of[3], (F_IN, HID), F_IN ** -0.5, 0.25, ((1, 4),))
    pair_in = bell_draw(streams_of[4], (MLPS, 2 * L, HID), (2 * L) ** -0.5, 0.1875, ((2, 4),))
    pair_out = bell_draw(streams_of[5], (MLPS + 1, HID, L), HID ** -0.5, 0.25, ((1, 4),))
    hidden_bias = jnp.clip(jax.random.uniform(streams_of[6], (MLPS + 1, HID), jnp.float32, -1.0, 1.0) * block_scale(streams_of[6], (MLPS + 1, HID), ((1, 4),), -0.4, 0.0), -1.0, 1.0)
    norm_gain = jnp.clip(1.0 + 0.18 * jax.random.normal(streams_of[7], (MLPS + 1, L), jnp.float32), 0.1, 1.9)
    norm_shift = bell_draw(streams_of[8], (MLPS + 1, L), 0.5, 3.0, (), jnp.float32)
    head = bell_draw(streams_of[9], (L, F_OUT), L ** -0.5, 0.25)
    g2m_take = draw_g2m_take(jax.random.fold_in(streams_of[18], 71), part)
    g2m_from = draw_g2m_from(jax.random.fold_in(streams_of[18], 71), part)
    g2m_to = draw_g2m_to(jax.random.fold_in(streams_of[18], 71), part)
    m2m_take = draw_m2m_take(jax.random.fold_in(streams_of[18], 71), part)
    m2m_from = draw_m2m_from(jax.random.fold_in(streams_of[18], 71), part)
    m2m_to = draw_m2m_to(jax.random.fold_in(streams_of[18], 71), part)
    m2g_take = draw_m2g_take(jax.random.fold_in(streams_of[18], 71), part)
    m2g_from = draw_m2g_from(jax.random.fold_in(streams_of[18], 71), part)
    return {"x_grid": x_grid, "mesh_pos": mesh_pos, "pos_weight": pos_weight, "embed_in": embed_in, "pair_in": pair_in, "pair_out": pair_out, "hidden_bias": hidden_bias, "norm_gain": norm_gain, "norm_shift": norm_shift, "head": head, "g2m_take": g2m_take, "g2m_from": g2m_from, "g2m_to": g2m_to, "m2m_take": m2m_take, "m2m_from": m2m_from, "m2m_to": m2m_to, "m2g_take": m2g_take, "m2g_from": m2g_from}


EPSILON = 1e-05

def layer_norm(values, gain_row, shift_row):
    average = lax.optimization_barrier(jnp.mean(values, axis=-1, keepdims=True))
    centered = values - average
    variance = lax.optimization_barrier(jnp.mean(centered * centered, axis=-1, keepdims=True))
    return centered * lax.rsqrt(variance + EPSILON) * gain_row + shift_row

def finish_section(hidden, section_id, pair_out, norm_gain, norm_shift):
    summed = jnp.dot(hidden, pair_out[section_id], preferred_element_type=jnp.float32)
    return layer_norm(summed, norm_gain[section_id], norm_shift[section_id])

def sender_rows(take_rows, senders, edge_count, source_rows):
    capacity = take_rows.shape[2]
    dest_band = jnp.arange(senders.shape[0], dtype=jnp.int32) // edge_count
    source = senders // capacity
    slot_index = senders % capacity
    local_row = take_rows[source, dest_band, slot_index]
    return (source * source_rows + local_row).astype(jnp.int32)

def reference(x_grid, mesh_pos, pos_weight, embed_in, pair_in, pair_out, hidden_bias, norm_gain, norm_shift, head, g2m_take, g2m_from, g2m_to, m2m_take, m2m_from, m2m_to, m2g_take, m2g_from):
    embed_id = MLPS

    def edge_messages(section_id, send_latent, send_rows, recv_latent, recv_rows):
        weights = pair_in[section_id]
        send_part = jnp.dot(send_latent, weights[:L], preferred_element_type=jnp.float32)
        recv_part = jnp.dot(recv_latent, weights[L:], preferred_element_type=jnp.float32)
        preact = send_part[send_rows] + recv_part[recv_rows] + hidden_bias[section_id]
        hidden = jax.nn.silu(preact).astype(jnp.bfloat16)
        return finish_section(hidden, section_id, pair_out, norm_gain, norm_shift).astype(jnp.bfloat16)

    def node_update(section_id, latent, aggregate):
        weights = pair_in[section_id]
        preact = jnp.dot(latent, weights[:L], preferred_element_type=jnp.float32) + jnp.dot(aggregate, weights[L:], preferred_element_type=jnp.float32) + hidden_bias[section_id]
        hidden = jax.nn.silu(preact).astype(jnp.bfloat16)
        return latent.astype(jnp.float32) + finish_section(hidden, section_id, pair_out, norm_gain, norm_shift)

    def mesh_sum(messages, receivers):
        return jax.ops.segment_sum(messages.astype(jnp.float32), receivers, num_segments=NM).astype(jnp.bfloat16)
    preact = jnp.dot(x_grid, embed_in, preferred_element_type=jnp.float32) + hidden_bias[embed_id]
    grid_latent = finish_section(jax.nn.silu(preact).astype(jnp.bfloat16), embed_id, pair_out, norm_gain, norm_shift).astype(jnp.bfloat16)
    mesh_latent = mesh_pos[0][:, None] * pos_weight[0][None, :] + mesh_pos[1][:, None] * pos_weight[1][None, :]
    mesh_latent = (mesh_latent + mesh_pos[2][:, None] * pos_weight[2][None, :]).astype(jnp.bfloat16)
    g2m_recv = jnp.arange(N_BAND * E1, dtype=jnp.int32) // E1 * MD + g2m_to
    messages = edge_messages(0, grid_latent, sender_rows(g2m_take, g2m_from, E1, GD), mesh_latent, g2m_recv)
    aggregate = mesh_sum(messages, g2m_recv)
    mesh_latent = node_update(1, mesh_latent, aggregate).astype(jnp.bfloat16)
    m2m_recv = jnp.arange(N_BAND * E2, dtype=jnp.int32) // E2 * MD + m2m_to
    m2m_send = sender_rows(m2m_take, m2m_from, E2, MD)
    for layer_id in range(LAYERS):
        section_id = 2 + 2 * layer_id
        messages = edge_messages(section_id, mesh_latent, m2m_send, mesh_latent, m2m_recv)
        aggregate = mesh_sum(messages, m2m_recv)
        mesh_latent = node_update(section_id + 1, mesh_latent, aggregate).astype(jnp.bfloat16)
    section_id = 2 * LAYERS + 2
    m2g_recv = jnp.arange(N_BAND * E3, dtype=jnp.int32) // 3
    messages = edge_messages(section_id, mesh_latent, sender_rows(m2g_take, m2g_from, E3, MD), grid_latent, m2g_recv)
    grid_sum = messages.astype(jnp.float32).reshape(NG, 3, L).sum(axis=1).astype(jnp.bfloat16)
    final_latent = node_update(section_id + 1, grid_latent, grid_sum).astype(jnp.bfloat16)
    return jnp.dot(final_latent, head, preferred_element_type=jnp.float32)
```

```python
import jax
import jax.numpy as jnp
from jax import lax
from jax.sharding import PartitionSpec as P

LAYERS = 2
EPSILON = 1e-05


def layer_norm(values, gain_row, shift_row):
    average = jnp.mean(values, axis=-1, keepdims=True)
    centered = values - average
    variance = jnp.mean(centered * centered, axis=-1, keepdims=True)
    return centered * lax.rsqrt(variance + EPSILON) * gain_row + shift_row


def local(
    x_grid,
    mesh_pos,
    pos_weight,
    embed_in,
    pair_in,
    pair_out,
    hidden_bias,
    norm_gain,
    norm_shift,
    head,
    g2m_take,
    g2m_from,
    g2m_to,
    m2m_take,
    m2m_from,
    m2m_to,
    m2g_take,
    m2g_from,
):
    quarters = lax.axis_size("feat")
    bands = lax.axis_size("band")
    feat_index = lax.axis_index("feat")
    band_index = lax.axis_index("band")
    latent = norm_gain.shape[1]
    embed_id = pair_out.shape[0] - 1
    band_mesh = mesh_pos.shape[1]
    band_grid = x_grid.shape[0]
    mesh_rows = band_mesh // quarters
    grid_rows = band_grid // quarters

    def own(full, axis=0):
        count = full.shape[axis] // quarters
        return lax.dynamic_slice_in_dim(full, feat_index * count, count, axis)

    bias = lax.all_gather(hidden_bias, "feat", axis=1, tiled=True)
    embed_w = lax.all_gather(embed_in, "feat", axis=0, tiled=False)
    out_w = {}
    in_w = {}
    out_w[embed_id] = lax.all_gather(pair_out[embed_id], "feat", axis=0, tiled=True)
    for s in range(embed_id):
        in_w[s] = lax.all_gather(pair_in[s], "feat", axis=0, tiled=False)
        out_w[s] = lax.all_gather(pair_out[s], "feat", axis=0, tiled=True)

    def sender_ids(take, senders, source_rows):
        cap = take.shape[2]
        table = lax.all_to_all(take[0], "band", split_axis=0, concat_axis=0, tiled=True)
        rows = table + (jnp.arange(bands, dtype=jnp.int32) * source_rows)[:, None]
        return jnp.take(rows.reshape(-1), own(senders), axis=0)

    g2m_ids = sender_ids(g2m_take, g2m_from, band_grid)
    m2m_ids = sender_ids(m2m_take, m2m_from, band_mesh)
    m2g_ids = sender_ids(m2g_take, m2g_from, band_mesh)

    def first(rows, weights):
        return jnp.concatenate(
            [jnp.dot(rows, weights[f], preferred_element_type=jnp.float32) for f in range(quarters)],
            axis=1,
        )

    def finish(preact, section_id):
        hidden = jax.nn.silu(preact + bias[section_id]).astype(jnp.bfloat16)
        summed = jnp.dot(hidden, out_w[section_id], preferred_element_type=jnp.float32)
        return layer_norm(summed, norm_gain[section_id], norm_shift[section_id])

    def everyone(rows):
        return lax.all_gather(rows, ("band", "feat"), axis=0, tiled=True)

    def edges(section_id, table, ids, receiver_latent, spread_receiver):
        send_part = first(jnp.take(table, ids, axis=0), in_w[section_id][:, :latent])
        recv_part = spread_receiver(first(receiver_latent, in_w[section_id][:, latent:]))
        return finish(send_part + recv_part, section_id).astype(jnp.bfloat16)

    def node_update(section_id, own_latent, aggregate):
        preact = first(own_latent, in_w[section_id][:, :latent]) + first(
            aggregate, in_w[section_id][:, latent:]
        )
        return (own_latent.astype(jnp.float32) + finish(preact, section_id)).astype(jnp.bfloat16)

    def mesh_section(section_id, table, ids, receivers_all, own_latent):
        receivers = own(receivers_all) - feat_index * mesh_rows
        messages = edges(
            section_id, table, ids, own_latent, lambda part: jnp.take(part, receivers, axis=0)
        )
        onehot = (
            receivers[None, :] == jnp.arange(mesh_rows, dtype=jnp.int32)[:, None]
        ).astype(jnp.bfloat16)
        aggregate = jnp.dot(onehot, messages, preferred_element_type=jnp.float32)
        return node_update(section_id + 1, own_latent, aggregate.astype(jnp.bfloat16))

    own_grid = finish(first(own(x_grid), embed_w), embed_id).astype(jnp.bfloat16)
    own_pos = own(mesh_pos, 1)
    mesh = own_pos[0][:, None] * pos_weight[0][None, :] + own_pos[1][:, None] * pos_weight[1][None, :]
    mesh = (mesh + own_pos[2][:, None] * pos_weight[2][None, :]).astype(jnp.bfloat16)
    mesh = mesh_section(0, everyone(own_grid), g2m_ids, g2m_to, mesh)
    for layer_id in range(LAYERS):
        mesh = mesh_section(2 + 2 * layer_id, everyone(mesh), m2m_ids, m2m_to, mesh)
    section_id = 2 * LAYERS + 2
    messages = edges(
        section_id, everyone(mesh), m2g_ids, own_grid, lambda part: jnp.repeat(part, 3, axis=0)
    )
    grid_sum = messages.astype(jnp.float32).reshape(-1, 3, latent).sum(axis=1).astype(jnp.bfloat16)
    final_latent = node_update(section_id + 1, own_grid, grid_sum)
    return jnp.dot(final_latent, head, preferred_element_type=jnp.float32)


def solution(mesh):
    return jax.shard_map(
        local,
        mesh=mesh,
        in_specs=(
            P(("parts", "band"), None),
            P(None, "band"),
            P(),
            P(None, "feat"),
            P(None, None, "feat"),
            P(None, "feat", None),
            P(None, "feat"),
            P(),
            P(),
            P(),
            P("band", None, None),
            P("band"),
            P("band"),
            P("band", None, None),
            P("band"),
            P("band"),
            P("band", None, None),
            P("band"),
        ),
        out_specs=P(("parts", "band", "feat"), None),
        check_vma=False,
    )
```

```python
import jax
import jax.numpy as jnp
from jax import lax
from jax.sharding import PartitionSpec as P

LAYERS = 2
EPSILON = 1e-05


def layer_norm(values, gain_row, shift_row):
    average = jnp.mean(values, axis=-1, keepdims=True)
    centered = values - average
    variance = jnp.mean(centered * centered, axis=-1, keepdims=True)
    return centered * lax.rsqrt(variance + EPSILON) * gain_row + shift_row


def local(
    x_grid,
    mesh_pos,
    pos_weight,
    embed_in,
    pair_in,
    pair_out,
    hidden_bias,
    norm_gain,
    norm_shift,
    head,
    g2m_take,
    g2m_from,
    g2m_to,
    m2m_take,
    m2m_from,
    m2m_to,
    m2g_take,
    m2g_from,
):
    quarters = lax.axis_size("feat")
    bands = lax.axis_size("band")
    feat_index = lax.axis_index("feat")
    band_index = lax.axis_index("band")
    latent = norm_gain.shape[1]
    embed_id = pair_out.shape[0] - 1
    band_mesh = mesh_pos.shape[1]
    band_grid = x_grid.shape[0]
    mesh_rows = band_mesh // quarters
    grid_rows = band_grid // quarters

    def own(full, axis=0):
        count = full.shape[axis] // quarters
        return lax.dynamic_slice_in_dim(full, feat_index * count, count, axis)

    bits = [1 << b for b in reversed(range(quarters.bit_length() - 1))]

    def swap(value, bit):
        return lax.ppermute(value, "feat", [(f, f ^ bit) for f in range(quarters)])

    def pieces(value):
        parts = [value]
        for bit in bits:
            parts = parts + [swap(part, bit) for part in parts]
        return parts

    order = [0]
    for bit in bits:
        order = order + [other ^ bit for other in order]
    slot_of = jnp.array([order.index(f) for f in range(quarters)], jnp.int32)

    bias = jnp.concatenate(pieces(hidden_bias), axis=1)
    embed_w = pieces(embed_in)
    out_w = {embed_id: jnp.concatenate(pieces(pair_out[embed_id]), axis=0)}
    in_w = {}
    for s in range(0, embed_id, 2):
        in_parts = pieces(pair_in[s : s + 2])
        out_parts = pieces(pair_out[s : s + 2])
        for t in range(2):
            in_w[s + t] = [part[t] for part in in_parts]
            out_w[s + t] = jnp.concatenate([part[t] for part in out_parts], axis=0)

    tables = lax.all_to_all(
        jnp.concatenate([g2m_take[0], m2m_take[0], m2g_take[0]], axis=1),
        "band", split_axis=0, concat_axis=0, tiled=True,
    )

    def sender_ids(begin, take, senders, source_rows):
        cap = take.shape[2]
        count = source_rows // quarters
        rows = tables[:, begin : begin + cap]
        slot = jnp.take(slot_of, (rows // count) ^ feat_index, axis=0)
        source = jnp.arange(bands, dtype=jnp.int32)[:, None]
        rows = slot * (bands * count) + source * count + rows % count
        return jnp.take(rows.reshape(-1), own(senders), axis=0)

    g2m_ids = sender_ids(0, g2m_take, g2m_from, band_grid)
    m2m_ids = sender_ids(g2m_take.shape[2], m2m_take, m2m_from, band_mesh)
    m2g_ids = sender_ids(g2m_take.shape[2] + m2m_take.shape[2], m2g_take, m2g_from, band_mesh)

    def first(rows, weights):
        return jnp.concatenate(
            [jnp.dot(rows, weights[f], preferred_element_type=jnp.float32) for f in range(quarters)],
            axis=1,
        )

    def finish(preact, section_id):
        hidden = jax.nn.silu(preact + bias[section_id]).astype(jnp.bfloat16)
        summed = jnp.dot(hidden, out_w[section_id], preferred_element_type=jnp.float32)
        return layer_norm(summed, norm_gain[section_id], norm_shift[section_id])

    def everyone(rows):
        parts = [rows]
        for bit in bits[:-1]:
            parts = parts + [swap(part, bit) for part in parts]
        parts = [lax.all_gather(part, "band", axis=0, tiled=True) for part in parts]
        parts = parts + [swap(part, bits[-1]) for part in parts]
        return jnp.concatenate(parts, axis=0)

    def edges(section_id, table, ids, receiver_latent, spread_receiver):
        send_part = first(jnp.take(table, ids, axis=0), [w[:latent] for w in in_w[section_id]])
        recv_part = spread_receiver(first(receiver_latent, [w[latent:] for w in in_w[section_id]]))
        return finish(send_part + recv_part, section_id).astype(jnp.bfloat16)

    def node_update(section_id, own_latent, aggregate):
        preact = first(own_latent, [w[:latent] for w in in_w[section_id]]) + first(
            aggregate, [w[latent:] for w in in_w[section_id]]
        )
        return (own_latent.astype(jnp.float32) + finish(preact, section_id)).astype(jnp.bfloat16)

    def mesh_section(section_id, table, ids, receivers_all, own_latent):
        receivers = own(receivers_all) - feat_index * mesh_rows
        messages = edges(
            section_id, table, ids, own_latent, lambda part: jnp.take(part, receivers, axis=0)
        )
        onehot = (
            receivers[None, :] == jnp.arange(mesh_rows, dtype=jnp.int32)[:, None]
        ).astype(jnp.bfloat16)
        aggregate = jnp.dot(onehot, messages, preferred_element_type=jnp.float32)
        return node_update(section_id + 1, own_latent, aggregate.astype(jnp.bfloat16))

    own_grid = finish(first(own(x_grid), embed_w), embed_id).astype(jnp.bfloat16)
    own_pos = own(mesh_pos, 1)
    mesh = own_pos[0][:, None] * pos_weight[0][None, :] + own_pos[1][:, None] * pos_weight[1][None, :]
    mesh = (mesh + own_pos[2][:, None] * pos_weight[2][None, :]).astype(jnp.bfloat16)
    mesh = mesh_section(0, everyone(own_grid), g2m_ids, g2m_to, mesh)
    for layer_id in range(LAYERS):
        mesh = mesh_section(2 + 2 * layer_id, everyone(mesh), m2m_ids, m2m_to, mesh)
    section_id = 2 * LAYERS + 2
    messages = edges(
        section_id, everyone(mesh), m2g_ids, own_grid, lambda part: jnp.repeat(part, 3, axis=0)
    )
    grid_sum = messages.astype(jnp.float32).reshape(-1, 3, latent).sum(axis=1).astype(jnp.bfloat16)
    final_latent = node_update(section_id + 1, own_grid, grid_sum)
    return jnp.dot(final_latent, head, preferred_element_type=jnp.float32)


def solution(mesh):
    return jax.shard_map(
        local,
        mesh=mesh,
        in_specs=(
            P(("parts", "band"), None),
            P(None, "band"),
            P(),
            P(None, "feat"),
            P(None, None, "feat"),
            P(None, "feat", None),
            P(None, "feat"),
            P(),
            P(),
            P(),
            P("band", None, None),
            P("band"),
            P("band"),
            P("band", None, None),
            P("band"),
            P("band"),
            P("band", None, None),
            P("band"),
        ),
        out_specs=P(("parts", "band", "feat"), None),
        check_vma=False,
    )
```

```python
import functools

import jax
import jax.numpy as jnp
from jax import lax
from jax.experimental import pallas as pl
from jax.experimental.pallas import tpu as pltpu
from jax.sharding import PartitionSpec as P

LAYERS = 2
EPSILON = 1e-05
CHUNK = 2048
F32 = jnp.float32
BF16 = jnp.bfloat16


def layer_norm(values, gain_row, shift_row):
    average = jnp.mean(values, axis=-1, keepdims=True)
    centered = values - average
    variance = jnp.mean(centered * centered, axis=-1, keepdims=True)
    return centered * lax.rsqrt(variance + EPSILON) * gain_row + shift_row


def silu(values):
    return 0.5 * values * (1.0 + jnp.tanh(0.5 * values))


def dot(a, b):
    return jnp.dot(a, b, preferred_element_type=F32)


def kernel_call(body, out_shape, operands, spaces, scratch=(), flops=0, vmem=24 << 20):
    return pl.pallas_call(
        body,
        out_shape=out_shape,
        in_specs=[pl.BlockSpec(memory_space=space) for space in spaces],
        out_specs=jax.tree.map(lambda _: pl.BlockSpec(memory_space=pltpu.VMEM), out_shape),
        scratch_shapes=list(scratch),
        compiler_params=pltpu.CompilerParams(vmem_limit_bytes=vmem),
        cost_estimate=pl.CostEstimate(flops=flops, bytes_accessed=4 << 20, transcendentals=0),
    )(*operands)


def embed_hidden(order, index_ref, x_ref, w_ref, bias_ref, *outs):
    me = index_ref[0]
    rows = outs[0].shape[0]
    for other, out in zip(order, outs):
        begin = pl.multiple_of((me ^ other) * rows, rows)
        out[...] = silu(dot(x_ref[pl.ds(begin, rows), :], w_ref[...]) + bias_ref[...]).astype(BF16)


def embed_finish(section_id, count, *refs):
    hidden = jnp.concatenate([r[...] for r in refs[:count]], axis=1)
    weights = jnp.concatenate([r[...] for r in refs[count : 2 * count]], axis=0)
    gain, shift, out = refs[2 * count :]
    row = slice(section_id, section_id + 1)
    out[...] = layer_norm(dot(hidden, weights), gain[row, :], shift[row, :]).astype(BF16)


def unpack(pieces, t, latent):
    w_in = jnp.concatenate([w[t, : 2 * latent, :] for w in pieces], axis=1)
    width = pieces[0].shape[2]
    w_out = jnp.concatenate(
        [
            jnp.concatenate(
                [w[t, 2 * latent + b : 2 * latent + b + width, :] for b in range(0, latent, width)],
                axis=1,
            )
            for w in pieces
        ],
        axis=0,
    )
    return w_in, w_out


def phase(section_id, tables, count, mesh_like, *refs):
    table_refs = refs[:tables]
    pieces = refs[tables : tables + count]
    bias, gain, shift, ids, own_ref = refs[tables + count : tables + count + 5]
    rest = refs[tables + count + 5 :]
    if mesh_like:
        recv_col, recv_row, out, table, sem = rest
    else:
        head, out, table, sem = rest
    copies = []
    begin = 0
    for i, ref in enumerate(table_refs):
        copies.append(pltpu.make_async_copy(ref, table.at[pl.ds(begin, ref.shape[0])], sem.at[i]))
        begin += ref.shape[0]
    for copy in copies:
        copy.start()
    own = own_ref[...]
    rows, latent = own.shape
    edges = ids.shape[0]
    w_in, w_out = unpack(pieces, 0, latent)
    if mesh_like:
        spread = recv_col[...] == lax.broadcasted_iota(jnp.int32, (edges, rows), 1)
        received = dot(spread.astype(BF16), own).astype(BF16)
        preact = dot(received, w_in[latent:]) + bias[section_id : section_id + 1, :]
    else:
        preact = dot(own, w_in[latent:]) + bias[section_id : section_id + 1, :]
        preact = jnp.concatenate([preact] * (edges // rows), axis=0)
    for copy in copies:
        copy.wait()
    sent = None
    for start in range(0, begin, CHUNK):
        size = min(CHUNK, begin - start)
        hot = ids[...] == lax.broadcasted_iota(jnp.int32, (edges, size), 1) + start
        part = dot(hot.astype(BF16), table[pl.ds(start, size), :])
        sent = part if sent is None else sent + part
    preact = preact + dot(sent.astype(BF16), w_in[:latent])
    row = slice(section_id, section_id + 1)
    messages = layer_norm(dot(silu(preact).astype(BF16), w_out), gain[row, :], shift[row, :])
    messages = messages.astype(BF16)
    if mesh_like:
        collect = lax.broadcasted_iota(jnp.int32, (rows, edges), 0) == recv_row[...]
        aggregate = dot(collect.astype(BF16), messages).astype(BF16)
    else:
        total = messages[:rows].astype(F32)
        for begin in range(rows, edges, rows):
            total = total + messages[begin : begin + rows].astype(F32)
        aggregate = total.astype(BF16)
    w_in, w_out = unpack(pieces, 1, latent)
    row = slice(section_id + 1, section_id + 2)
    preact = dot(own, w_in[:latent]) + dot(aggregate, w_in[latent:]) + bias[row, :]
    update = layer_norm(dot(silu(preact).astype(BF16), w_out), gain[row, :], shift[row, :])
    updated = (own.astype(F32) + update).astype(BF16)
    if mesh_like:
        out[...] = updated
    else:
        out[...] = dot(updated, head[...])


def local(
    x_grid,
    mesh_pos,
    pos_weight,
    embed_in,
    pair_in,
    pair_out,
    hidden_bias,
    norm_gain,
    norm_shift,
    head,
    g2m_take,
    g2m_from,
    g2m_to,
    m2m_take,
    m2m_from,
    m2m_to,
    m2g_take,
    m2g_from,
):
    quarters = lax.axis_size("feat")
    bands = lax.axis_size("band")
    feat_index = lax.axis_index("feat")
    band_index = lax.axis_index("band")
    latent = norm_gain.shape[1]
    width = hidden_bias.shape[1]
    embed_id = pair_out.shape[0] - 1
    band_mesh = mesh_pos.shape[1]
    band_grid = x_grid.shape[0]
    mesh_rows = band_mesh // quarters
    grid_rows = band_grid // quarters
    direct = bands <= 4
    vmem, anywhere, scalar = pltpu.VMEM, pl.ANY, pltpu.SMEM

    bits = [1 << b for b in reversed(range(quarters.bit_length() - 1))]
    order = [0]
    for bit in bits:
        order = order + [other ^ bit for other in order]

    def own(full, axis=0):
        count = full.shape[axis] // quarters
        return lax.dynamic_slice_in_dim(full, feat_index * count, count, axis)

    def swap(value, bit):
        return lax.ppermute(value, "feat", [(f, f ^ bit) for f in range(quarters)])

    def pieces(value):
        parts = [value]
        for bit in bits:
            parts = parts + [swap(part, bit) for part in parts]
        return parts

    def everyone(rows):
        if direct:
            parts = [rows] + [
                lax.ppermute(rows, "band", [(b, (b + step) % bands) for b in range(bands)])
                for step in range(1, bands)
            ]
            for bit in bits:
                parts = parts + [swap(part, bit) for part in parts]
            return parts
        parts = [rows]
        for bit in bits[:-1]:
            parts = parts + [swap(part, bit) for part in parts]
        parts = [lax.all_gather(part, "band", axis=0, tiled=True) for part in parts]
        return parts + [swap(part, bits[-1]) for part in parts]

    tables = lax.all_to_all(
        jnp.concatenate([g2m_take[0], m2m_take[0], m2g_take[0]], axis=1),
        "band",
        split_axis=0,
        concat_axis=0,
        tiled=True,
    )

    def sender_ids(begin, take, senders, source_rows):
        cap = take.shape[2]
        count = source_rows // quarters
        rows = tables[:, begin : begin + cap]
        other = (rows // count) ^ feat_index
        slot = jnp.zeros_like(other)
        for i, bit in enumerate(bits):
            slot = slot + jnp.where(other & bit != 0, 1 << i, 0)
        source = jnp.arange(bands, dtype=jnp.int32)[:, None]
        if direct:
            source = (band_index - source) % bands
        rows = (slot * bands + source) * count + rows % count
        return rows.reshape(-1).at[senders].get(mode="promise_in_bounds")

    grid_edges = own(m2g_from).reshape(grid_rows, -1).T.reshape(-1)
    g2m_ids = sender_ids(0, g2m_take, own(g2m_from), band_grid)[:, None]
    m2m_ids = sender_ids(g2m_take.shape[2], m2m_take, own(m2m_from), band_mesh)[:, None]
    m2g_ids = sender_ids(g2m_take.shape[2] + m2m_take.shape[2], m2g_take, grid_edges, band_mesh)[:, None]
    g2m_recv = own(g2m_to) - feat_index * mesh_rows
    m2m_recv = own(m2m_to) - feat_index * mesh_rows

    hidden = kernel_call(
        functools.partial(embed_hidden, order),
        [jax.ShapeDtypeStruct((grid_rows, width), BF16)] * quarters,
        (feat_index.astype(jnp.int32)[None], x_grid, embed_in, hidden_bias[embed_id:]),
        (scalar, vmem, vmem, vmem),
    )
    hidden = [hidden[0]] + [swap(h, other) for h, other in zip(hidden[1:], order[1:])]
    out_pieces = pieces(pair_out[embed_id])
    grid = kernel_call(
        functools.partial(embed_finish, embed_id, quarters),
        jax.ShapeDtypeStruct((grid_rows, latent), BF16),
        (*hidden, *out_pieces, norm_gain, norm_shift),
        (vmem,) * (2 * quarters + 2),
    )

    bias = jnp.concatenate(pieces(hidden_bias), axis=1)

    def packed(first_id):
        turned = pair_out[first_id : first_id + 2].reshape(2, width, latent // width, width)
        turned = turned.transpose(0, 2, 1, 3).reshape(2, latent, width)
        return jnp.concatenate([pair_in[first_id : first_id + 2], turned], axis=1)

    groups = [pieces(packed(s)) for s in range(0, embed_id, 2)]

    def run(section_id, table, ids, own_latent, extra, out_shape, mesh_like):
        rows = sum(part.shape[0] for part in table)
        edges = ids.shape[0]
        return kernel_call(
            functools.partial(phase, section_id, len(table), quarters, mesh_like),
            out_shape,
            (*table, *groups[section_id // 2], bias, norm_gain, norm_shift, ids, own_latent, *extra),
            (anywhere,) * len(table) + (vmem,) * (quarters + 5 + len(extra)),
            scratch=(
                pltpu.VMEM((rows, latent), BF16),
                pltpu.SemaphoreType.DMA((len(table),)),
            ),
            flops=2 * edges * latent * (rows + 3 * latent),
            vmem=(20 << 20) + 2 * rows * latent * 2,
        )

    own_pos = own(mesh_pos, 1)
    mesh = own_pos[0][:, None] * pos_weight[0][None, :] + own_pos[1][:, None] * pos_weight[1][None, :]
    mesh = (mesh + own_pos[2][:, None] * pos_weight[2][None, :]).astype(BF16)
    shape = jax.ShapeDtypeStruct((mesh_rows, latent), BF16)
    mesh = run(0, everyone(grid), g2m_ids, mesh, (g2m_recv[:, None], g2m_recv[None, :]), shape, True)
    for layer_id in range(LAYERS):
        mesh = run(
            2 + 2 * layer_id,
            everyone(mesh),
            m2m_ids,
            mesh,
            (m2m_recv[:, None], m2m_recv[None, :]),
            shape,
            True,
        )
    return run(
        2 * LAYERS + 2,
        everyone(mesh),
        m2g_ids,
        grid,
        (head,),
        jax.ShapeDtypeStruct((grid_rows, head.shape[1]), F32),
        False,
    )


def solution(mesh):
    return jax.shard_map(
        local,
        mesh=mesh,
        in_specs=(
            P(("parts", "band"), None),
            P(None, "band"),
            P(),
            P(None, "feat"),
            P(None, None, "feat"),
            P(None, "feat", None),
            P(None, "feat"),
            P(),
            P(),
            P(),
            P("band", None, None),
            P("band"),
            P("band"),
            P("band", None, None),
            P("band"),
            P("band"),
            P("band", None, None),
            P("band"),
        ),
        out_specs=P(("parts", "band", "feat"), None),
        check_vma=False,
    )
```

```python
import functools

import jax
import jax.numpy as jnp
from jax import lax
from jax.experimental import pallas as pl
from jax.experimental.pallas import tpu as pltpu
from jax.sharding import PartitionSpec as P

LAYERS = 2
EPSILON = 1e-05
CHUNK = 2048
F32 = jnp.float32
BF16 = jnp.bfloat16


def layer_norm(values, gain_row, shift_row):
    average = jnp.mean(values, axis=-1, keepdims=True)
    centered = values - average
    variance = jnp.mean(centered * centered, axis=-1, keepdims=True)
    return centered * lax.rsqrt(variance + EPSILON) * gain_row + shift_row


def silu(values):
    return 0.5 * values * (1.0 + jnp.tanh(0.5 * values))


def dot(a, b):
    return jnp.dot(a, b, preferred_element_type=F32)


def kernel_call(body, out_shape, operands, spaces, scratch=(), flops=0, vmem=24 << 20):
    return pl.pallas_call(
        body,
        out_shape=out_shape,
        in_specs=[pl.BlockSpec(memory_space=space) for space in spaces],
        out_specs=jax.tree.map(lambda _: pl.BlockSpec(memory_space=pltpu.VMEM), out_shape),
        scratch_shapes=list(scratch),
        compiler_params=pltpu.CompilerParams(vmem_limit_bytes=vmem),
        cost_estimate=pl.CostEstimate(flops=flops, bytes_accessed=4 << 20, transcendentals=0),
    )(*operands)


def embed_hidden(order, section_id, index_ref, x_ref, w_ref, bias_ref, *outs):
    me = index_ref[0]
    bias = bias_ref[section_id : section_id + 1, :]
    rows = outs[0].shape[0]
    for other, out in zip(order, outs):
        begin = pl.multiple_of((me ^ other) * rows, rows)
        out[...] = silu(dot(x_ref[pl.ds(begin, rows), :], w_ref[...]) + bias).astype(BF16)


def embed_finish(section_id, count, *refs):
    hidden = jnp.concatenate([r[...] for r in refs[:count]], axis=1)
    weights = jnp.concatenate([r[...] for r in refs[count : 2 * count]], axis=0)
    gain, shift, out = refs[2 * count :]
    row = slice(section_id, section_id + 1)
    out[...] = layer_norm(dot(hidden, weights), gain[row, :], shift[row, :]).astype(BF16)


def phase(section_id, tables, places, mesh_like, *refs):
    part_ref = refs[0]
    table_refs = refs[1 : 1 + tables]
    refs = refs[1 + tables :]
    pieces = refs[: len(places)]
    refs = refs[len(places) :]
    w_count = count = max(slot for _, slot in places) + 1
    biases = refs[:count]
    gain, shift, ids, own_ref = refs[count : count + 4]
    rest = refs[count + 4 :]
    if mesh_like:
        recv_col, recv_row, out, table, w_in, w_out, table_sem, w_sem = rest
    else:
        head, out, table, w_in, w_out, table_sem, w_sem = rest
    own = own_ref[...]
    rows, latent = own.shape
    width = latent // w_count
    edges = ids.shape[0]
    part = part_ref[0]
    w_copies = []
    for (kind, slot), ref in zip(places, pieces):
        if kind is None:
            src, dst_in, dst_out = (ref, w_in, w_out)
            lead = (slice(None),)
        else:
            t = part if kind == 0 else 1 - part
            src, dst_in, dst_out = (ref, w_in.at[t], w_out.at[t])
            lead = ()
        columns = pl.ds(slot * width, width)
        w_copies.append((src.at[(*lead, pl.ds(0, 2 * latent))], dst_in.at[(*lead, slice(None), columns)]))
        for b in range(0, latent, width):
            w_copies.append(
                (src.at[(*lead, pl.ds(2 * latent + b, width))], dst_out.at[(*lead, columns, pl.ds(b, width))])
            )
    w_copies = [pltpu.make_async_copy(src, dst, w_sem.at[i]) for i, (src, dst) in enumerate(w_copies)]
    copies = []
    begin = 0
    for i, ref in enumerate(table_refs):
        copies.append(pltpu.make_async_copy(ref, table.at[pl.ds(begin, ref.shape[0])], table_sem.at[i]))
        begin += ref.shape[0]
    for copy in copies + w_copies:
        copy.start()
    def bias(t):
        return jnp.concatenate([b[section_id + t : section_id + t + 1, :] for b in biases], axis=1)

    if mesh_like:
        spread = recv_col[...] == lax.broadcasted_iota(jnp.int32, (edges, rows), 1)
        received = dot(spread.astype(BF16), own).astype(BF16)
    for copy in copies:
        copy.wait()
    sent = None
    for start in range(0, begin, CHUNK):
        size = min(CHUNK, begin - start)
        hot = ids[...] == lax.broadcasted_iota(jnp.int32, (edges, size), 1) + start
        term = dot(hot.astype(BF16), table[pl.ds(start, size), :])
        sent = term if sent is None else sent + term
    for copy in w_copies:
        copy.wait()
    if mesh_like:
        preact = dot(received, w_in[0, latent:, :])
    else:
        preact = dot(own, w_in[0, latent:, :])
        preact = jnp.concatenate([preact] * (edges // rows), axis=0)
    preact = preact + dot(sent.astype(BF16), w_in[0, :latent, :]) + bias(0)
    row = slice(section_id, section_id + 1)
    messages = layer_norm(dot(silu(preact).astype(BF16), w_out[0]), gain[row, :], shift[row, :])
    messages = messages.astype(BF16)
    if mesh_like:
        collect = lax.broadcasted_iota(jnp.int32, (rows, edges), 0) == recv_row[...]
        aggregate = dot(collect.astype(BF16), messages).astype(BF16)
    else:
        total = messages[:rows].astype(F32)
        for begin in range(rows, edges, rows):
            total = total + messages[begin : begin + rows].astype(F32)
        aggregate = total.astype(BF16)
    row = slice(section_id + 1, section_id + 2)
    preact = dot(own, w_in[1, :latent, :]) + dot(aggregate, w_in[1, latent:, :]) + bias(1)
    update = layer_norm(dot(silu(preact).astype(BF16), w_out[1]), gain[row, :], shift[row, :])
    updated = (own.astype(F32) + update).astype(BF16)
    if mesh_like:
        out[...] = updated
    else:
        out[...] = dot(updated, head[...])


def local(
    x_grid,
    mesh_pos,
    pos_weight,
    embed_in,
    pair_in,
    pair_out,
    hidden_bias,
    norm_gain,
    norm_shift,
    head,
    g2m_take,
    g2m_from,
    g2m_to,
    m2m_take,
    m2m_from,
    m2m_to,
    m2g_take,
    m2g_from,
):
    quarters = lax.axis_size("feat")
    bands = lax.axis_size("band")
    feat_index = lax.axis_index("feat")
    band_index = lax.axis_index("band")
    latent = norm_gain.shape[1]
    width = hidden_bias.shape[1]
    embed_id = pair_out.shape[0] - 1
    band_mesh = mesh_pos.shape[1]
    band_grid = x_grid.shape[0]
    mesh_rows = band_mesh // quarters
    grid_rows = band_grid // quarters
    direct = bands <= 4
    parts = lax.axis_size("parts")
    part_index = lax.axis_index("parts")
    halves = parts == 2
    vmem, hbm, scalar = pltpu.VMEM, pltpu.HBM, pltpu.SMEM

    bits = [1 << b for b in reversed(range(quarters.bit_length() - 1))]
    order = [0]
    for bit in bits:
        order = order + [other ^ bit for other in order]

    def own(full, axis=0):
        count = full.shape[axis] // quarters
        return lax.dynamic_slice_in_dim(full, feat_index * count, count, axis)

    def swap(value, bit):
        return lax.ppermute(value, "feat", [(f, f ^ bit) for f in range(quarters)])

    def pieces(value):
        parts = [value]
        for bit in bits:
            parts = parts + [swap(part, bit) for part in parts]
        return parts

    def everyone(rows):
        if direct:
            parts = [rows] + [
                lax.ppermute(rows, "band", [(b, (b + step) % bands) for b in range(bands)])
                for step in range(1, bands)
            ]
            for bit in bits:
                parts = parts + [swap(part, bit) for part in parts]
            return parts
        parts = [rows]
        for bit in bits[:-1]:
            parts = parts + [swap(part, bit) for part in parts]
        parts = [lax.all_gather(part, "band", axis=0, tiled=True) for part in parts]
        return parts + [swap(part, bits[-1]) for part in parts]

    tables = lax.all_to_all(
        jnp.concatenate([g2m_take[0], m2m_take[0], m2g_take[0]], axis=1),
        "band",
        split_axis=0,
        concat_axis=0,
        tiled=True,
    )

    def sender_ids(begin, take, senders, source_rows):
        cap = take.shape[2]
        count = source_rows // quarters
        rows = tables[:, begin : begin + cap]
        other = (rows // count) ^ feat_index
        slot = jnp.zeros_like(other)
        for i, bit in enumerate(bits):
            slot = slot + jnp.where(other & bit != 0, 1 << i, 0)
        source = jnp.arange(bands, dtype=jnp.int32)[:, None]
        if direct:
            source = (band_index - source) % bands
        rows = (slot * bands + source) * count + rows % count
        return rows.reshape(-1).at[senders].get(mode="promise_in_bounds")

    grid_edges = own(m2g_from).reshape(grid_rows, -1).T.reshape(-1)
    g2m_ids = sender_ids(0, g2m_take, own(g2m_from), band_grid)[:, None]
    m2m_ids = sender_ids(g2m_take.shape[2], m2m_take, own(m2m_from), band_mesh)[:, None]
    m2g_ids = sender_ids(g2m_take.shape[2] + m2m_take.shape[2], m2g_take, grid_edges, band_mesh)[:, None]
    g2m_recv = own(g2m_to) - feat_index * mesh_rows
    m2m_recv = own(m2m_to) - feat_index * mesh_rows

    hidden = kernel_call(
        functools.partial(embed_hidden, order, embed_id),
        [jax.ShapeDtypeStruct((grid_rows, width), BF16)] * quarters,
        (feat_index.astype(jnp.int32)[None], x_grid, embed_in, hidden_bias),
        (scalar, vmem, vmem, vmem),
    )
    hidden = [hidden[0]] + [swap(h, other) for h, other in zip(hidden[1:], order[1:])]
    out_pieces = pieces(pair_out[embed_id])
    grid = kernel_call(
        functools.partial(embed_finish, embed_id, quarters),
        jax.ShapeDtypeStruct((grid_rows, latent), BF16),
        (*hidden, *out_pieces, norm_gain, norm_shift),
        (vmem,) * (2 * quarters + 2),
    )
    grid, ids = lax.optimization_barrier(
        (grid, (g2m_ids, m2m_ids, m2g_ids, g2m_recv[:, None], m2m_recv[:, None]))
    )
    g2m_ids, m2m_ids, m2g_ids, g2m_column, m2m_column = ids
    biases = pieces(hidden_bias)

    def packed(section_id):
        turned = lax.dynamic_index_in_dim(pair_out, section_id, 0, False)
        turned = turned.reshape(width, latent // width, width)
        turned = turned.transpose(1, 0, 2).reshape(latent, width)
        return jnp.concatenate([lax.dynamic_index_in_dim(pair_in, section_id, 0, False), turned], axis=0)

    def group(section_id, after):
        if not halves:
            mine = jnp.stack([packed(section_id), packed(section_id + 1)])
            if after is not None:
                mine, _ = lax.optimization_barrier((mine, after))
            return [((None, slot), piece) for slot, piece in enumerate(pieces(mine))]
        first = packed(section_id + part_index)
        second = packed(section_id + 1 - part_index)
        if after is not None:
            first, second, _ = lax.optimization_barrier((first, second, after))
        across = swap(first, bits[0])
        over = lax.ppermute(across, "parts", [(0, 1), (1, 0)])
        found = [((0, 0), first), ((1, 0), second), ((0, 1), across), ((1, 1), over)]
        for i, bit in enumerate(bits[1:]):
            found = found + [((kind, slot + (2 << i)), swap(piece, bit)) for (kind, slot), piece in found]
        return found

    def run(section_id, table, after, ids, own_latent, extra, out_shape, mesh_like):
        rows = sum(part.shape[0] for part in table)
        edges = ids.shape[0]
        weights = group(section_id, after)
        places = [place for place, _ in weights]
        weights = [piece for _, piece in weights]
        return kernel_call(
            functools.partial(phase, section_id, len(table), places, mesh_like),
            out_shape,
            (part_index.astype(jnp.int32)[None], *table, *weights, *biases, norm_gain, norm_shift, ids, own_latent, *extra),
            (scalar,) + (hbm,) * (len(table) + len(weights)) + (vmem,) * (quarters + 4 + len(extra)),
            scratch=(
                pltpu.VMEM((rows, latent), BF16),
                pltpu.VMEM((2, 2 * latent, latent), BF16),
                pltpu.VMEM((2, latent, latent), BF16),
                pltpu.SemaphoreType.DMA((len(table),)),
                pltpu.SemaphoreType.DMA((len(weights) * (1 + quarters),)),
            ),
            flops=2 * edges * latent * (rows + 3 * latent),
            vmem=(20 << 20) + 2 * rows * latent * 2,
        )

    own_pos = own(mesh_pos, 1)
    mesh = own_pos[0][:, None] * pos_weight[0][None, :] + own_pos[1][:, None] * pos_weight[1][None, :]
    mesh = (mesh + own_pos[2][:, None] * pos_weight[2][None, :]).astype(BF16)
    shape = jax.ShapeDtypeStruct((mesh_rows, latent), BF16)
    table = everyone(grid)
    mesh = run(0, table, None, g2m_ids, mesh, (g2m_column, g2m_recv[None, :]), shape, True)
    for layer_id in range(LAYERS):
        after = table[2 * bands - 1] if direct else None
        table = everyone(mesh)
        mesh = run(
            2 + 2 * layer_id, table, after, m2m_ids, mesh, (m2m_column, m2m_recv[None, :]), shape, True
        )
    after = table[2 * bands - 1] if direct else None
    return run(
        2 * LAYERS + 2,
        everyone(mesh),
        after,
        m2g_ids,
        grid,
        (head,),
        jax.ShapeDtypeStruct((grid_rows, head.shape[1]), F32),
        False,
    )


def solution(mesh):
    return jax.shard_map(
        local,
        mesh=mesh,
        in_specs=(
            P(("parts", "band"), None),
            P(None, "band"),
            P(),
            P(None, "feat"),
            P(None, None, "feat"),
            P(None, "feat", None),
            P(None, "feat"),
            P(),
            P(),
            P(),
            P("band", None, None),
            P("band"),
            P("band"),
            P("band", None, None),
            P("band"),
            P("band"),
            P("band", None, None),
            P("band"),
        ),
        out_specs=P(("parts", "band", "feat"), None),
        check_vma=False,
    )
```

```python
import functools

import jax
import jax.numpy as jnp
from jax import lax
from jax.experimental import pallas as pl
from jax.experimental.pallas import tpu as pltpu
from jax.sharding import PartitionSpec as P

LAYERS = 2
EPSILON = 1e-05
CHUNK = 2048
BIAS_ROWS = 16
F32 = jnp.float32
BF16 = jnp.bfloat16


def layer_norm(values, gain_row, shift_row):
    average = jnp.mean(values, axis=-1, keepdims=True)
    centered = values - average
    variance = jnp.mean(centered * centered, axis=-1, keepdims=True)
    return centered * lax.rsqrt(variance + EPSILON) * gain_row + shift_row


def silu(values):
    return 0.5 * values * (1.0 + jnp.tanh(0.5 * values))


def dot(a, b):
    return jnp.dot(a, b, preferred_element_type=F32)


def kernel_call(body, out_shape, operands, spaces, scratch=(), outs=None, flops=0, vmem=24 << 20):
    if outs is None:
        outs = jax.tree.map(lambda _: pltpu.VMEM, out_shape)
    return pl.pallas_call(
        body,
        out_shape=out_shape,
        in_specs=[pl.BlockSpec(memory_space=space) for space in spaces],
        out_specs=jax.tree.map(lambda space: pl.BlockSpec(memory_space=space), outs),
        scratch_shapes=list(scratch),
        compiler_params=pltpu.CompilerParams(vmem_limit_bytes=vmem),
        cost_estimate=pl.CostEstimate(flops=flops, bytes_accessed=4 << 20, transcendentals=0),
    )(*operands)


def started(pairs, sem):
    copies = [pltpu.make_async_copy(src, dst, sem.at[i]) for i, (src, dst) in enumerate(pairs)]
    for copy in copies:
        copy.start()
    return copies


def wait_all(copies):
    for copy in copies:
        copy.wait()


def embed_hidden(order, section_id, place_ref, x_hbm, w_hbm, out_hbm, bias_ref, *refs):
    out_w = refs[0]
    outs = refs[1 : 1 + len(order)]
    x_ref, w_ref, sem = refs[1 + len(order) :]
    copies = started([(x_hbm, x_ref), (w_hbm, w_ref), (out_hbm.at[section_id], out_w)], sem)
    wait_all(copies)
    me = place_ref[0]
    bias = bias_ref[section_id : section_id + 1, :]
    rows = outs[0].shape[0]
    for other, out in zip(order, outs):
        begin = pl.multiple_of((me ^ other) * rows, rows)
        out[...] = silu(dot(x_ref[pl.ds(begin, rows), :], w_ref[...]) + bias).astype(BF16)


def embed_finish(section_id, count, *refs):
    hidden = jnp.concatenate([r[...] for r in refs[:count]], axis=1)
    weights = jnp.concatenate([r[...] for r in refs[count : 2 * count]], axis=0)
    gain, shift, out = refs[2 * count :]
    row = slice(section_id, section_id + 1)
    out[...] = layer_norm(dot(hidden, weights), gain[row, :], shift[row, :]).astype(BF16)


def pack(first_id, place_ref, in_hbm, out_hbm, bias_ref, *refs):
    outs = refs[:-2]
    terms, sem = refs[-2:]
    part = place_ref[2]
    inner, width = in_hbm.shape[1:]
    latent = out_hbm.shape[2]
    pairs = []
    for i, out in enumerate(outs):
        section_id = first_id + (i - i % 2) + (part if i % 2 == 0 else 1 - part)
        pairs.append((in_hbm.at[section_id], out.at[pl.ds(0, inner)]))
        for b in range(0, latent, width):
            pairs.append((out_hbm.at[section_id, :, pl.ds(b, width)], out.at[pl.ds(inner + b, width)]))
        rest = bias_ref[pl.ds(section_id, 1), :]
        index = lax.broadcasted_iota(jnp.int32, (BIAS_ROWS, width), 0)
        value = jnp.zeros((BIAS_ROWS, width), F32)
        for term in range(3):
            head = rest.astype(BF16).astype(F32)
            value = jnp.where(index == term, head, value)
            rest = rest - head
        terms[i] = value.astype(BF16)
        pairs.append((terms.at[i], out.at[pl.ds(inner + latent, BIAS_ROWS)]))
    wait_all(started(pairs, sem))


def route(bits, direct, caps, counts, edges, place_ref, tables, from_g, from_m, from_d, to_g, to_m, pos, pos_w, *outs):
    ids_g, ids_m, ids_d, col_g, col_m, row_g, row_m, mesh_out = outs
    me, band = place_ref[0], place_ref[1]
    bands = tables.shape[0]

    def column(row):
        return jnp.broadcast_to(row, (8, row.shape[1])).T[:, :1].astype(jnp.int32)

    begin = 0
    for cap, count, size, senders, out in zip(caps, counts, edges, (from_g, from_m, from_d), (ids_g, ids_m, ids_d)):
        padded = -(-cap // 128) * 128
        names = senders[:, pl.ds(pl.multiple_of(me * size, size), size)]
        total = jnp.zeros((16, size), F32)
        for s in range(bands):
            value = tables[s : s + 1, begin : begin + padded]
            other = (value >> (count.bit_length() - 1)) ^ me
            slot = jnp.zeros_like(other)
            for i, bit in enumerate(bits):
                slot = slot + jnp.where((other & bit) != 0, 1 << i, 0)
            source = s
            if direct:
                source = jnp.where(band >= s, band - s, band - s + bands)
            value = (slot * bands + source) * count + (value & (count - 1))
            index = lax.broadcasted_iota(jnp.int32, (16, padded), 0)
            high = jnp.broadcast_to((value >> 7).astype(F32), index.shape)
            low = jnp.broadcast_to((value & 127).astype(F32), index.shape)
            digits = jnp.where(index == 0, high, jnp.where(index == 1, low, 0.0)).astype(BF16)
            slots = lax.broadcasted_iota(jnp.int32, (padded, size), 0)
            hot = jnp.where((slots + s * cap == names) & (slots < cap), 1.0, 0.0).astype(BF16)
            total = total + dot(digits, hot)
        out[...] = column(total[0:1] * 128.0 + total[1:2])
        begin += padded
    for size, rows, to, col, row in ((edges[0], mesh_out.shape[0], to_g, col_g, row_g), (edges[1], mesh_out.shape[0], to_m, col_m, row_m)):
        mine = to[:, pl.ds(pl.multiple_of(me * size, size), size)] - me * rows
        row[...] = mine
        col[...] = column(mine.astype(F32))
    rows = mesh_out.shape[0]
    mine = pos[:, pl.ds(pl.multiple_of(me * rows, rows), rows)]
    index = lax.broadcasted_iota(jnp.int32, (8, rows), 0)
    stacked = jnp.zeros((8, rows), F32)
    for t in range(3):
        stacked = jnp.where(index == t, mine[t : t + 1, :], stacked)
    turned = stacked.T
    mesh = turned[:, 0:1] * pos_w[0:1, :] + turned[:, 1:2] * pos_w[1:2, :]
    mesh_out[...] = (mesh + turned[:, 2:3] * pos_w[2:3, :]).astype(BF16)


def phase(section_id, tables, places, last, *refs):
    place_ref = refs[0]
    table_refs = refs[1 : 1 + tables]
    refs = refs[1 + tables :]
    pieces = refs[: len(places)]
    gain, shift, ids, own_ref, *rest = refs[len(places) :]
    if last:
        head_hbm, out_hbm, table, w_in, w_out, w_bias, table_sem, w_sem, head, out, head_sem = rest
    else:
        recv_col, recv_row, out, table, w_in, w_out, w_bias, table_sem, w_sem = rest
    own = own_ref[...]
    rows, latent = own.shape
    width = pieces[0].shape[1]
    edges = ids.shape[0]
    part = place_ref[2]
    pairs = []
    begin = 0
    for ref in table_refs:
        pairs.append((ref, table.at[pl.ds(begin, ref.shape[0])]))
        begin += ref.shape[0]
    t_copies = started(pairs, table_sem)
    pairs = []
    for (kind, slot), ref in zip(places, pieces):
        t = part if kind == 0 else 1 - part
        columns = pl.ds(slot * width, width)
        pairs.append((ref.at[pl.ds(0, 2 * latent)], w_in.at[t, :, columns]))
        for b in range(0, latent, width):
            pairs.append((ref.at[pl.ds(2 * latent + b, width)], w_out.at[t, columns, pl.ds(b, width)]))
        pairs.append((ref.at[pl.ds(3 * latent, BIAS_ROWS)], w_bias.at[t, :, columns]))
    w_copies = started(pairs, w_sem)
    if last:
        h_copies = started([(head_hbm, head)], head_sem)
        degree = edges // rows
        edge = lax.broadcasted_iota(jnp.int32, (edges, rows), 0)
        node = lax.broadcasted_iota(jnp.int32, (edges, rows), 1) * degree
        spread = (edge >= node) & (edge < node + degree)
        edge = lax.broadcasted_iota(jnp.int32, (rows, edges), 1)
        node = lax.broadcasted_iota(jnp.int32, (rows, edges), 0) * degree
        collect = (edge >= node) & (edge < node + degree)
    else:
        spread = recv_col[...] == lax.broadcasted_iota(jnp.int32, (edges, rows), 1)
        collect = lax.broadcasted_iota(jnp.int32, (rows, edges), 0) == recv_row[...]
    received = dot(spread.astype(BF16), own).astype(BF16)
    wait_all(t_copies)
    sent = None
    for start in range(0, begin, CHUNK):
        size = min(CHUNK, begin - start)
        hot = ids[...] == lax.broadcasted_iota(jnp.int32, (edges, size), 1) + start
        term = dot(hot.astype(BF16), table[pl.ds(start, size), :])
        sent = term if sent is None else sent + term
    wait_all(w_copies)

    def mlp(t, first, second):
        terms = w_bias[t].astype(F32)
        bias = (terms[0:1] + terms[1:2]) + terms[2:3]
        preact = dot(first, w_in[t, :latent, :]) + dot(second, w_in[t, latent:, :]) + bias
        row = slice(section_id + t, section_id + t + 1)
        return layer_norm(dot(silu(preact).astype(BF16), w_out[t]), gain[row, :], shift[row, :])

    messages = mlp(0, sent.astype(BF16), received).astype(BF16)
    aggregate = dot(collect.astype(BF16), messages).astype(BF16)
    updated = (own.astype(F32) + mlp(1, own, aggregate)).astype(BF16)
    if last:
        wait_all(h_copies)
        out[...] = dot(updated, head[...])
        wait_all(started([(out, out_hbm)], head_sem))
    else:
        out[...] = updated


def local(
    x_grid,
    mesh_pos,
    pos_weight,
    embed_in,
    pair_in,
    pair_out,
    hidden_bias,
    norm_gain,
    norm_shift,
    head,
    g2m_take,
    g2m_from,
    g2m_to,
    m2m_take,
    m2m_from,
    m2m_to,
    m2g_take,
    m2g_from,
):
    quarters = lax.axis_size("feat")
    bands = lax.axis_size("band")
    feat_index = lax.axis_index("feat")
    band_index = lax.axis_index("band")
    latent = norm_gain.shape[1]
    width = hidden_bias.shape[1]
    embed_id = pair_out.shape[0] - 1
    band_mesh = mesh_pos.shape[1]
    band_grid = x_grid.shape[0]
    mesh_rows = band_mesh // quarters
    grid_rows = band_grid // quarters
    direct = bands <= 4
    part_index = lax.axis_index("parts")
    vmem, hbm, scalar = pltpu.VMEM, pltpu.HBM, pltpu.SMEM
    place = jnp.stack([feat_index, band_index, part_index]).astype(jnp.int32)

    bits = [1 << b for b in reversed(range(quarters.bit_length() - 1))]
    order = [0]
    for bit in bits:
        order = order + [other ^ bit for other in order]

    def swap(value, bit):
        return lax.ppermute(value, "feat", [(f, f ^ bit) for f in range(quarters)])

    def pieces(value):
        parts = [value]
        for bit in bits:
            parts = parts + [swap(part, bit) for part in parts]
        return parts

    def everyone(rows):
        if direct:
            parts = [rows] + [
                lax.ppermute(rows, "band", [(b, (b + step) % bands) for b in range(bands)])
                for step in range(1, bands)
            ]
            for bit in bits:
                parts = parts + [swap(part, bit) for part in parts]
            return parts
        parts = [rows]
        for bit in bits[:-1]:
            parts = parts + [swap(part, bit) for part in parts]
        parts = [lax.all_gather(part, "band", axis=0, tiled=True) for part in parts]
        return parts + [swap(part, bits[-1]) for part in parts]

    hidden = kernel_call(
        functools.partial(embed_hidden, order, embed_id),
        [jax.ShapeDtypeStruct((width, latent), BF16)]
        + [jax.ShapeDtypeStruct((grid_rows, width), BF16)] * quarters,
        (place, x_grid, embed_in, pair_out, hidden_bias),
        (scalar, hbm, hbm, hbm, vmem),
        scratch=(
            pltpu.VMEM(x_grid.shape, BF16),
            pltpu.VMEM(embed_in.shape, BF16),
            pltpu.SemaphoreType.DMA((3,)),
        ),
    )
    out_pieces = pieces(hidden[0])
    hidden = [hidden[1]] + [swap(h, other) for h, other in zip(hidden[2:], order[1:])]

    def packs(first_id, sections):
        shape = jax.ShapeDtypeStruct((3 * latent + BIAS_ROWS, width), BF16)
        return kernel_call(
            functools.partial(pack, first_id),
            [shape] * sections,
            (place, pair_in, pair_out, hidden_bias),
            (scalar, hbm, hbm, vmem),
            scratch=(
                pltpu.VMEM((sections, BIAS_ROWS, width), BF16),
                pltpu.SemaphoreType.DMA((sections * (2 + latent // width),)),
            ),
            outs=[hbm] * sections,
        )

    packed = packs(0, 2)
    later = packs(2, embed_id - 2)

    takes = [take[0] for take in (g2m_take, m2m_take, m2g_take)]
    caps = [take.shape[1] for take in takes]
    takes = [jnp.pad(take, ((0, 0), (0, -take.shape[1] % 128))) for take in takes]
    tables = lax.all_to_all(
        jnp.concatenate(takes, axis=1), "band", split_axis=0, concat_axis=0, tiled=True
    )
    edges = [names.shape[0] // quarters for names in (g2m_from, m2m_from, m2g_from)]
    columns = [jax.ShapeDtypeStruct((n, 1), jnp.int32) for n in edges + edges[:2]]
    lines = [jax.ShapeDtypeStruct((1, n), jnp.int32) for n in edges[:2]]
    shape = jax.ShapeDtypeStruct((mesh_rows, latent), BF16)
    routed = kernel_call(
        functools.partial(route, bits, direct, caps, (grid_rows, mesh_rows, mesh_rows), edges),
        [*columns, *lines, shape],
        (place, tables, *[v[None, :] for v in (g2m_from, m2m_from, m2g_from, g2m_to, m2m_to)], mesh_pos, pos_weight),
        (scalar,) + (vmem,) * 8,
    )
    hidden, out_pieces, routed, later = lax.optimization_barrier((hidden, out_pieces, routed, later))
    ids_g, ids_m, ids_d, col_g, col_m, row_g, row_m, mesh = routed
    packed = packed + later
    grid = kernel_call(
        functools.partial(embed_finish, embed_id, quarters),
        jax.ShapeDtypeStruct((grid_rows, latent), BF16),
        (*hidden, *out_pieces, norm_gain, norm_shift),
        (vmem,) * (2 * quarters + 2),
    )

    def group(section_id, after):
        first, second = packed[section_id : section_id + 2]
        if after is not None:
            first, second, _ = lax.optimization_barrier((first, second, after))
        across = swap(first, bits[0])
        over = lax.ppermute(across, "parts", [(0, 1), (1, 0)])
        found = [((0, 0), first), ((1, 0), second), ((0, 1), across), ((1, 1), over)]
        for i, bit in enumerate(bits[1:]):
            found = found + [((kind, slot + (2 << i)), swap(piece, bit)) for (kind, slot), piece in found]
        return found

    def run(section_id, table, after, ids, own_latent, extra, last=False):
        rows = sum(part.shape[0] for part in table)
        weights = group(section_id, after)
        places = [p for p, _ in weights]
        weights = [piece for _, piece in weights]
        scratch = [
            pltpu.VMEM((rows, latent), BF16),
            pltpu.VMEM((2, 2 * latent, latent), BF16),
            pltpu.VMEM((2, latent, latent), BF16),
            pltpu.VMEM((2, BIAS_ROWS, latent), BF16),
            pltpu.SemaphoreType.DMA((len(table),)),
            pltpu.SemaphoreType.DMA((len(weights) * (2 + quarters),)),
        ]
        out_shape = jax.ShapeDtypeStruct(own_latent.shape, BF16)
        if last:
            out_shape = jax.ShapeDtypeStruct((own_latent.shape[0], head.shape[1]), F32)
            scratch += [
                pltpu.VMEM(head.shape, BF16),
                pltpu.VMEM(out_shape.shape, F32),
                pltpu.SemaphoreType.DMA((1,)),
            ]
        return kernel_call(
            functools.partial(phase, section_id, len(table), places, last),
            out_shape,
            (place, *table, *weights, norm_gain, norm_shift, ids, own_latent, *extra),
            (scalar,) + (hbm,) * (len(table) + len(weights)) + (vmem,) * 4 + ((hbm,) if last else (vmem, vmem)),
            scratch=scratch,
            outs=hbm if last else vmem,
            flops=2 * ids.shape[0] * latent * (rows + 3 * latent),
            vmem=(20 << 20) + 2 * rows * latent * 2,
        )

    def held(table):
        return table[2 * bands - 1] if direct else None

    table = everyone(grid)
    mesh = run(0, table, None, ids_g, mesh, (col_g, row_g))
    for layer_id in range(LAYERS):
        after = held(table)
        table = everyone(mesh)
        mesh = run(2 + 2 * layer_id, table, after, ids_m, mesh, (col_m, row_m))
    return run(2 * LAYERS + 2, everyone(mesh), held(table), ids_d, grid, (head,), True)


def solution(mesh):
    return jax.shard_map(
        local,
        mesh=mesh,
        in_specs=(
            P(("parts", "band"), None),
            P(None, "band"),
            P(),
            P(None, "feat"),
            P(None, None, "feat"),
            P(None, "feat", None),
            P(None, "feat"),
            P(),
            P(),
            P(),
            P("band", None, None),
            P("band"),
            P("band"),
            P("band", None, None),
            P("band"),
            P("band"),
            P("band", None, None),
            P("band"),
        ),
        out_specs=P(("parts", "band", "feat"), None),
        check_vma=False,
    )
```

```python
import functools

import jax
import jax.numpy as jnp
from jax import lax
from jax.experimental import pallas as pl
from jax.experimental.pallas import tpu as pltpu
from jax.sharding import PartitionSpec as P

LAYERS = 2
EPSILON = 1e-05
CHUNK = 2048
BIAS_ROWS = 16
GRANT = 60 << 20
F32 = jnp.float32
BF16 = jnp.bfloat16


def layer_norm(values, gain_row, shift_row):
    average = jnp.mean(values, axis=-1, keepdims=True)
    centered = values - average
    variance = jnp.mean(centered * centered, axis=-1, keepdims=True)
    return centered * lax.rsqrt(variance + EPSILON) * gain_row + shift_row


def silu(values):
    return 0.5 * values * (1.0 + jnp.tanh(0.5 * values))


def dot(a, b):
    return jnp.dot(a, b, preferred_element_type=F32)


def kernel_call(body, out_shape, operands, spaces, scratch=(), outs=None, flops=0, vmem=24 << 20):
    if outs is None:
        outs = jax.tree.map(lambda _: pltpu.VMEM, out_shape)
    return pl.pallas_call(
        body,
        out_shape=out_shape,
        in_specs=[pl.BlockSpec(memory_space=space) for space in spaces],
        out_specs=jax.tree.map(lambda space: pl.BlockSpec(memory_space=space), outs),
        scratch_shapes=list(scratch),
        compiler_params=pltpu.CompilerParams(vmem_limit_bytes=vmem),
        cost_estimate=pl.CostEstimate(flops=flops, bytes_accessed=4 << 20, transcendentals=0),
    )(*operands)


def started(pairs, sem):
    copies = [pltpu.make_async_copy(src, dst, sem.at[i]) for i, (src, dst) in enumerate(pairs)]
    for copy in copies:
        copy.start()
    return copies


def wait_all(copies):
    for copy in copies:
        copy.wait()


def embed_hidden(order, section_id, place_ref, x_hbm, w_hbm, out_hbm, bias_ref, *refs):
    out_w = refs[0]
    outs = refs[1 : 1 + len(order)]
    x_ref, w_ref, sem = refs[1 + len(order) :]
    copies = started([(x_hbm, x_ref), (w_hbm, w_ref), (out_hbm.at[section_id], out_w)], sem)
    wait_all(copies)
    me = place_ref[0]
    bias = bias_ref[section_id : section_id + 1, :]
    rows = outs[0].shape[0]
    for other, out in zip(order, outs):
        begin = pl.multiple_of((me ^ other) * rows, rows)
        product = lax.dot_general(
            x_ref[:, pl.ds(begin, rows)], w_ref[...], (((0,), (0,)), ((), ())), preferred_element_type=F32
        )
        out[...] = silu(product + bias).astype(BF16)


def embed_finish(section_id, count, *refs):
    hidden = jnp.concatenate([r[...] for r in refs[:count]], axis=1)
    weights = jnp.concatenate([r[...] for r in refs[count : 2 * count]], axis=0)
    gain, shift, out = refs[2 * count :]
    row = slice(section_id, section_id + 1)
    out[...] = layer_norm(dot(hidden, weights), gain[row, :], shift[row, :]).astype(BF16)


def pack(first_id, place_ref, in_hbm, out_hbm, bias_ref, *refs):
    outs = refs[:-2]
    terms, sem = refs[-2:]
    part = place_ref[2]
    inner, width = in_hbm.shape[1:]
    latent = out_hbm.shape[2]
    pairs = []
    for i, out in enumerate(outs):
        section_id = first_id + (i - i % 2) + (part if i % 2 == 0 else 1 - part)
        pairs.append((in_hbm.at[section_id], out.at[pl.ds(0, inner)]))
        for b in range(0, latent, width):
            pairs.append((out_hbm.at[section_id, :, pl.ds(b, width)], out.at[pl.ds(inner + b, width)]))
        rest = bias_ref[pl.ds(section_id, 1), :]
        index = lax.broadcasted_iota(jnp.int32, (BIAS_ROWS, width), 0)
        value = jnp.zeros((BIAS_ROWS, width), F32)
        for term in range(3):
            head = rest.astype(BF16).astype(F32)
            value = jnp.where(index == term, head, value)
            rest = rest - head
        terms[i] = value.astype(BF16)
        pairs.append((terms.at[i], out.at[pl.ds(inner + latent, BIAS_ROWS)]))
    wait_all(started(pairs, sem))


def route(bits, direct, caps, counts, edges, place_ref, tables, from_g, from_m, from_d, to_g, to_m, pos, pos_w, *outs):
    ids_g, ids_m, ids_d, col_g, col_m, row_g, row_m, mesh_out = outs
    me, band = place_ref[0], place_ref[1]
    bands = tables.shape[0]

    def column(row):
        return jnp.broadcast_to(row, (8, row.shape[1])).T[:, :1].astype(jnp.int32)

    begin = 0
    for cap, count, size, senders, out in zip(caps, counts, edges, (from_g, from_m, from_d), (ids_g, ids_m, ids_d)):
        padded = -(-cap // 128) * 128
        names = senders[:, pl.ds(pl.multiple_of(me * size, size), size)]
        total = jnp.zeros((16, size), F32)
        for s in range(bands):
            value = tables[s : s + 1, begin : begin + padded]
            other = (value >> (count.bit_length() - 1)) ^ me
            slot = jnp.zeros_like(other)
            for i, bit in enumerate(bits):
                slot = slot + jnp.where((other & bit) != 0, 1 << i, 0)
            source = s
            if direct:
                source = jnp.where(band >= s, band - s, band - s + bands)
            value = (slot * bands + source) * count + (value & (count - 1))
            index = lax.broadcasted_iota(jnp.int32, (16, padded), 0)
            high = jnp.broadcast_to((value >> 7).astype(F32), index.shape)
            low = jnp.broadcast_to((value & 127).astype(F32), index.shape)
            digits = jnp.where(index == 0, high, jnp.where(index == 1, low, 0.0)).astype(BF16)
            slots = lax.broadcasted_iota(jnp.int32, (padded, size), 0)
            hot = jnp.where((slots + s * cap == names) & (slots < cap), 1.0, 0.0).astype(BF16)
            total = total + dot(digits, hot)
        out[...] = column(total[0:1] * 128.0 + total[1:2])
        begin += padded
    for size, rows, to, col, row in ((edges[0], mesh_out.shape[0], to_g, col_g, row_g), (edges[1], mesh_out.shape[0], to_m, col_m, row_m)):
        mine = to[:, pl.ds(pl.multiple_of(me * size, size), size)] - me * rows
        row[...] = mine
        col[...] = column(mine.astype(F32))
    rows = mesh_out.shape[0]
    mine = pos[:, pl.ds(pl.multiple_of(me * rows, rows), rows)]
    index = lax.broadcasted_iota(jnp.int32, (8, rows), 0)
    stacked = jnp.zeros((8, rows), F32)
    for t in range(3):
        stacked = jnp.where(index == t, mine[t : t + 1, :], stacked)
    turned = stacked.T
    mesh = turned[:, 0:1] * pos_w[0:1, :] + turned[:, 1:2] * pos_w[1:2, :]
    mesh_out[...] = (mesh + turned[:, 2:3] * pos_w[2:3, :]).astype(BF16)


def stage(places, last, *refs):
    place_ref = refs[0]
    pieces = refs[1 : 1 + len(places)]
    own_ref, *rest = refs[1 + len(places) :]
    if last:
        w_send, w_out, w_agg, w_out2, recv_pre, node_pre = rest
    else:
        recv_col, w_send, w_out, w_agg, w_out2, recv_pre, node_pre = rest
    own = own_ref[...]
    rows, latent = own.shape
    width = pieces[0].shape[1]
    edges = recv_pre.shape[0]
    if last:
        degree = edges // rows
        edge = lax.broadcasted_iota(jnp.int32, (edges, rows), 0)
        node = lax.broadcasted_iota(jnp.int32, (edges, rows), 1) * degree
        spread = (edge >= node) & (edge < node + degree)
    else:
        spread = recv_col[...] == lax.broadcasted_iota(jnp.int32, (edges, rows), 1)
    received = dot(spread.astype(BF16), own).astype(BF16)

    def bias(refs):
        terms = [ref[pl.ds(3 * latent, BIAS_ROWS), :].astype(F32) for ref in refs]
        return jnp.concatenate([(t[0:1] + t[1:2]) + t[2:3] for t in terms], axis=1)

    def fill(target, out, begin, refs):
        for slot, ref in enumerate(refs):
            columns = pl.ds(slot * width, width)
            target[:, columns] = ref[pl.ds(begin, latent), :]
            for b in range(0, latent, width):
                out[columns, pl.ds(b, width)] = ref[pl.ds(2 * latent + b, width), :]

    def emit(edge_kind):
        ordered = [
            [ref for _, ref in sorted(
                    ((slot, ref) for (kind, slot), ref in zip(places, pieces) if kind == wanted),
                    key=lambda pair: pair[0],
                )]
            for wanted in (edge_kind, 1 - edge_kind)
        ]
        first, second = ordered
        fill(w_send, w_out, 0, first)
        fill(w_agg, w_out2, latent, second)
        weights = jnp.concatenate([ref[pl.ds(latent, latent), :] for ref in first], axis=1)
        recv_pre[...] = dot(received, weights) + bias(first)
        weights = jnp.concatenate([ref[pl.ds(0, latent), :] for ref in second], axis=1)
        node_pre[...] = dot(own, weights) + bias(second)

    part = place_ref[2]
    pl.when(part == 0)(functools.partial(emit, 0))
    pl.when(part == 1)(functools.partial(emit, 1))


def phase(section_id, tables, last, *refs):
    table_refs = refs[:tables]
    ids, own_ref, w_send, w_out, w_agg, w_out2, recv_pre, node_pre, gain, shift, extra, out = refs[tables:]
    rows, latent = own_ref.shape
    edges = ids.shape[0]
    chunks = [[]]
    held = 0
    for ref in table_refs:
        size = min(ref.shape[0], CHUNK)
        for begin in range(0, ref.shape[0], size):
            if held + size > CHUNK:
                chunks.append([])
                held = 0
            chunks[-1].append(ref[pl.ds(begin, size), :])
            held += size
    preact = recv_pre[...]
    sent = None
    start = 0
    for chunk in chunks:
        chunk = jnp.concatenate(chunk, axis=0) if len(chunk) > 1 else chunk[0]
        hot = ids[...] == lax.broadcasted_iota(jnp.int32, (edges, chunk.shape[0]), 1) + start
        term = dot(hot.astype(BF16), chunk)
        sent = term if sent is None else sent + term
        start += chunk.shape[0]
    preact = preact + dot(sent.astype(BF16), w_send[...])

    def finish(t, preact, weights):
        row = slice(section_id + t, section_id + t + 1)
        return layer_norm(dot(silu(preact).astype(BF16), weights[...]), gain[row, :], shift[row, :])

    messages = finish(0, preact, w_out).astype(BF16)
    if last:
        degree = edges // rows
        edge = lax.broadcasted_iota(jnp.int32, (rows, edges), 1)
        node = lax.broadcasted_iota(jnp.int32, (rows, edges), 0) * degree
        collect = (edge >= node) & (edge < node + degree)
    else:
        collect = lax.broadcasted_iota(jnp.int32, (rows, edges), 0) == extra[...]
    aggregate = dot(collect.astype(BF16), messages).astype(BF16)
    update = finish(1, node_pre[...] + dot(aggregate, w_agg[...]), w_out2)
    updated = (own_ref[...].astype(F32) + update).astype(BF16)
    if last:
        out[...] = lax.dot_general(
            extra[...], updated, (((1,), (1,)), ((), ())), preferred_element_type=F32
        )
    else:
        out[...] = updated


def local(
    x_grid,
    mesh_pos,
    pos_weight,
    embed_in,
    pair_in,
    pair_out,
    hidden_bias,
    norm_gain,
    norm_shift,
    head,
    g2m_take,
    g2m_from,
    g2m_to,
    m2m_take,
    m2m_from,
    m2m_to,
    m2g_take,
    m2g_from,
):
    quarters = lax.axis_size("feat")
    bands = lax.axis_size("band")
    feat_index = lax.axis_index("feat")
    band_index = lax.axis_index("band")
    latent = norm_gain.shape[1]
    width = hidden_bias.shape[1]
    embed_id = pair_out.shape[0] - 1
    band_mesh = mesh_pos.shape[1]
    band_grid = x_grid.shape[0]
    mesh_rows = band_mesh // quarters
    grid_rows = band_grid // quarters
    direct = bands <= 4
    part_index = lax.axis_index("parts")
    vmem, hbm, scalar = pltpu.VMEM, pltpu.HBM, pltpu.SMEM
    place = jnp.stack([feat_index, band_index, part_index]).astype(jnp.int32)

    bits = [1 << b for b in reversed(range(quarters.bit_length() - 1))]
    order = [0]
    for bit in bits:
        order = order + [other ^ bit for other in order]

    def swap(value, bit):
        return lax.ppermute(value, "feat", [(f, f ^ bit) for f in range(quarters)])

    def pieces(value):
        parts = [value]
        for bit in bits:
            parts = parts + [swap(part, bit) for part in parts]
        return parts

    def everyone(rows):
        if direct:
            parts = [rows] + [
                lax.ppermute(rows, "band", [(b, (b + step) % bands) for b in range(bands)])
                for step in range(1, bands)
            ]
            for bit in bits:
                parts = parts + [swap(part, bit) for part in parts]
            return parts
        parts = [rows]
        for bit in bits[:-1]:
            parts = parts + [swap(part, bit) for part in parts]
        parts = [lax.all_gather(part, "band", axis=0, tiled=True) for part in parts]
        return parts + [swap(part, bits[-1]) for part in parts]

    hidden = kernel_call(
        functools.partial(embed_hidden, order, embed_id),
        [jax.ShapeDtypeStruct((width, latent), BF16)]
        + [jax.ShapeDtypeStruct((grid_rows, width), BF16)] * quarters,
        (place, x_grid.T, embed_in, pair_out, hidden_bias),
        (scalar, hbm, hbm, hbm, vmem),
        scratch=(
            pltpu.VMEM(x_grid.shape[::-1], BF16),
            pltpu.VMEM(embed_in.shape, BF16),
            pltpu.SemaphoreType.DMA((3,)),
        ),
        vmem=GRANT,
    )
    out_pieces = pieces(hidden[0])
    hidden = [hidden[1]] + [swap(h, other) for h, other in zip(hidden[2:], order[1:])]

    def packs(first_id, sections):
        shape = jax.ShapeDtypeStruct((3 * latent + BIAS_ROWS, width), BF16)
        return kernel_call(
            functools.partial(pack, first_id),
            [shape] * sections,
            (place, pair_in, pair_out, hidden_bias),
            (scalar, hbm, hbm, vmem),
            scratch=(
                pltpu.VMEM((sections, BIAS_ROWS, width), BF16),
                pltpu.SemaphoreType.DMA((sections * (2 + latent // width),)),
            ),
            outs=[hbm] * sections,
            vmem=GRANT,
        )

    takes = [take[0] for take in (g2m_take, m2m_take, m2g_take)]
    caps = [take.shape[1] for take in takes]
    takes = [jnp.pad(take, ((0, 0), (0, -take.shape[1] % 128))) for take in takes]
    tables = lax.all_to_all(
        jnp.concatenate(takes, axis=1), "band", split_axis=0, concat_axis=0, tiled=True
    )
    edges = [names.shape[0] // quarters for names in (g2m_from, m2m_from, m2g_from)]
    columns = [jax.ShapeDtypeStruct((n, 1), jnp.int32) for n in edges + edges[:2]]
    lines = [jax.ShapeDtypeStruct((1, n), jnp.int32) for n in edges[:2]]
    shape = jax.ShapeDtypeStruct((mesh_rows, latent), BF16)
    routed = kernel_call(
        functools.partial(route, bits, direct, caps, (grid_rows, mesh_rows, mesh_rows), edges),
        [*columns, *lines, shape],
        (place, tables, *[v[None, :] for v in (g2m_from, m2m_from, m2g_from, g2m_to, m2m_to)], mesh_pos, pos_weight),
        (scalar,) + (vmem,) * 8,
        vmem=GRANT,
    )
    pair_in, pair_out, _ = lax.optimization_barrier((pair_in, pair_out, routed[-1]))
    packed = packs(0, 2)
    later = packs(2, embed_id - 2)
    hidden, out_pieces, routed, packed, later = lax.optimization_barrier(
        (hidden, out_pieces, routed, packed, later)
    )
    ids_g, ids_m, ids_d, col_g, col_m, row_g, row_m, mesh = routed
    packed = packed + later
    grid = kernel_call(
        functools.partial(embed_finish, embed_id, quarters),
        jax.ShapeDtypeStruct((grid_rows, latent), BF16),
        (*hidden, *out_pieces, norm_gain, norm_shift),
        (vmem,) * (2 * quarters + 2),
    )

    def group(section_id, after, gate):
        first, second = packed[section_id : section_id + 2]
        if after is not None:
            first, second, _ = lax.optimization_barrier((first, second, after))
        across = swap(first, bits[0])
        if after is not None:
            across, _ = lax.optimization_barrier((across, gate))
        over = lax.ppermute(across, "parts", [(0, 1), (1, 0)])
        found = [((0, 0), first), ((1, 0), second), ((0, 1), across), ((1, 1), over)]
        for i, bit in enumerate(bits[1:]):
            found = found + [((kind, slot + (2 << i)), swap(piece, bit)) for (kind, slot), piece in found]
        return found

    def run(section_id, table, after, ids, own_latent, column, extra, last=False):
        rows = sum(part.shape[0] for part in table)
        edges = ids.shape[0]
        weights = group(section_id, after, table[1])
        places = [p for p, _ in weights]
        weights = [piece for _, piece in weights]
        square = jax.ShapeDtypeStruct((latent, latent), BF16)
        columns = () if last else (column,)
        staged = kernel_call(
            functools.partial(stage, places, last),
            [square] * 4
            + [jax.ShapeDtypeStruct((n, latent), F32) for n in (edges, own_latent.shape[0])],
            (place, *weights, own_latent, *columns),
            (scalar,) + (vmem,) * (len(weights) + 1 + len(columns)),
            flops=4 * edges * latent * latent,
            vmem=20 << 20,
        )
        out_shape = jax.ShapeDtypeStruct(own_latent.shape, BF16)
        if last:
            out_shape = jax.ShapeDtypeStruct((head.shape[1], own_latent.shape[0]), F32)
        return kernel_call(
            functools.partial(phase, section_id, len(table), last),
            out_shape,
            (*table, ids, own_latent, *staged, norm_gain, norm_shift, extra),
            (vmem,) * (len(table) + 11),
            flops=2 * edges * latent * (rows + 3 * latent),
            vmem=(20 << 20) + rows * latent * 2,
        )

    def held(table):
        return table[2 * bands - 1] if direct else table[-1]

    table = everyone(grid)
    mesh = run(0, table, None, ids_g, mesh, col_g, row_g)
    for layer_id in range(LAYERS):
        after = held(table)
        table = everyone(mesh)
        mesh = run(2 + 2 * layer_id, table, after, ids_m, mesh, col_m, row_m)
    return run(2 * LAYERS + 2, everyone(mesh), held(table), ids_d, grid, None, head.T, True).T


def solution(mesh):
    return jax.shard_map(
        local,
        mesh=mesh,
        in_specs=(
            P(("parts", "band"), None),
            P(None, "band"),
            P(),
            P(None, "feat"),
            P(None, None, "feat"),
            P(None, "feat", None),
            P(None, "feat"),
            P(),
            P(),
            P(),
            P("band", None, None),
            P("band"),
            P("band"),
            P("band", None, None),
            P("band"),
            P("band"),
            P("band", None, None),
            P("band"),
        ),
        out_specs=P(("parts", "band", "feat"), None),
        check_vma=False,
    )
```

```python
import functools

import jax
import jax.numpy as jnp
from jax import lax
from jax.experimental import pallas as pl
from jax.experimental.pallas import tpu as pltpu
from jax.sharding import PartitionSpec as P

LAYERS = 2
EPSILON = 1e-05
CHUNK = 2048
BIAS_ROWS = 16
GRANT = 60 << 20
F32 = jnp.float32
BF16 = jnp.bfloat16


def layer_norm(values, gain_row, shift_row):
    average = jnp.mean(values, axis=-1, keepdims=True)
    centered = values - average
    variance = jnp.mean(centered * centered, axis=-1, keepdims=True)
    return centered * lax.rsqrt(variance + EPSILON) * gain_row + shift_row


def silu(values):
    return 0.5 * values * (1.0 + jnp.tanh(0.5 * values))


def dot(a, b):
    return jnp.dot(a, b, preferred_element_type=F32)


def kernel_call(body, out_shape, operands, spaces, scratch=(), outs=None, flops=0, vmem=24 << 20):
    if outs is None:
        outs = jax.tree.map(lambda _: pltpu.VMEM, out_shape)
    return pl.pallas_call(
        body,
        out_shape=out_shape,
        in_specs=[pl.BlockSpec(memory_space=space) for space in spaces],
        out_specs=jax.tree.map(lambda space: pl.BlockSpec(memory_space=space), outs),
        scratch_shapes=list(scratch),
        compiler_params=pltpu.CompilerParams(vmem_limit_bytes=vmem),
        cost_estimate=pl.CostEstimate(flops=flops, bytes_accessed=4 << 20, transcendentals=0),
    )(*operands)


def started(pairs, sem):
    copies = [pltpu.make_async_copy(src, dst, sem.at[i]) for i, (src, dst) in enumerate(pairs)]
    for copy in copies:
        copy.start()
    return copies


def wait_all(copies):
    for copy in copies:
        copy.wait()


def embed_hidden(order, section_id, place_ref, x_hbm, w_hbm, out_hbm, bias_ref, take_g, take_m, take_d, *refs):
    out_w = refs[0]
    outs = refs[1 : 1 + len(order)]
    x_ref, w_ref, sem = refs[-3:]
    bands = take_g.shape[1]
    for step, out in enumerate(refs[1 + len(order) : -3]):
        target = place_ref[1] + step
        target = jnp.where(target >= bands, target - bands, target)
        begin = 0
        for take in (take_g, take_m, take_d):
            out[:, begin : begin + take.shape[2]] = take[0, pl.ds(target, 1), :]
            begin += take.shape[2]
    copies = started([(x_hbm, x_ref), (w_hbm, w_ref), (out_hbm.at[section_id], out_w)], sem)
    wait_all(copies)
    me = place_ref[0]
    bias = bias_ref[section_id : section_id + 1, :]
    rows = outs[0].shape[0]
    for other, out in zip(order, outs):
        begin = pl.multiple_of((me ^ other) * rows, rows)
        product = lax.dot_general(
            x_ref[:, pl.ds(begin, rows)], w_ref[...], (((0,), (0,)), ((), ())), preferred_element_type=F32
        )
        out[...] = silu(product + bias).astype(BF16)


def embed_finish(section_id, count, *refs):
    hidden = jnp.concatenate([r[...] for r in refs[:count]], axis=1)
    weights = jnp.concatenate([r[...] for r in refs[count : 2 * count]], axis=0)
    gain, shift, out = refs[2 * count :]
    row = slice(section_id, section_id + 1)
    out[...] = layer_norm(dot(hidden, weights), gain[row, :], shift[row, :]).astype(BF16)


def pack(first_id, place_ref, in_hbm, out_hbm, bias_ref, *refs):
    outs = refs[:-2]
    terms, sem = refs[-2:]
    part = place_ref[2]
    inner, width = in_hbm.shape[1:]
    latent = out_hbm.shape[2]
    pairs = []
    for i, out in enumerate(outs):
        section_id = first_id + (i - i % 2) + (part if i % 2 == 0 else 1 - part)
        pairs.append((in_hbm.at[section_id], out.at[pl.ds(0, inner)]))
        for b in range(0, latent, width):
            pairs.append((out_hbm.at[section_id, :, pl.ds(b, width)], out.at[pl.ds(inner + b, width)]))
        rest = bias_ref[pl.ds(section_id, 1), :]
        index = lax.broadcasted_iota(jnp.int32, (BIAS_ROWS, width), 0)
        value = jnp.zeros((BIAS_ROWS, width), F32)
        for term in range(3):
            head = rest.astype(BF16).astype(F32)
            value = jnp.where(index == term, head, value)
            rest = rest - head
        terms[i] = value.astype(BF16)
        pairs.append((terms.at[i], out.at[pl.ds(inner + latent, BIAS_ROWS)]))
    wait_all(started(pairs, sem))


def route(bits, direct, bands, caps, counts, edges, place_ref, *refs):
    tables = refs[: bands if direct else 1]
    from_g, from_m, from_d, to_g, to_m, pos, pos_w, *outs = refs[len(tables) :]
    ids_g, ids_m, ids_d, col_g, col_m, row_g, row_m, mesh_out = outs
    me, band = place_ref[0], place_ref[1]

    def column(row):
        return jnp.broadcast_to(row, (8, row.shape[1])).T[:, :1].astype(jnp.int32)

    begin = 0
    for cap, count, size, senders, out in zip(caps, counts, edges, (from_g, from_m, from_d), (ids_g, ids_m, ids_d)):
        padded = -(-cap // 128) * 128
        names = senders[:, pl.ds(pl.multiple_of(me * size, size), size)]
        total = jnp.zeros((16, size), F32)
        for s in range(bands):
            if direct:
                value = tables[s][:, begin : begin + padded]
                source = jnp.where(band >= s, band - s, band - s + bands)
            else:
                value = tables[0][s : s + 1, begin : begin + padded]
                source = s
            other = (value >> (count.bit_length() - 1)) ^ me
            slot = jnp.zeros_like(other)
            for i, bit in enumerate(bits):
                slot = slot + jnp.where((other & bit) != 0, 1 << i, 0)
            value = (slot * bands + s) * count + (value & (count - 1))
            index = lax.broadcasted_iota(jnp.int32, (16, padded), 0)
            high = jnp.broadcast_to((value >> 7).astype(F32), index.shape)
            low = jnp.broadcast_to((value & 127).astype(F32), index.shape)
            digits = jnp.where(index == 0, high, jnp.where(index == 1, low, 0.0)).astype(BF16)
            slots = lax.broadcasted_iota(jnp.int32, (padded, size), 0)
            hot = jnp.where((slots + source * cap == names) & (slots < cap), 1.0, 0.0).astype(BF16)
            total = total + dot(digits, hot)
        out[...] = column(total[0:1] * 128.0 + total[1:2])
        begin += padded
    for size, rows, to, col, row in ((edges[0], mesh_out.shape[0], to_g, col_g, row_g), (edges[1], mesh_out.shape[0], to_m, col_m, row_m)):
        mine = to[:, pl.ds(pl.multiple_of(me * size, size), size)] - me * rows
        row[...] = mine
        col[...] = column(mine.astype(F32))
    rows = mesh_out.shape[0]
    mine = pos[:, pl.ds(pl.multiple_of(me * rows, rows), rows)]
    index = lax.broadcasted_iota(jnp.int32, (8, rows), 0)
    stacked = jnp.zeros((8, rows), F32)
    for t in range(3):
        stacked = jnp.where(index == t, mine[t : t + 1, :], stacked)
    turned = stacked.T
    mesh = turned[:, 0:1] * pos_w[0:1, :] + turned[:, 1:2] * pos_w[1:2, :]
    mesh_out[...] = (mesh + turned[:, 2:3] * pos_w[2:3, :]).astype(BF16)


def stage(places, last, *refs):
    place_ref = refs[0]
    pieces = refs[1 : 1 + len(places)]
    own_ref, *rest = refs[1 + len(places) :]
    if last:
        w_send, w_out, w_agg, w_out2, recv_pre, node_pre = rest
    else:
        recv_col, w_send, w_out, w_agg, w_out2, recv_pre, node_pre = rest
    own = own_ref[...]
    rows, latent = own.shape
    width = pieces[0].shape[1]
    edges = recv_pre.shape[0]
    if last:
        degree = edges // rows
        edge = lax.broadcasted_iota(jnp.int32, (edges, rows), 0)
        node = lax.broadcasted_iota(jnp.int32, (edges, rows), 1) * degree
        spread = (edge >= node) & (edge < node + degree)
    else:
        spread = recv_col[...] == lax.broadcasted_iota(jnp.int32, (edges, rows), 1)
    received = dot(spread.astype(BF16), own).astype(BF16)

    def bias(refs):
        terms = [ref[pl.ds(3 * latent, BIAS_ROWS), :].astype(F32) for ref in refs]
        return jnp.concatenate([(t[0:1] + t[1:2]) + t[2:3] for t in terms], axis=1)

    def fill(target, out, begin, refs):
        for slot, ref in enumerate(refs):
            columns = pl.ds(slot * width, width)
            target[:, columns] = ref[pl.ds(begin, latent), :]
            for b in range(0, latent, width):
                out[columns, pl.ds(b, width)] = ref[pl.ds(2 * latent + b, width), :]

    def emit(edge_kind):
        ordered = [
            [ref for _, ref in sorted(
                    ((slot, ref) for (kind, slot), ref in zip(places, pieces) if kind == wanted),
                    key=lambda pair: pair[0],
                )]
            for wanted in (edge_kind, 1 - edge_kind)
        ]
        first, second = ordered
        fill(w_send, w_out, 0, first)
        fill(w_agg, w_out2, latent, second)
        weights = jnp.concatenate([ref[pl.ds(latent, latent), :] for ref in first], axis=1)
        recv_pre[...] = dot(received, weights) + bias(first)
        weights = jnp.concatenate([ref[pl.ds(0, latent), :] for ref in second], axis=1)
        node_pre[...] = dot(own, weights) + bias(second)

    part = place_ref[2]
    pl.when(part == 0)(functools.partial(emit, 0))
    pl.when(part == 1)(functools.partial(emit, 1))


def phase(section_id, tables, last, *refs):
    table_refs = refs[:tables]
    ids, own_ref, w_send, w_out, w_agg, w_out2, recv_pre, node_pre, gain, shift, extra, out = refs[tables:]
    rows, latent = own_ref.shape
    edges = ids.shape[0]
    chunks = [[]]
    held = 0
    for ref in table_refs:
        size = min(ref.shape[0], CHUNK)
        for begin in range(0, ref.shape[0], size):
            if held + size > CHUNK:
                chunks.append([])
                held = 0
            chunks[-1].append(ref[pl.ds(begin, size), :])
            held += size
    preact = recv_pre[...]
    sent = None
    start = 0
    for chunk in chunks:
        chunk = jnp.concatenate(chunk, axis=0) if len(chunk) > 1 else chunk[0]
        hot = ids[...] == lax.broadcasted_iota(jnp.int32, (edges, chunk.shape[0]), 1) + start
        term = dot(hot.astype(BF16), chunk)
        sent = term if sent is None else sent + term
        start += chunk.shape[0]
    preact = preact + dot(sent.astype(BF16), w_send[...])

    def finish(t, preact, weights):
        row = slice(section_id + t, section_id + t + 1)
        return layer_norm(dot(silu(preact).astype(BF16), weights[...]), gain[row, :], shift[row, :])

    messages = finish(0, preact, w_out).astype(BF16)
    if last:
        degree = edges // rows
        edge = lax.broadcasted_iota(jnp.int32, (rows, edges), 1)
        node = lax.broadcasted_iota(jnp.int32, (rows, edges), 0) * degree
        collect = (edge >= node) & (edge < node + degree)
    else:
        collect = lax.broadcasted_iota(jnp.int32, (rows, edges), 0) == extra[...]
    aggregate = dot(collect.astype(BF16), messages).astype(BF16)
    update = finish(1, node_pre[...] + dot(aggregate, w_agg[...]), w_out2)
    updated = (own_ref[...].astype(F32) + update).astype(BF16)
    if last:
        out[...] = lax.dot_general(
            extra[...], updated, (((1,), (1,)), ((), ())), preferred_element_type=F32
        )
    else:
        out[...] = updated


def local(
    x_grid,
    mesh_pos,
    pos_weight,
    embed_in,
    pair_in,
    pair_out,
    hidden_bias,
    norm_gain,
    norm_shift,
    head,
    g2m_take,
    g2m_from,
    g2m_to,
    m2m_take,
    m2m_from,
    m2m_to,
    m2g_take,
    m2g_from,
):
    quarters = lax.axis_size("feat")
    bands = lax.axis_size("band")
    feat_index = lax.axis_index("feat")
    band_index = lax.axis_index("band")
    latent = norm_gain.shape[1]
    width = hidden_bias.shape[1]
    embed_id = pair_out.shape[0] - 1
    band_mesh = mesh_pos.shape[1]
    band_grid = x_grid.shape[0]
    mesh_rows = band_mesh // quarters
    grid_rows = band_grid // quarters
    direct = bands <= 4
    part_index = lax.axis_index("parts")
    vmem, hbm, scalar = pltpu.VMEM, pltpu.HBM, pltpu.SMEM
    place = jnp.stack([feat_index, band_index, part_index]).astype(jnp.int32)

    bits = [1 << b for b in reversed(range(quarters.bit_length() - 1))]
    order = [0]
    for bit in bits:
        order = order + [other ^ bit for other in order]

    def swap(value, bit):
        return lax.ppermute(value, "feat", [(f, f ^ bit) for f in range(quarters)])

    def shift(value, step):
        return lax.ppermute(value, "band", [(b, (b + step) % bands) for b in range(bands)])

    def pieces(value):
        parts = [value]
        for bit in bits:
            parts = parts + [swap(part, bit) for part in parts]
        return parts

    def everyone(rows):
        if direct:
            parts = [rows] + [shift(rows, step) for step in range(1, bands)]
            for bit in bits:
                parts = parts + [swap(part, bit) for part in parts]
            return parts
        parts = [rows]
        for bit in bits[:-1]:
            parts = parts + [swap(part, bit) for part in parts]
        parts = [lax.all_gather(part, "band", axis=0, tiled=True) for part in parts]
        return parts + [swap(part, bits[-1]) for part in parts]

    caps = [take.shape[2] for take in (g2m_take, m2m_take, m2g_take)]
    direct = direct and all(cap % 128 == 0 for cap in caps)
    hidden = kernel_call(
        functools.partial(embed_hidden, order, embed_id),
        [jax.ShapeDtypeStruct((width, latent), BF16)]
        + [jax.ShapeDtypeStruct((grid_rows, width), BF16)] * quarters
        + [jax.ShapeDtypeStruct((1, sum(caps)), jnp.int32)] * (bands if direct else 0),
        (place, x_grid.T, embed_in, pair_out, hidden_bias, g2m_take, m2m_take, m2g_take),
        (scalar, hbm, hbm, hbm, vmem, vmem, vmem, vmem),
        scratch=(
            pltpu.VMEM(x_grid.shape[::-1], BF16),
            pltpu.VMEM(embed_in.shape, BF16),
            pltpu.SemaphoreType.DMA((3,)),
        ),
        vmem=GRANT,
    )
    out_pieces = pieces(hidden[0])
    rows = hidden[1 + quarters :]
    hidden = [hidden[1]] + [swap(h, other) for h, other in zip(hidden[2:], order[1:])]

    def packs(first_id, sections):
        shape = jax.ShapeDtypeStruct((3 * latent + BIAS_ROWS, width), BF16)
        return kernel_call(
            functools.partial(pack, first_id),
            [shape] * sections,
            (place, pair_in, pair_out, hidden_bias),
            (scalar, hbm, hbm, vmem),
            scratch=(
                pltpu.VMEM((sections, BIAS_ROWS, width), BF16),
                pltpu.SemaphoreType.DMA((sections * (2 + latent // width),)),
            ),
            vmem=GRANT,
        )

    if direct:
        tables = [rows[0]] + [shift(row, step) for step, row in enumerate(rows[1:], 1)]
    else:
        takes = [jnp.pad(t[0], ((0, 0), (0, -t.shape[2] % 128))) for t in (g2m_take, m2m_take, m2g_take)]
        tables = [
            lax.all_to_all(
                jnp.concatenate(takes, axis=1), "band", split_axis=0, concat_axis=0, tiled=True
            )
        ]
    edges = [names.shape[0] // quarters for names in (g2m_from, m2m_from, m2g_from)]
    columns = [jax.ShapeDtypeStruct((n, 1), jnp.int32) for n in edges + edges[:2]]
    lines = [jax.ShapeDtypeStruct((1, n), jnp.int32) for n in edges[:2]]
    shape = jax.ShapeDtypeStruct((mesh_rows, latent), BF16)
    names = [v[None, :] for v in (g2m_from, m2m_from, m2g_from, g2m_to, m2m_to)]
    packed = packs(0, 2)
    later = packs(2, embed_id - 2)
    hidden, out_pieces, names, packed, later = lax.optimization_barrier(
        (hidden, out_pieces, names, packed, later)
    )
    packed = packed + later
    routed = kernel_call(
        functools.partial(route, bits, direct, bands, caps, (grid_rows, mesh_rows, mesh_rows), edges),
        [*columns, *lines, shape],
        (place, *tables, *names, mesh_pos, pos_weight),
        (scalar,) + (vmem,) * (len(tables) + 7),
        vmem=24 << 20,
    )
    ids_g, ids_m, ids_d, col_g, col_m, row_g, row_m, mesh = routed
    grid = kernel_call(
        functools.partial(embed_finish, embed_id, quarters),
        jax.ShapeDtypeStruct((grid_rows, latent), BF16),
        (*hidden, *out_pieces, norm_gain, norm_shift),
        (vmem,) * (2 * quarters + 2),
    )

    def group(section_id, after, table):
        first, second = packed[section_id : section_id + 2]
        if after is not None:
            first, _ = lax.optimization_barrier((first, after))
        across = swap(first, bits[0])
        across, _ = lax.optimization_barrier((across, table[1]))
        over = lax.ppermute(across, "parts", [(0, 1), (1, 0)])
        found = [((0, 0), first), ((1, 0), second), ((0, 1), across), ((1, 1), over)]
        for i, bit in enumerate(bits[1:]):
            other = [((kind, slot + (2 << i)), piece) for (kind, slot), piece in found]
            for place_of, piece in other:
                piece, _ = lax.optimization_barrier((piece, table[bands - 1 if direct else 1]))
                found.append((place_of, swap(piece, bit)))
        return found

    def run(section_id, table, after, ids, own_latent, column, extra, last=False):
        rows = sum(part.shape[0] for part in table)
        edges = ids.shape[0]
        weights = group(section_id, after, table)
        places = [p for p, _ in weights]
        weights = [piece for _, piece in weights]
        square = jax.ShapeDtypeStruct((latent, latent), BF16)
        columns = () if last else (column,)
        staged = kernel_call(
            functools.partial(stage, places, last),
            [square] * 4
            + [jax.ShapeDtypeStruct((n, latent), F32) for n in (edges, own_latent.shape[0])],
            (place, *weights, own_latent, *columns),
            (scalar,) + (vmem,) * (len(weights) + 1 + len(columns)),
            flops=4 * edges * latent * latent,
            vmem=20 << 20,
        )
        out_shape = jax.ShapeDtypeStruct(own_latent.shape, BF16)
        if last:
            out_shape = jax.ShapeDtypeStruct((head.shape[1], own_latent.shape[0]), F32)
        return kernel_call(
            functools.partial(phase, section_id, len(table), last),
            out_shape,
            (*table, ids, own_latent, *staged, norm_gain, norm_shift, extra),
            (vmem,) * (len(table) + 11),
            flops=2 * edges * latent * (rows + 3 * latent),
            vmem=(20 << 20) + rows * latent * 2,
        )

    def held(table):
        return table[2 * bands - 1] if direct else table[-1]

    table = everyone(grid)
    mesh = run(0, table, None, ids_g, mesh, col_g, row_g)
    for layer_id in range(LAYERS):
        after = held(table)
        table = everyone(mesh)
        mesh = run(2 + 2 * layer_id, table, after, ids_m, mesh, col_m, row_m)
    return run(2 * LAYERS + 2, everyone(mesh), held(table), ids_d, grid, None, head.T, True).T


def solution(mesh):
    return jax.shard_map(
        local,
        mesh=mesh,
        in_specs=(
            P(("parts", "band"), None),
            P(None, "band"),
            P(),
            P(None, "feat"),
            P(None, None, "feat"),
            P(None, "feat", None),
            P(None, "feat"),
            P(),
            P(),
            P(),
            P("band", None, None),
            P("band"),
            P("band"),
            P("band", None, None),
            P("band"),
            P("band"),
            P("band", None, None),
            P("band"),
        ),
        out_specs=P(("parts", "band", "feat"), None),
        check_vma=False,
    )
```

```python
import functools

import jax
import jax.numpy as jnp
from jax import lax
from jax.experimental import pallas as pl
from jax.experimental.pallas import tpu as pltpu
from jax.sharding import PartitionSpec as P

LAYERS = 2
EPSILON = 1e-05
CHUNK = 2048
BIAS_ROWS = 16
GRANT = 60 << 20
F32 = jnp.float32
BF16 = jnp.bfloat16


def layer_norm(values, gain_row, shift_row):
    average = jnp.mean(values, axis=-1, keepdims=True)
    centered = values - average
    variance = jnp.mean(centered * centered, axis=-1, keepdims=True)
    return centered * lax.rsqrt(variance + EPSILON) * gain_row + shift_row


def silu(values):
    return 0.5 * values * (1.0 + jnp.tanh(0.5 * values))


def dot(a, b):
    return jnp.dot(a, b, preferred_element_type=F32)


def kernel_call(body, out_shape, operands, spaces, scratch=(), outs=None, flops=0, vmem=24 << 20):
    if outs is None:
        outs = jax.tree.map(lambda _: pltpu.VMEM, out_shape)
    return pl.pallas_call(
        body,
        out_shape=out_shape,
        in_specs=[pl.BlockSpec(memory_space=space) for space in spaces],
        out_specs=jax.tree.map(lambda space: pl.BlockSpec(memory_space=space), outs),
        scratch_shapes=list(scratch),
        compiler_params=pltpu.CompilerParams(vmem_limit_bytes=vmem),
        cost_estimate=pl.CostEstimate(flops=flops, bytes_accessed=4 << 20, transcendentals=0),
    )(*operands)


def started(pairs, sem):
    copies = [pltpu.make_async_copy(src, dst, sem.at[i]) for i, (src, dst) in enumerate(pairs)]
    for copy in copies:
        copy.start()
    return copies


def wait_all(copies):
    for copy in copies:
        copy.wait()


def embed_hidden(order, section_id, place_ref, x_hbm, w_hbm, out_hbm, bias_ref, take_g, take_m, take_d, *refs):
    out_w = refs[0]
    outs = refs[1 : 1 + len(order)]
    x_ref, w_ref, sem = refs[-3:]
    bands = take_g.shape[1]
    for step, out in enumerate(refs[1 + len(order) : -3]):
        target = place_ref[1] + step
        target = jnp.where(target >= bands, target - bands, target)
        begin = 0
        for take in (take_g, take_m, take_d):
            out[:, begin : begin + take.shape[2]] = take[0, pl.ds(target, 1), :]
            begin += take.shape[2]
    copies = started([(x_hbm, x_ref), (w_hbm, w_ref), (out_hbm.at[section_id], out_w)], sem)
    wait_all(copies)
    me = place_ref[0]
    bias = bias_ref[section_id : section_id + 1, :]
    rows = outs[0].shape[0]
    for other, out in zip(order, outs):
        begin = pl.multiple_of((me ^ other) * rows, rows)
        product = lax.dot_general(
            x_ref[:, pl.ds(begin, rows)], w_ref[...], (((0,), (0,)), ((), ())), preferred_element_type=F32
        )
        out[...] = silu(product + bias).astype(BF16)


def embed_finish(section_id, count, *refs):
    hidden = jnp.concatenate([r[...] for r in refs[:count]], axis=1)
    weights = jnp.concatenate([r[...] for r in refs[count : 2 * count]], axis=0)
    gain, shift, out = refs[2 * count :]
    row = slice(section_id, section_id + 1)
    out[...] = layer_norm(dot(hidden, weights), gain[row, :], shift[row, :]).astype(BF16)


def pack(place_ref, in_hbm, out_ref, bias_ref, packed, *refs):
    crossing, sem = refs[:-1], refs[-1]
    part = place_ref[2]
    inner, width = in_hbm.shape[1:]
    latent = out_ref.shape[2]
    targets = []
    pairs = []
    for i in range(packed.shape[0]):
        section_id = (i - i % 2) + (part if i % 2 == 0 else 1 - part)
        targets.append((section_id, [packed.at[i]] + ([crossing[i // 2]] if i % 2 == 0 else [])))
        pairs += [(in_hbm.at[section_id], out.at[pl.ds(0, inner)]) for out in targets[-1][1]]
    copies = started(pairs, sem)
    for section_id, outs in targets:
        rest = bias_ref[pl.ds(section_id, 1), :]
        index = lax.broadcasted_iota(jnp.int32, (BIAS_ROWS, width), 0)
        value = jnp.zeros((BIAS_ROWS, width), F32)
        for term in range(3):
            head = rest.astype(BF16).astype(F32)
            value = jnp.where(index == term, head, value)
            rest = rest - head
        second = out_ref[section_id]
        for out in outs:
            out[pl.ds(inner + latent, BIAS_ROWS), :] = value.astype(BF16)
            for b in range(0, latent, width):
                out[pl.ds(inner + b, width), :] = second[:, b : b + width]
    wait_all(copies)


def route(bits, direct, bands, caps, counts, edges, place_ref, *refs):
    tables = refs[: bands if direct else 1]
    from_g, from_m, from_d, to_g, to_m, pos, pos_w, *outs = refs[len(tables) :]
    ids_g, ids_m, ids_d, col_g, col_m, row_g, row_m, mesh_out = outs
    me, band = place_ref[0], place_ref[1]

    def column(row):
        return jnp.broadcast_to(row, (8, row.shape[1])).T[:, :1].astype(jnp.int32)

    begin = 0
    for cap, count, size, senders, out in zip(caps, counts, edges, (from_g, from_m, from_d), (ids_g, ids_m, ids_d)):
        padded = -(-cap // 128) * 128
        names = senders[:, pl.ds(pl.multiple_of(me * size, size), size)]
        total = jnp.zeros((16, size), F32)
        for s in range(bands):
            if direct:
                value = tables[s][:, begin : begin + padded]
                source = jnp.where(band >= s, band - s, band - s + bands)
            else:
                value = tables[0][s : s + 1, begin : begin + padded]
                source = s
            other = (value >> (count.bit_length() - 1)) ^ me
            slot = jnp.zeros_like(other)
            for i, bit in enumerate(bits):
                slot = slot + jnp.where((other & bit) != 0, 1 << i, 0)
            value = (slot * bands + s) * count + (value & (count - 1))
            index = lax.broadcasted_iota(jnp.int32, (16, padded), 0)
            high = jnp.broadcast_to((value >> 7).astype(F32), index.shape)
            low = jnp.broadcast_to((value & 127).astype(F32), index.shape)
            digits = jnp.where(index == 0, high, jnp.where(index == 1, low, 0.0)).astype(BF16)
            slots = lax.broadcasted_iota(jnp.int32, (padded, size), 0)
            hot = jnp.where((slots + source * cap == names) & (slots < cap), 1.0, 0.0).astype(BF16)
            total = total + dot(digits, hot)
        out[...] = column(total[0:1] * 128.0 + total[1:2])
        begin += padded
    for size, rows, to, col, row in ((edges[0], mesh_out.shape[0], to_g, col_g, row_g), (edges[1], mesh_out.shape[0], to_m, col_m, row_m)):
        mine = to[:, pl.ds(pl.multiple_of(me * size, size), size)] - me * rows
        row[...] = mine
        col[...] = column(mine.astype(F32))
    rows = mesh_out.shape[0]
    mine = pos[:, pl.ds(pl.multiple_of(me * rows, rows), rows)]
    index = lax.broadcasted_iota(jnp.int32, (8, rows), 0)
    stacked = jnp.zeros((8, rows), F32)
    for t in range(3):
        stacked = jnp.where(index == t, mine[t : t + 1, :], stacked)
    turned = stacked.T
    mesh = turned[:, 0:1] * pos_w[0:1, :] + turned[:, 1:2] * pos_w[1:2, :]
    mesh_out[...] = (mesh + turned[:, 2:3] * pos_w[2:3, :]).astype(BF16)


def stage(group_id, last, *refs):
    place_ref, mine_hbm, other_hbm, *across, own_ref = refs[:8]
    rest = refs[8:]
    if not last:
        recv_col, *rest = rest
    w_send, w_out, w_agg, w_out2, recv_pre, node_pre, mine, other, sem = rest
    chosen = pl.ds(2 * group_id, 2)
    copies = started([(mine_hbm.at[chosen], mine), (other_hbm.at[chosen], other)], sem)
    x_first, y_second, cx_first, cy_second = across
    kinds = (
        [mine.at[0], x_first, other.at[0], cx_first],
        [mine.at[1], y_second, other.at[1], cy_second],
    )
    own = own_ref[...]
    rows, latent = own.shape
    width = mine.shape[2]
    edges = recv_pre.shape[0]
    if last:
        degree = edges // rows
        edge = lax.broadcasted_iota(jnp.int32, (edges, rows), 0)
        node = lax.broadcasted_iota(jnp.int32, (edges, rows), 1) * degree
        spread = (edge >= node) & (edge < node + degree)
    else:
        spread = recv_col[...] == lax.broadcasted_iota(jnp.int32, (edges, rows), 1)
    received = dot(spread.astype(BF16), own).astype(BF16)

    def bias(refs):
        terms = [ref[pl.ds(3 * latent, BIAS_ROWS), :].astype(F32) for ref in refs]
        return jnp.concatenate([(t[0:1] + t[1:2]) + t[2:3] for t in terms], axis=1)

    def fill(target, out, begin, refs):
        for slot, ref in enumerate(refs):
            columns = pl.ds(slot * width, width)
            target[:, columns] = ref[pl.ds(begin, latent), :]
            for b in range(0, latent, width):
                out[columns, pl.ds(b, width)] = ref[pl.ds(2 * latent + b, width), :]

    wait_all(copies)

    def emit(edge_kind):
        first, second = kinds[edge_kind], kinds[1 - edge_kind]
        fill(w_send, w_out, 0, first)
        fill(w_agg, w_out2, latent, second)
        weights = jnp.concatenate([ref[pl.ds(latent, latent), :] for ref in first], axis=1)
        recv_pre[...] = dot(received, weights) + bias(first)
        weights = jnp.concatenate([ref[pl.ds(0, latent), :] for ref in second], axis=1)
        node_pre[...] = dot(own, weights) + bias(second)

    part = place_ref[2]
    pl.when(part == 0)(functools.partial(emit, 0))
    pl.when(part == 1)(functools.partial(emit, 1))


def phase(section_id, tables, last, *refs):
    table_refs = refs[:tables]
    ids, own_ref, w_send, w_out, w_agg, w_out2, recv_pre, node_pre, gain, shift, extra, out = refs[tables:]
    rows, latent = own_ref.shape
    edges = ids.shape[0]
    chunks = [[]]
    held = 0
    for ref in table_refs:
        size = min(ref.shape[0], CHUNK)
        for begin in range(0, ref.shape[0], size):
            if held + size > CHUNK:
                chunks.append([])
                held = 0
            chunks[-1].append(ref[pl.ds(begin, size), :])
            held += size
    preact = recv_pre[...]
    sent = None
    start = 0
    for chunk in chunks:
        chunk = jnp.concatenate(chunk, axis=0) if len(chunk) > 1 else chunk[0]
        hot = ids[...] == lax.broadcasted_iota(jnp.int32, (edges, chunk.shape[0]), 1) + start
        term = dot(hot.astype(BF16), chunk)
        sent = term if sent is None else sent + term
        start += chunk.shape[0]
    preact = preact + dot(sent.astype(BF16), w_send[...])

    def finish(t, preact, weights):
        row = slice(section_id + t, section_id + t + 1)
        return layer_norm(dot(silu(preact).astype(BF16), weights[...]), gain[row, :], shift[row, :])

    messages = finish(0, preact, w_out).astype(BF16)
    if last:
        degree = edges // rows
        edge = lax.broadcasted_iota(jnp.int32, (rows, edges), 1)
        node = lax.broadcasted_iota(jnp.int32, (rows, edges), 0) * degree
        collect = (edge >= node) & (edge < node + degree)
    else:
        collect = lax.broadcasted_iota(jnp.int32, (rows, edges), 0) == extra[...]
    aggregate = dot(collect.astype(BF16), messages).astype(BF16)
    update = finish(1, node_pre[...] + dot(aggregate, w_agg[...]), w_out2)
    updated = (own_ref[...].astype(F32) + update).astype(BF16)
    if last:
        out[...] = lax.dot_general(
            extra[...], updated, (((1,), (1,)), ((), ())), preferred_element_type=F32
        )
    else:
        out[...] = updated


def local(
    x_grid,
    mesh_pos,
    pos_weight,
    embed_in,
    pair_in,
    pair_out,
    hidden_bias,
    norm_gain,
    norm_shift,
    head,
    g2m_take,
    g2m_from,
    g2m_to,
    m2m_take,
    m2m_from,
    m2m_to,
    m2g_take,
    m2g_from,
):
    quarters = lax.axis_size("feat")
    bands = lax.axis_size("band")
    feat_index = lax.axis_index("feat")
    band_index = lax.axis_index("band")
    latent = norm_gain.shape[1]
    width = hidden_bias.shape[1]
    embed_id = pair_out.shape[0] - 1
    band_mesh = mesh_pos.shape[1]
    band_grid = x_grid.shape[0]
    mesh_rows = band_mesh // quarters
    grid_rows = band_grid // quarters
    direct = bands <= 4
    part_index = lax.axis_index("parts")
    vmem, hbm, scalar = pltpu.VMEM, pltpu.HBM, pltpu.SMEM
    place = jnp.stack([feat_index, band_index, part_index]).astype(jnp.int32)

    bits = [1 << b for b in reversed(range(quarters.bit_length() - 1))]
    order = [0]
    for bit in bits:
        order = order + [other ^ bit for other in order]

    def swap(value, bit):
        return lax.ppermute(value, "feat", [(f, f ^ bit) for f in range(quarters)])

    def shift(value, step):
        return lax.ppermute(value, "band", [(b, (b + step) % bands) for b in range(bands)])

    def pieces(value):
        parts = [value]
        for bit in bits:
            parts = parts + [swap(part, bit) for part in parts]
        return parts

    def everyone(rows):
        if direct:
            parts = [rows] + [shift(rows, step) for step in range(1, bands)]
            for bit in bits:
                parts = parts + [swap(part, bit) for part in parts]
            return parts
        parts = [rows]
        for bit in bits[:-1]:
            parts = parts + [swap(part, bit) for part in parts]
        parts = [lax.all_gather(part, "band", axis=0, tiled=True) for part in parts]
        return parts + [swap(part, bits[-1]) for part in parts]

    caps = [take.shape[2] for take in (g2m_take, m2m_take, m2g_take)]
    direct = direct and all(cap % 128 == 0 for cap in caps)
    names = [v[None, :] for v in (g2m_from, m2m_from, m2g_from, g2m_to, m2m_to)]
    names, x_grid, place = lax.optimization_barrier((names, x_grid, place))
    hidden = kernel_call(
        functools.partial(embed_hidden, order, embed_id),
        [jax.ShapeDtypeStruct((width, latent), BF16)]
        + [jax.ShapeDtypeStruct((grid_rows, width), BF16)] * quarters
        + [jax.ShapeDtypeStruct((1, sum(caps)), jnp.int32)] * (bands if direct else 0),
        (place, x_grid.T, embed_in, pair_out, hidden_bias, g2m_take, m2m_take, m2g_take),
        (scalar, hbm, hbm, hbm, vmem, vmem, vmem, vmem),
        scratch=(
            pltpu.VMEM(x_grid.shape[::-1], BF16),
            pltpu.VMEM(embed_in.shape, BF16),
            pltpu.SemaphoreType.DMA((3,)),
        ),
        vmem=GRANT,
    )
    out_pieces = pieces(hidden[0])
    rows = hidden[1 + quarters :]
    hidden = [hidden[1]] + [swap(h, other) for h, other in zip(hidden[2:], order[1:])]

    sections = embed_id
    piece = (3 * latent + BIAS_ROWS, width)
    packed, *crossing = kernel_call(
        pack,
        [jax.ShapeDtypeStruct((sections, *piece), BF16)]
        + [jax.ShapeDtypeStruct(piece, BF16)] * (sections // 2),
        (place, pair_in, pair_out, hidden_bias),
        (scalar, hbm, vmem, vmem),
        scratch=(pltpu.SemaphoreType.DMA((sections + sections // 2,)),),
        vmem=20 << 20,
    )
    swapped = swap(packed, bits[1])

    if direct:
        tables = [rows[0]] + [shift(row, step) for step, row in enumerate(rows[1:], 1)]
    else:
        takes = [jnp.pad(t[0], ((0, 0), (0, -t.shape[2] % 128))) for t in (g2m_take, m2m_take, m2g_take)]
        tables = [
            lax.all_to_all(
                jnp.concatenate(takes, axis=1), "band", split_axis=0, concat_axis=0, tiled=True
            )
        ]
    edges = [names.shape[0] // quarters for names in (g2m_from, m2m_from, m2g_from)]
    columns = [jax.ShapeDtypeStruct((n, 1), jnp.int32) for n in edges + edges[:2]]
    lines = [jax.ShapeDtypeStruct((1, n), jnp.int32) for n in edges[:2]]
    shape = jax.ShapeDtypeStruct((mesh_rows, latent), BF16)
    routed = kernel_call(
        functools.partial(route, bits, direct, bands, caps, (grid_rows, mesh_rows, mesh_rows), edges),
        [*columns, *lines, shape],
        (place, *tables, *names, mesh_pos, pos_weight),
        (scalar,) + (vmem,) * (len(tables) + 7),
        vmem=24 << 20,
    )
    ids_g, ids_m, ids_d, col_g, col_m, row_g, row_m, mesh = routed
    grid = kernel_call(
        functools.partial(embed_finish, embed_id, quarters),
        jax.ShapeDtypeStruct((grid_rows, latent), BF16),
        (*hidden, *out_pieces, norm_gain, norm_shift),
        (vmem,) * (2 * quarters + 2),
    )

    def cross(group_id, after):
        first = crossing[group_id]
        if after is not None:
            first, _ = lax.optimization_barrier((first, after))
        return swap(first, bits[0])

    def share(first, after):
        if after is not None:
            first, _ = lax.optimization_barrier((first, after))
        second = lax.ppermute(first, "parts", [(0, 1), (1, 0)])
        return [first, second, swap(first, bits[1]), swap(second, bits[1])]

    def run(section_id, table, across, ids, own_latent, column, extra, last=False):
        rows = sum(part.shape[0] for part in table)
        edges = ids.shape[0]
        square = jax.ShapeDtypeStruct((latent, latent), BF16)
        columns = () if last else (column,)
        staged = kernel_call(
            functools.partial(stage, section_id // 2, last),
            [square] * 4
            + [jax.ShapeDtypeStruct((n, latent), F32) for n in (edges, own_latent.shape[0])],
            (place, packed, swapped, *across, own_latent, *columns),
            (scalar, hbm, hbm) + (vmem,) * (5 + len(columns)),
            scratch=[pltpu.VMEM((2, *piece), BF16)] * 2 + [pltpu.SemaphoreType.DMA((2,))],
            flops=4 * edges * latent * latent,
            vmem=20 << 20,
        )
        out_shape = jax.ShapeDtypeStruct(own_latent.shape, BF16)
        if last:
            out_shape = jax.ShapeDtypeStruct((head.shape[1], own_latent.shape[0]), F32)
        return kernel_call(
            functools.partial(phase, section_id, len(table), last),
            out_shape,
            (*table, ids, own_latent, *staged, norm_gain, norm_shift, extra),
            (vmem,) * (len(table) + 11),
            flops=2 * edges * latent * (rows + 3 * latent),
            vmem=(20 << 20) + rows * latent * 2,
        )

    def held(table):
        return table[2 * bands - 1] if direct else table[-1]

    across = share(cross(0, None), None)
    table = everyone(grid)
    later = cross(1, grid)
    mesh = run(0, table, across, ids_g, mesh, col_g, row_g)
    for layer_id in range(LAYERS):
        across = share(later, held(table))
        table = everyone(mesh)
        later = cross(2 + layer_id, mesh)
        mesh = run(2 + 2 * layer_id, table, across, ids_m, mesh, col_m, row_m)
    across = share(later, held(table))
    return run(2 * LAYERS + 2, everyone(mesh), across, ids_d, grid, None, head.T, True).T


def solution(mesh):
    return jax.shard_map(
        local,
        mesh=mesh,
        in_specs=(
            P(("parts", "band"), None),
            P(None, "band"),
            P(),
            P(None, "feat"),
            P(None, None, "feat"),
            P(None, "feat", None),
            P(None, "feat"),
            P(),
            P(),
            P(),
            P("band", None, None),
            P("band"),
            P("band"),
            P("band", None, None),
            P("band"),
            P("band"),
            P("band", None, None),
            P("band"),
        ),
        out_specs=P(("parts", "band", "feat"), None),
        check_vma=False,
    )
```

```python
import functools

import jax
import jax.numpy as jnp
from jax import lax
from jax.experimental import pallas as pl
from jax.experimental.pallas import tpu as pltpu
from jax.sharding import PartitionSpec as P

LAYERS = 2
EPSILON = 1e-05
CHUNK = 2048
BIAS_ROWS = 16
GRANT = 60 << 20
F32 = jnp.float32
BF16 = jnp.bfloat16


def layer_norm(values, gain_row, shift_row):
    average = jnp.mean(values, axis=-1, keepdims=True)
    centered = values - average
    variance = jnp.mean(centered * centered, axis=-1, keepdims=True)
    return centered * lax.rsqrt(variance + EPSILON) * gain_row + shift_row


def silu(values):
    return 0.5 * values * (1.0 + jnp.tanh(0.5 * values))


def dot(a, b):
    return jnp.dot(a, b, preferred_element_type=F32)


def kernel_call(body, out_shape, operands, spaces, scratch=(), outs=None, flops=0, vmem=24 << 20):
    if outs is None:
        outs = jax.tree.map(lambda _: pltpu.VMEM, out_shape)
    return pl.pallas_call(
        body,
        out_shape=out_shape,
        in_specs=[pl.BlockSpec(memory_space=space) for space in spaces],
        out_specs=jax.tree.map(lambda space: pl.BlockSpec(memory_space=space), outs),
        scratch_shapes=list(scratch),
        compiler_params=pltpu.CompilerParams(vmem_limit_bytes=vmem),
        cost_estimate=pl.CostEstimate(flops=flops, bytes_accessed=4 << 20, transcendentals=0),
    )(*operands)


def started(pairs, sem):
    copies = [pltpu.make_async_copy(src, dst, sem.at[i]) for i, (src, dst) in enumerate(pairs)]
    for copy in copies:
        copy.start()
    return copies


def wait_all(copies):
    for copy in copies:
        copy.wait()


def embed_hidden(order, section_id, place_ref, x_hbm, w_hbm, out_hbm, bias_ref, own_out, *refs):
    sends = refs[:-3]
    x_ref, w_ref, sem = refs[-3:]
    latent = out_hbm.shape[2]
    width = w_ref.shape[1]
    rows = own_out.shape[0]
    pairs = [(x_hbm, x_ref), (w_hbm, w_ref)]
    for out in sends:
        for b in range(0, latent, width):
            pairs.append((out_hbm.at[section_id, :, pl.ds(b, width)], out.at[pl.ds(b, width)]))
    copies = started(pairs, sem)
    wait_all(copies[:2])
    me = place_ref[0]
    bias = bias_ref[section_id : section_id + 1, :]
    first, second = sends
    _, across, core, diagonal = order
    for other, out, begin in (
        (across, first, latent + rows),
        (diagonal, first, latent),
        (core, second, latent),
        (0, own_out, 0),
    ):
        source = pl.multiple_of((me ^ other) * rows, rows)
        product = lax.dot_general(
            x_ref[:, pl.ds(source, rows)], w_ref[...], (((0,), (0,)), ((), ())), preferred_element_type=F32
        )
        out[pl.ds(begin, rows), :] = silu(product + bias).astype(BF16)
    wait_all(copies[2:])


def embed_finish(section_id, own_ref, out_ref, across, core, diagonal, gain, shift, out):
    rows, latent = out.shape
    width = own_ref.shape[1]
    hidden = [own_ref[...], across[pl.ds(latent + rows, rows), :]]
    hidden += [ref[pl.ds(latent, rows), :] for ref in (core, diagonal)]
    weights = [
        jnp.concatenate([ref[pl.ds(b, width), :] for b in range(0, latent, width)], axis=1)
        for ref in (out_ref, across, core, diagonal)
    ]
    product = dot(jnp.concatenate(hidden, axis=1), jnp.concatenate(weights, axis=0))
    row = slice(section_id, section_id + 1)
    out[...] = layer_norm(product, gain[row, :], shift[row, :]).astype(BF16)


def pack(place_ref, in_hbm, out_ref, bias_ref, packed, *refs):
    crossing, sem = refs[:-1], refs[-1]
    part = place_ref[2]
    inner, width = in_hbm.shape[1:]
    latent = out_ref.shape[2]
    targets = []
    pairs = []
    for i in range(packed.shape[0]):
        section_id = (i - i % 2) + (part if i % 2 == 0 else 1 - part)
        targets.append((section_id, [packed.at[i]] + ([crossing[i // 2]] if i % 2 == 0 else [])))
        pairs += [(in_hbm.at[section_id], out.at[pl.ds(0, inner)]) for out in targets[-1][1]]
    copies = started(pairs, sem)
    for section_id, outs in targets:
        rest = bias_ref[pl.ds(section_id, 1), :]
        index = lax.broadcasted_iota(jnp.int32, (BIAS_ROWS, width), 0)
        value = jnp.zeros((BIAS_ROWS, width), F32)
        for term in range(3):
            head = rest.astype(BF16).astype(F32)
            value = jnp.where(index == term, head, value)
            rest = rest - head
        second = out_ref[section_id]
        for out in outs:
            out[pl.ds(inner + latent, BIAS_ROWS), :] = value.astype(BF16)
            for b in range(0, latent, width):
                out[pl.ds(inner + b, width), :] = second[:, b : b + width]
    wait_all(copies)


def route(bits, direct, bands, caps, counts, edges, place_ref, *refs):
    tables = refs[: bands if direct else 1]
    from_g, from_m, from_d, to_g, to_m, pos, pos_w, *outs = refs[len(tables) :]
    ids_g, ids_m, ids_d, col_g, col_m, row_g, row_m, mesh_out = outs
    me, band = place_ref[0], place_ref[1]

    def column(row):
        return jnp.broadcast_to(row, (8, row.shape[1])).T[:, :1].astype(jnp.int32)

    begin = 0
    for cap, count, size, senders, out in zip(caps, counts, edges, (from_g, from_m, from_d), (ids_g, ids_m, ids_d)):
        padded = -(-cap // 128) * 128
        names = senders[:, pl.ds(pl.multiple_of(me * size, size), size)]
        total = jnp.zeros((16, size), F32)
        for s in range(bands):
            if direct:
                value = tables[s][pl.ds(band, 1), begin : begin + padded]
                source = jnp.where(band >= s, band - s, band - s + bands)
            else:
                value = tables[0][s : s + 1, begin : begin + padded]
                source = s
            other = (value >> (count.bit_length() - 1)) ^ me
            slot = jnp.zeros_like(other)
            for i, bit in enumerate(bits):
                slot = slot + jnp.where((other & bit) != 0, 1 << i, 0)
            value = (slot * bands + s) * count + (value & (count - 1))
            index = lax.broadcasted_iota(jnp.int32, (16, padded), 0)
            high = jnp.broadcast_to((value >> 7).astype(F32), index.shape)
            low = jnp.broadcast_to((value & 127).astype(F32), index.shape)
            digits = jnp.where(index == 0, high, jnp.where(index == 1, low, 0.0)).astype(BF16)
            slots = lax.broadcasted_iota(jnp.int32, (padded, size), 0)
            hot = jnp.where((slots + source * cap == names) & (slots < cap), 1.0, 0.0).astype(BF16)
            total = total + dot(digits, hot)
        out[...] = column(total[0:1] * 128.0 + total[1:2])
        begin += padded
    for size, rows, to, col, row in ((edges[0], mesh_out.shape[0], to_g, col_g, row_g), (edges[1], mesh_out.shape[0], to_m, col_m, row_m)):
        mine = to[:, pl.ds(pl.multiple_of(me * size, size), size)] - me * rows
        row[...] = mine
        col[...] = column(mine.astype(F32))
    rows = mesh_out.shape[0]
    mine = pos[:, pl.ds(pl.multiple_of(me * rows, rows), rows)]
    index = lax.broadcasted_iota(jnp.int32, (8, rows), 0)
    stacked = jnp.zeros((8, rows), F32)
    for t in range(3):
        stacked = jnp.where(index == t, mine[t : t + 1, :], stacked)
    turned = stacked.T
    mesh = turned[:, 0:1] * pos_w[0:1, :] + turned[:, 1:2] * pos_w[1:2, :]
    mesh_out[...] = (mesh + turned[:, 2:3] * pos_w[2:3, :]).astype(BF16)


def stage(group_id, last, *refs):
    place_ref, mine_hbm, other_hbm, *across, own_ref = refs[:8]
    rest = refs[8:]
    if not last:
        recv_col, *rest = rest
    w_send, w_out, w_agg, w_out2, recv_pre, node_pre, mine, other, sem = rest
    chosen = pl.ds(2 * group_id, 2)
    copies = started([(mine_hbm.at[chosen], mine), (other_hbm.at[chosen], other)], sem)
    x_first, y_second, cx_first, cy_second = across
    kinds = (
        [mine.at[0], x_first, other.at[0], cx_first],
        [mine.at[1], y_second, other.at[1], cy_second],
    )
    own = own_ref[...]
    rows, latent = own.shape
    width = mine.shape[2]
    edges = recv_pre.shape[0]
    if last:
        degree = edges // rows
        edge = lax.broadcasted_iota(jnp.int32, (edges, rows), 0)
        node = lax.broadcasted_iota(jnp.int32, (edges, rows), 1) * degree
        spread = (edge >= node) & (edge < node + degree)
    else:
        spread = recv_col[...] == lax.broadcasted_iota(jnp.int32, (edges, rows), 1)
    received = dot(spread.astype(BF16), own).astype(BF16)

    def bias(refs):
        terms = [ref[pl.ds(3 * latent, BIAS_ROWS), :].astype(F32) for ref in refs]
        return jnp.concatenate([(t[0:1] + t[1:2]) + t[2:3] for t in terms], axis=1)

    def fill(target, out, begin, refs):
        for slot, ref in enumerate(refs):
            columns = pl.ds(slot * width, width)
            target[:, columns] = ref[pl.ds(begin, latent), :]
            for b in range(0, latent, width):
                out[columns, pl.ds(b, width)] = ref[pl.ds(2 * latent + b, width), :]

    wait_all(copies)

    def emit(edge_kind):
        first, second = kinds[edge_kind], kinds[1 - edge_kind]
        fill(w_send, w_out, 0, first)
        fill(w_agg, w_out2, latent, second)
        weights = jnp.concatenate([ref[pl.ds(latent, latent), :] for ref in first], axis=1)
        recv_pre[...] = dot(received, weights) + bias(first)
        weights = jnp.concatenate([ref[pl.ds(0, latent), :] for ref in second], axis=1)
        node_pre[...] = dot(own, weights) + bias(second)

    part = place_ref[2]
    pl.when(part == 0)(functools.partial(emit, 0))
    pl.when(part == 1)(functools.partial(emit, 1))


def phase(section_id, tables, last, *refs):
    table_refs = refs[:tables]
    ids, own_ref, w_send, w_out, w_agg, w_out2, recv_pre, node_pre, gain, shift, extra, out = refs[tables:]
    rows, latent = own_ref.shape
    edges = ids.shape[0]
    chunks = [[]]
    held = 0
    for ref in table_refs:
        size = min(ref.shape[0], CHUNK)
        for begin in range(0, ref.shape[0], size):
            if held + size > CHUNK:
                chunks.append([])
                held = 0
            chunks[-1].append(ref[pl.ds(begin, size), :])
            held += size
    preact = recv_pre[...]
    sent = None
    start = 0
    for chunk in chunks:
        chunk = jnp.concatenate(chunk, axis=0) if len(chunk) > 1 else chunk[0]
        hot = ids[...] == lax.broadcasted_iota(jnp.int32, (edges, chunk.shape[0]), 1) + start
        term = dot(hot.astype(BF16), chunk)
        sent = term if sent is None else sent + term
        start += chunk.shape[0]
    preact = preact + dot(sent.astype(BF16), w_send[...])

    def finish(t, preact, weights):
        row = slice(section_id + t, section_id + t + 1)
        return layer_norm(dot(silu(preact).astype(BF16), weights[...]), gain[row, :], shift[row, :])

    messages = finish(0, preact, w_out).astype(BF16)
    if last:
        degree = edges // rows
        edge = lax.broadcasted_iota(jnp.int32, (rows, edges), 1)
        node = lax.broadcasted_iota(jnp.int32, (rows, edges), 0) * degree
        collect = (edge >= node) & (edge < node + degree)
    else:
        collect = lax.broadcasted_iota(jnp.int32, (rows, edges), 0) == extra[...]
    aggregate = dot(collect.astype(BF16), messages).astype(BF16)
    update = finish(1, node_pre[...] + dot(aggregate, w_agg[...]), w_out2)
    updated = (own_ref[...].astype(F32) + update).astype(BF16)
    if last:
        out[...] = lax.dot_general(
            extra[...], updated, (((1,), (1,)), ((), ())), preferred_element_type=F32
        )
    else:
        out[...] = updated


def local(
    x_grid,
    mesh_pos,
    pos_weight,
    embed_in,
    pair_in,
    pair_out,
    hidden_bias,
    norm_gain,
    norm_shift,
    head,
    g2m_take,
    g2m_from,
    g2m_to,
    m2m_take,
    m2m_from,
    m2m_to,
    m2g_take,
    m2g_from,
):
    quarters = lax.axis_size("feat")
    bands = lax.axis_size("band")
    feat_index = lax.axis_index("feat")
    band_index = lax.axis_index("band")
    latent = norm_gain.shape[1]
    width = hidden_bias.shape[1]
    embed_id = pair_out.shape[0] - 1
    band_mesh = mesh_pos.shape[1]
    band_grid = x_grid.shape[0]
    mesh_rows = band_mesh // quarters
    grid_rows = band_grid // quarters
    direct = bands <= 4
    part_index = lax.axis_index("parts")
    vmem, hbm, scalar = pltpu.VMEM, pltpu.HBM, pltpu.SMEM
    place = jnp.stack([feat_index, band_index, part_index]).astype(jnp.int32)

    bits = [1 << b for b in reversed(range(quarters.bit_length() - 1))]
    order = [0]
    for bit in bits:
        order = order + [other ^ bit for other in order]

    def swap(value, bit):
        return lax.ppermute(value, "feat", [(f, f ^ bit) for f in range(quarters)])

    def shift(value, step):
        return lax.ppermute(value, "band", [(b, (b + step) % bands) for b in range(bands)])

    def pieces(value):
        parts = [value]
        for bit in bits:
            parts = parts + [swap(part, bit) for part in parts]
        return parts

    def spread(rows):
        if direct:
            parts = [rows] + [shift(rows, step) for step in range(1, bands)]
            return parts + [swap(part, bits[0]) for part in parts]
        parts = [rows, swap(rows, bits[0])]
        return [lax.all_gather(part, "band", axis=0, tiled=True) for part in parts]

    def complete(parts, staged):
        last, _ = lax.optimization_barrier((parts[-1], staged))
        return parts + [swap(part, bits[1]) for part in parts[:-1] + [last]]

    caps = [take.shape[2] for take in (g2m_take, m2m_take, m2g_take)]
    direct = direct and all(cap % 128 == 0 for cap in caps)
    if direct:
        whole = jnp.concatenate([g2m_take[0], m2m_take[0], m2g_take[0]], axis=1)
        tables = [whole] + [shift(whole, step) for step in range(1, bands)]
    else:
        takes = [jnp.pad(t[0], ((0, 0), (0, -t.shape[2] % 128))) for t in (g2m_take, m2m_take, m2g_take)]
        tables = [
            lax.all_to_all(
                jnp.concatenate(takes, axis=1), "band", split_axis=0, concat_axis=0, tiled=True
            )
        ]
    names = [v[None, :] for v in (g2m_from, m2m_from, m2g_from, g2m_to, m2m_to)]
    names, place = lax.optimization_barrier((names, place))
    hidden, *sends = kernel_call(
        functools.partial(embed_hidden, order, embed_id),
        [jax.ShapeDtypeStruct((n, width), BF16) for n in (grid_rows, latent + 2 * grid_rows, latent + grid_rows)],
        (place, x_grid.T, embed_in, pair_out, hidden_bias),
        (scalar, hbm, hbm, hbm, vmem),
        scratch=(
            pltpu.VMEM(x_grid.shape[::-1], BF16),
            pltpu.VMEM(embed_in.shape, BF16),
            pltpu.SemaphoreType.DMA((2 + 2 * latent // width,)),
        ),
        vmem=GRANT,
    )
    met = swap(sends[0], bits[0])
    received = [met, swap(sends[1], bits[1]), swap(met, bits[1])]
    place_after, _ = lax.optimization_barrier((place, hidden))

    sections = embed_id
    piece = (3 * latent + BIAS_ROWS, width)
    packed, *crossing = kernel_call(
        pack,
        [jax.ShapeDtypeStruct((sections, *piece), BF16)]
        + [jax.ShapeDtypeStruct(piece, BF16)] * (sections // 2),
        (place_after, pair_in, pair_out, hidden_bias),
        (scalar, hbm, vmem, vmem),
        scratch=(pltpu.SemaphoreType.DMA((sections + sections // 2,)),),
        vmem=20 << 20,
    )
    edges = [v.shape[0] // quarters for v in (g2m_from, m2m_from, m2g_from)]
    columns = [jax.ShapeDtypeStruct((n, 1), jnp.int32) for n in edges + edges[:2]]
    lines = [jax.ShapeDtypeStruct((1, n), jnp.int32) for n in edges[:2]]
    shape = jax.ShapeDtypeStruct((mesh_rows, latent), BF16)
    received, tables = lax.optimization_barrier((received, tables))
    grid = kernel_call(
        functools.partial(embed_finish, embed_id),
        jax.ShapeDtypeStruct((grid_rows, latent), BF16),
        (hidden, sends[0], *received, norm_gain, norm_shift),
        (vmem,) * 7,
    )
    routed = kernel_call(
        functools.partial(route, bits, direct, bands, caps, (grid_rows, mesh_rows, mesh_rows), edges),
        [*columns, *lines, shape],
        (place, *tables, *names, mesh_pos, pos_weight),
        (scalar,) + (vmem,) * (len(tables) + 7),
        vmem=24 << 20,
    )
    ids_g, ids_m, ids_d, col_g, col_m, row_g, row_m, mesh = routed
    swapped = swap(lax.optimization_barrier((packed, grid))[0], bits[1])

    def cross(group_id, after):
        first = crossing[group_id]
        if after is not None:
            first, _ = lax.optimization_barrier((first, after))
        return swap(first, bits[0])

    def share(first, after):
        if after is not None:
            first, _ = lax.optimization_barrier((first, after))
        second = lax.ppermute(first, "parts", [(0, 1), (1, 0)])
        return [first, second, swap(first, bits[1]), swap(second, bits[1])]

    def run(section_id, parts, across, ids, own_latent, column, extra, last=False):
        edges = ids.shape[0]
        square = jax.ShapeDtypeStruct((latent, latent), BF16)
        columns = () if last else (column,)
        staged = kernel_call(
            functools.partial(stage, section_id // 2, last),
            [square] * 4
            + [jax.ShapeDtypeStruct((n, latent), F32) for n in (edges, own_latent.shape[0])],
            (place, packed, swapped, *across, own_latent, *columns),
            (scalar, hbm, hbm) + (vmem,) * (5 + len(columns)),
            scratch=[pltpu.VMEM((2, *piece), BF16)] * 2 + [pltpu.SemaphoreType.DMA((2,))],
            flops=4 * edges * latent * latent,
            vmem=20 << 20,
        )
        table = complete(parts, staged)
        rows = sum(part.shape[0] for part in table)
        out_shape = jax.ShapeDtypeStruct(own_latent.shape, BF16)
        if last:
            out_shape = jax.ShapeDtypeStruct((head.shape[1], own_latent.shape[0]), F32)
        return kernel_call(
            functools.partial(phase, section_id, len(table), last),
            out_shape,
            (*table, ids, own_latent, *staged, norm_gain, norm_shift, extra),
            (vmem,) * (len(table) + 11),
            flops=2 * edges * latent * (rows + 3 * latent),
            vmem=(20 << 20) + rows * latent * 2,
        )

    across = share(cross(0, met), None)
    parts = spread(grid)
    later = cross(1, parts[bands + 1] if direct else grid)
    mesh = run(0, parts, across, ids_g, mesh, col_g, row_g)
    for layer_id in range(LAYERS):
        across = share(later, parts[-1])
        parts = spread(mesh)
        later = cross(2 + layer_id, mesh)
        mesh = run(2 + 2 * layer_id, parts, across, ids_m, mesh, col_m, row_m)
    across = share(later, parts[-1])
    return run(2 * LAYERS + 2, spread(mesh), across, ids_d, grid, None, head.T, True).T


def solution(mesh):
    return jax.shard_map(
        local,
        mesh=mesh,
        in_specs=(
            P(("parts", "band"), None),
            P(None, "band"),
            P(),
            P(None, "feat"),
            P(None, None, "feat"),
            P(None, "feat", None),
            P(None, "feat"),
            P(),
            P(),
            P(),
            P("band", None, None),
            P("band"),
            P("band"),
            P("band", None, None),
            P("band"),
            P("band"),
            P("band", None, None),
            P("band"),
        ),
        out_specs=P(("parts", "band", "feat"), None),
        check_vma=False,
    )
```

```python
import functools

import jax
import jax.numpy as jnp
from jax import lax
from jax.experimental import pallas as pl
from jax.experimental.pallas import tpu as pltpu
from jax.sharding import PartitionSpec as P

LAYERS = 2
EPSILON = 1e-05
CHUNK = 2048
BIAS_ROWS = 16
GRANT = 60 << 20
F32 = jnp.float32
BF16 = jnp.bfloat16


def layer_norm(values, gain_row, shift_row):
    average = jnp.mean(values, axis=-1, keepdims=True)
    centered = values - average
    variance = jnp.mean(centered * centered, axis=-1, keepdims=True)
    return centered * lax.rsqrt(variance + EPSILON) * gain_row + shift_row


def silu(values):
    return 0.5 * values * (1.0 + jnp.tanh(0.5 * values))


def dot(a, b):
    return jnp.dot(a, b, preferred_element_type=F32)


def kernel_call(body, out_shape, operands, spaces, scratch=(), outs=None, flops=0, vmem=24 << 20):
    if outs is None:
        outs = jax.tree.map(lambda _: pltpu.VMEM, out_shape)
    return pl.pallas_call(
        body,
        out_shape=out_shape,
        in_specs=[pl.BlockSpec(memory_space=space) for space in spaces],
        out_specs=jax.tree.map(lambda space: pl.BlockSpec(memory_space=space), outs),
        scratch_shapes=list(scratch),
        compiler_params=pltpu.CompilerParams(vmem_limit_bytes=vmem),
        cost_estimate=pl.CostEstimate(flops=flops, bytes_accessed=4 << 20, transcendentals=0),
    )(*operands)


def started(pairs, sem):
    copies = [pltpu.make_async_copy(src, dst, sem.at[i]) for i, (src, dst) in enumerate(pairs)]
    for copy in copies:
        copy.start()
    return copies


def wait_all(copies):
    for copy in copies:
        copy.wait()


def embed_hidden(order, section_id, place_ref, x_hbm, w_hbm, out_hbm, bias_ref, own_out, *refs):
    sends = refs[:-3]
    x_ref, w_ref, sem = refs[-3:]
    latent = out_hbm.shape[2]
    width = w_ref.shape[1]
    rows = own_out.shape[0]
    pairs = [(x_hbm, x_ref), (w_hbm, w_ref)]
    for out in sends:
        for b in range(0, latent, width):
            pairs.append((out_hbm.at[section_id, :, pl.ds(b, width)], out.at[pl.ds(b, width)]))
    copies = started(pairs, sem)
    wait_all(copies[:2])
    me = place_ref[0]
    bias = bias_ref[section_id : section_id + 1, :]
    first, second = sends
    _, across, core, diagonal = order
    for other, out, begin in (
        (across, first, latent + rows),
        (diagonal, first, latent),
        (core, second, latent),
        (0, own_out, 0),
    ):
        source = pl.multiple_of((me ^ other) * rows, rows)
        product = lax.dot_general(
            x_ref[:, pl.ds(source, rows)], w_ref[...], (((0,), (0,)), ((), ())), preferred_element_type=F32
        )
        out[pl.ds(begin, rows), :] = silu(product + bias).astype(BF16)
    wait_all(copies[2:])


def embed_finish(section_id, own_ref, out_ref, across, core, diagonal, gain, shift, out):
    rows, latent = out.shape
    width = own_ref.shape[1]
    hidden = [own_ref[...], across[pl.ds(latent + rows, rows), :]]
    hidden += [ref[pl.ds(latent, rows), :] for ref in (core, diagonal)]
    weights = [
        jnp.concatenate([ref[pl.ds(b, width), :] for b in range(0, latent, width)], axis=1)
        for ref in (out_ref, across, core, diagonal)
    ]
    product = dot(jnp.concatenate(hidden, axis=1), jnp.concatenate(weights, axis=0))
    row = slice(section_id, section_id + 1)
    out[...] = layer_norm(product, gain[row, :], shift[row, :]).astype(BF16)


def pack(place_ref, in_hbm, out_ref, bias_ref, *refs):
    groups = (len(refs) - 2) // 2
    packed, bundle, crossing, sem = refs[:groups], refs[groups], refs[groups + 1 : -1], refs[-1]
    part = place_ref[2]
    inner, width = in_hbm.shape[1:]
    latent = out_ref.shape[2]
    targets = []
    pairs = []
    for i in range(2 * groups):
        section_id = (i - i % 2) + (part if i % 2 == 0 else 1 - part)
        outs = [packed[i // 2].at[i % 2]]
        if i % 2 == 0:
            outs.append(crossing[i // 2])
        if i > 1:
            outs.append(bundle.at[i - 2])
        targets.append((section_id, outs))
        pairs += [(in_hbm.at[section_id], out.at[pl.ds(0, inner)]) for out in targets[-1][1]]
    copies = started(pairs, sem)
    for section_id, outs in targets:
        rest = bias_ref[pl.ds(section_id, 1), :]
        index = lax.broadcasted_iota(jnp.int32, (BIAS_ROWS, width), 0)
        value = jnp.zeros((BIAS_ROWS, width), F32)
        for term in range(3):
            head = rest.astype(BF16).astype(F32)
            value = jnp.where(index == term, head, value)
            rest = rest - head
        second = out_ref[section_id]
        for out in outs:
            out[pl.ds(inner + latent, BIAS_ROWS), :] = value.astype(BF16)
            for b in range(0, latent, width):
                out[pl.ds(inner + b, width), :] = second[:, b : b + width]
    wait_all(copies)


def route(bits, direct, bands, caps, counts, edges, place_ref, *refs):
    tables = refs[: bands if direct else 1]
    from_g, from_m, from_d, to_g, to_m, pos, pos_w, *outs = refs[len(tables) :]
    ids_g, ids_m, ids_d, col_g, col_m, row_g, row_m, mesh_out = outs
    me, band = place_ref[0], place_ref[1]

    def column(row):
        return jnp.broadcast_to(row, (8, row.shape[1])).T[:, :1].astype(jnp.int32)

    begin = 0
    for cap, count, size, senders, out in zip(caps, counts, edges, (from_g, from_m, from_d), (ids_g, ids_m, ids_d)):
        padded = -(-cap // 128) * 128
        names = senders[:, pl.ds(pl.multiple_of(me * size, size), size)]
        total = jnp.zeros((16, size), F32)
        for s in range(bands):
            if direct:
                value = tables[s][pl.ds(band, 1), begin : begin + padded]
                source = jnp.where(band >= s, band - s, band - s + bands)
            else:
                value = tables[0][s : s + 1, begin : begin + padded]
                source = s
            other = (value >> (count.bit_length() - 1)) ^ me
            slot = jnp.zeros_like(other)
            for i, bit in enumerate(bits):
                slot = slot + jnp.where((other & bit) != 0, 1 << i, 0)
            value = (slot * bands + s) * count + (value & (count - 1))
            index = lax.broadcasted_iota(jnp.int32, (16, padded), 0)
            high = jnp.broadcast_to((value >> 7).astype(F32), index.shape)
            low = jnp.broadcast_to((value & 127).astype(F32), index.shape)
            digits = jnp.where(index == 0, high, jnp.where(index == 1, low, 0.0)).astype(BF16)
            slots = lax.broadcasted_iota(jnp.int32, (padded, size), 0)
            hot = jnp.where((slots + source * cap == names) & (slots < cap), 1.0, 0.0).astype(BF16)
            total = total + dot(digits, hot)
        out[...] = column(total[0:1] * 128.0 + total[1:2])
        begin += padded
    for size, rows, to, col, row in ((edges[0], mesh_out.shape[0], to_g, col_g, row_g), (edges[1], mesh_out.shape[0], to_m, col_m, row_m)):
        mine = to[:, pl.ds(pl.multiple_of(me * size, size), size)] - me * rows
        row[...] = mine
        col[...] = column(mine.astype(F32))
    rows = mesh_out.shape[0]
    mine = pos[:, pl.ds(pl.multiple_of(me * rows, rows), rows)]
    index = lax.broadcasted_iota(jnp.int32, (8, rows), 0)
    stacked = jnp.zeros((8, rows), F32)
    for t in range(3):
        stacked = jnp.where(index == t, mine[t : t + 1, :], stacked)
    turned = stacked.T
    mesh = turned[:, 0:1] * pos_w[0:1, :] + turned[:, 1:2] * pos_w[1:2, :]
    mesh_out[...] = (mesh + turned[:, 2:3] * pos_w[2:3, :]).astype(BF16)


def stage(begin, last, *refs):
    place_ref, mine, other_hbm, *across, own_ref = refs[:8]
    rest = refs[8:]
    if not last:
        recv_col, *rest = rest
    w_send, w_out, w_agg, w_out2, recv_pre, node_pre, other, sem = rest
    copies = started([(other_hbm.at[pl.ds(begin, 2)], other)], sem)
    x_first, y_second, cx_first, cy_second = across
    kinds = (
        [mine.at[0], x_first, other.at[0], cx_first],
        [mine.at[1], y_second, other.at[1], cy_second],
    )
    own = own_ref[...]
    rows, latent = own.shape
    width = mine.shape[2]
    edges = recv_pre.shape[0]
    if last:
        degree = edges // rows
        edge = lax.broadcasted_iota(jnp.int32, (edges, rows), 0)
        node = lax.broadcasted_iota(jnp.int32, (edges, rows), 1) * degree
        spread = (edge >= node) & (edge < node + degree)
    else:
        spread = recv_col[...] == lax.broadcasted_iota(jnp.int32, (edges, rows), 1)
    received = dot(spread.astype(BF16), own).astype(BF16)

    def bias(refs):
        terms = [ref[pl.ds(3 * latent, BIAS_ROWS), :].astype(F32) for ref in refs]
        return jnp.concatenate([(t[0:1] + t[1:2]) + t[2:3] for t in terms], axis=1)

    def fill(target, out, begin, refs):
        for slot, ref in enumerate(refs):
            columns = pl.ds(slot * width, width)
            target[:, columns] = ref[pl.ds(begin, latent), :]
            for b in range(0, latent, width):
                out[columns, pl.ds(b, width)] = ref[pl.ds(2 * latent + b, width), :]

    wait_all(copies)

    def emit(edge_kind):
        first, second = kinds[edge_kind], kinds[1 - edge_kind]
        fill(w_send, w_out, 0, first)
        fill(w_agg, w_out2, latent, second)
        weights = jnp.concatenate([ref[pl.ds(latent, latent), :] for ref in first], axis=1)
        recv_pre[...] = dot(received, weights) + bias(first)
        weights = jnp.concatenate([ref[pl.ds(0, latent), :] for ref in second], axis=1)
        node_pre[...] = dot(own, weights) + bias(second)

    part = place_ref[2]
    pl.when(part == 0)(functools.partial(emit, 0))
    pl.when(part == 1)(functools.partial(emit, 1))


def stack(*refs):
    begin = 0
    for ref in refs[:-1]:
        refs[-1][pl.ds(begin, ref.shape[0]), :] = ref[...]
        begin += ref.shape[0]


def phase(section_id, tables, segments, last, *refs):
    table_refs = refs[:tables]
    ids, own_ref, w_send, w_out, w_agg, w_out2, recv_pre, node_pre, gain, shift, extra, out = refs[tables:]
    rows, latent = own_ref.shape
    edges = ids.shape[0]
    chunks = [[]]
    held = 0
    for which, first, count in segments:
        size = min(count, CHUNK)
        for begin in range(first, first + count, size):
            if held + size > CHUNK:
                chunks.append([])
                held = 0
            chunks[-1].append(table_refs[which][pl.ds(begin, size), :])
            held += size
    preact = recv_pre[...]
    sent = None
    start = 0
    for chunk in chunks:
        chunk = jnp.concatenate(chunk, axis=0) if len(chunk) > 1 else chunk[0]
        hot = ids[...] == lax.broadcasted_iota(jnp.int32, (edges, chunk.shape[0]), 1) + start
        term = dot(hot.astype(BF16), chunk)
        sent = term if sent is None else sent + term
        start += chunk.shape[0]
    preact = preact + dot(sent.astype(BF16), w_send[...])

    def finish(t, preact, weights):
        row = slice(section_id + t, section_id + t + 1)
        return layer_norm(dot(silu(preact).astype(BF16), weights[...]), gain[row, :], shift[row, :])

    messages = finish(0, preact, w_out).astype(BF16)
    if last:
        degree = edges // rows
        edge = lax.broadcasted_iota(jnp.int32, (rows, edges), 1)
        node = lax.broadcasted_iota(jnp.int32, (rows, edges), 0) * degree
        collect = (edge >= node) & (edge < node + degree)
    else:
        collect = lax.broadcasted_iota(jnp.int32, (rows, edges), 0) == extra[...]
    aggregate = dot(collect.astype(BF16), messages).astype(BF16)
    update = finish(1, node_pre[...] + dot(aggregate, w_agg[...]), w_out2)
    updated = (own_ref[...].astype(F32) + update).astype(BF16)
    if last:
        out[...] = lax.dot_general(
            extra[...], updated, (((1,), (1,)), ((), ())), preferred_element_type=F32
        )
    else:
        out[...] = updated


def local(
    x_grid,
    mesh_pos,
    pos_weight,
    embed_in,
    pair_in,
    pair_out,
    hidden_bias,
    norm_gain,
    norm_shift,
    head,
    g2m_take,
    g2m_from,
    g2m_to,
    m2m_take,
    m2m_from,
    m2m_to,
    m2g_take,
    m2g_from,
):
    quarters = lax.axis_size("feat")
    bands = lax.axis_size("band")
    feat_index = lax.axis_index("feat")
    band_index = lax.axis_index("band")
    latent = norm_gain.shape[1]
    width = hidden_bias.shape[1]
    embed_id = pair_out.shape[0] - 1
    band_mesh = mesh_pos.shape[1]
    band_grid = x_grid.shape[0]
    mesh_rows = band_mesh // quarters
    grid_rows = band_grid // quarters
    direct = bands <= 4
    part_index = lax.axis_index("parts")
    vmem, hbm, scalar = pltpu.VMEM, pltpu.HBM, pltpu.SMEM
    place = jnp.stack([feat_index, band_index, part_index]).astype(jnp.int32)

    bits = [1 << b for b in reversed(range(quarters.bit_length() - 1))]
    order = [0]
    for bit in bits:
        order = order + [other ^ bit for other in order]

    def swap(value, bit):
        return lax.ppermute(value, "feat", [(f, f ^ bit) for f in range(quarters)])

    def shift(value, step):
        return lax.ppermute(value, "band", [(b, (b + step) % bands) for b in range(bands)])

    def pieces(value):
        parts = [value]
        for bit in bits:
            parts = parts + [swap(part, bit) for part in parts]
        return parts

    def spread(rows, opening, second, next_id):
        if direct:
            near = [rows] + [shift(rows, step) for step in range(1, bands)]
            far = [opening]
            following = cross(next_id, far[0]) if 2 * next_id < sections else None
            far.append(swap(near[1], bits[0]))
            late, _ = lax.optimization_barrier((near[2:], (second, following)))
            return near + far + [swap(part, bits[0]) for part in late], following
        parts = [rows, swap(rows, bits[0])]
        following = cross(next_id, rows) if 2 * next_id < sections else None
        return [lax.all_gather(part, "band", axis=0, tiled=True) for part in parts], following

    def stacked(parts):
        rows = sum(part.shape[0] for part in parts)
        return kernel_call(
            stack,
            jax.ShapeDtypeStruct((rows, latent), BF16),
            parts,
            (vmem,) * len(parts),
            vmem=8 << 20,
        )

    def complete(parts, staged):
        if not direct:
            table = parts + [swap(part, bits[1]) for part in parts]
            return table, [(i, 0, part.shape[0]) for i, part in enumerate(table)]
        near, far = parts[:bands], parts[bands:]
        far, _ = lax.optimization_barrier((far, staged))
        table = parts + [swap(stacked(near), bits[1]), swap(stacked(far), bits[1])]
        return table, [(i, 0, part.shape[0]) for i, part in enumerate(table)]

    caps = [take.shape[2] for take in (g2m_take, m2m_take, m2g_take)]
    direct = direct and all(cap % 128 == 0 for cap in caps)
    if direct:
        whole = jnp.concatenate([g2m_take[0], m2m_take[0], m2g_take[0]], axis=1)
        tables = [whole] + [shift(whole, step) for step in range(1, bands)]
    else:
        takes = [jnp.pad(t[0], ((0, 0), (0, -t.shape[2] % 128))) for t in (g2m_take, m2m_take, m2g_take)]
        tables = [
            lax.all_to_all(
                jnp.concatenate(takes, axis=1), "band", split_axis=0, concat_axis=0, tiled=True
            )
        ]
    names = [v[None, :] for v in (g2m_from, m2m_from, m2g_from, g2m_to, m2m_to)]
    names, place = lax.optimization_barrier((names, place))
    hidden, *sends = kernel_call(
        functools.partial(embed_hidden, order, embed_id),
        [jax.ShapeDtypeStruct((n, width), BF16) for n in (grid_rows, latent + 2 * grid_rows, latent + grid_rows)],
        (place, x_grid.T, embed_in, pair_out, hidden_bias),
        (scalar, hbm, hbm, hbm, vmem),
        scratch=(
            pltpu.VMEM(x_grid.shape[::-1], BF16),
            pltpu.VMEM(embed_in.shape, BF16),
            pltpu.SemaphoreType.DMA((2 + 2 * latent // width,)),
        ),
        vmem=GRANT,
    )
    met = swap(sends[0], bits[0])
    received = [met, swap(sends[1], bits[1]), swap(met, bits[1])]
    place_after, _ = lax.optimization_barrier((place, hidden))
    nearby = received[1]

    sections = embed_id
    piece = (3 * latent + BIAS_ROWS, width)
    packed = kernel_call(
        pack,
        [jax.ShapeDtypeStruct((2, *piece), BF16)] * (sections // 2)
        + [jax.ShapeDtypeStruct((sections - 2, *piece), BF16)]
        + [jax.ShapeDtypeStruct(piece, BF16)] * (sections // 2),
        (place_after, pair_in, pair_out, hidden_bias),
        (scalar, hbm, vmem, vmem),
        scratch=(pltpu.SemaphoreType.DMA((2 * sections - 2 + sections // 2,)),),
        vmem=GRANT,
    )
    edges = [v.shape[0] // quarters for v in (g2m_from, m2m_from, m2g_from)]
    columns = [jax.ShapeDtypeStruct((n, 1), jnp.int32) for n in edges + edges[:2]]
    lines = [jax.ShapeDtypeStruct((1, n), jnp.int32) for n in edges[:2]]
    shape = jax.ShapeDtypeStruct((mesh_rows, latent), BF16)
    bundle = packed[sections // 2]
    crossing = packed[sections // 2 + 1 :]

    def held(value, after):
        return lax.optimization_barrier((value, after))[0]

    def cross(group_id, after):
        first = crossing[group_id]
        if after is not None:
            first, _ = lax.optimization_barrier((first, after))
        return swap(first, bits[0])

    first = cross(0, nearby)
    swapped = swap(held(packed[0], met), bits[1])
    received, tables, first, swapped = lax.optimization_barrier((received, tables, first, swapped))
    grid = kernel_call(
        functools.partial(embed_finish, embed_id),
        jax.ShapeDtypeStruct((grid_rows, latent), BF16),
        (hidden, sends[0], *received, norm_gain, norm_shift),
        (vmem,) * 7,
    )
    routed = kernel_call(
        functools.partial(route, bits, direct, bands, caps, (grid_rows, mesh_rows, mesh_rows), edges),
        [*columns, *lines, shape],
        (place, *tables, *names, mesh_pos, pos_weight),
        (scalar,) + (vmem,) * (len(tables) + 7),
        vmem=24 << 20,
    )
    ids_g, ids_m, ids_d, col_g, col_m, row_g, row_m, mesh = routed
    def over(first, after):
        first, _ = lax.optimization_barrier((first, after))
        return lax.ppermute(first, "parts", [(0, 1), (1, 0)])

    def share(first, second, after):
        first, second, _ = lax.optimization_barrier((first, second, after))
        return [first, second, swap(first, bits[1]), swap(second, bits[1])]

    def run(section_id, parts, swapped, across, ids, own_latent, column, extra, last=False):
        edges = ids.shape[0]
        square = jax.ShapeDtypeStruct((latent, latent), BF16)
        columns = () if last else (column,)
        staged = kernel_call(
            functools.partial(stage, max(section_id - 2, 0), last),
            [square] * 4
            + [jax.ShapeDtypeStruct((n, latent), F32) for n in (edges, own_latent.shape[0])],
            (place, packed[section_id // 2], swapped, *across, own_latent, *columns),
            (scalar, vmem, hbm) + (vmem,) * (5 + len(columns)),
            scratch=(pltpu.VMEM((2, *piece), BF16), pltpu.SemaphoreType.DMA((1,))),
            flops=4 * edges * latent * latent,
            vmem=20 << 20,
        )
        table, segments = complete(parts, staged)
        rows = sum(part.shape[0] for part in table)
        out_shape = jax.ShapeDtypeStruct(own_latent.shape, BF16)
        if last:
            out_shape = jax.ShapeDtypeStruct((head.shape[1], own_latent.shape[0]), F32)
        return kernel_call(
            functools.partial(phase, section_id, len(table), segments, last),
            out_shape,
            (*table, ids, own_latent, *staged, norm_gain, norm_shift, extra),
            (vmem,) * (len(table) + 11),
            flops=2 * edges * latent * (rows + 3 * latent),
            vmem=(20 << 20) + rows * latent * 2,
        )

    def window(group_id, rows, first):
        opening = swap(rows, bits[0]) if direct else rows
        second = over(first, rows)
        parts, following = spread(rows, opening, second, group_id + 1)
        near = tuple(parts[: len(parts) // 2])
        after = near if following is not None else (near, opening)
        return parts, share(first, second, after), following

    parts, across, first = window(0, grid, first)
    bundled = swap(held(bundle, parts[len(parts) // 2]), bits[1])
    mesh = run(0, parts, swapped, across, ids_g, mesh, col_g, row_g)
    for layer_id in range(LAYERS):
        parts, across, first = window(1 + layer_id, mesh, first)
        mesh = run(2 + 2 * layer_id, parts, bundled, across, ids_m, mesh, col_m, row_m)
    parts, across, _ = window(LAYERS + 1, mesh, first)
    return run(2 * LAYERS + 2, parts, bundled, across, ids_d, grid, None, head.T, True).T


def solution(mesh):
    return jax.shard_map(
        local,
        mesh=mesh,
        in_specs=(
            P(("parts", "band"), None),
            P(None, "band"),
            P(),
            P(None, "feat"),
            P(None, None, "feat"),
            P(None, "feat", None),
            P(None, "feat"),
            P(),
            P(),
            P(),
            P("band", None, None),
            P("band"),
            P("band"),
            P("band", None, None),
            P("band"),
            P("band"),
            P("band", None, None),
            P("band"),
        ),
        out_specs=P(("parts", "band", "feat"), None),
        check_vma=False,
    )
```

```python
import functools

import jax
import jax.numpy as jnp
from jax import lax
from jax.experimental import pallas as pl
from jax.experimental.pallas import tpu as pltpu
from jax.sharding import PartitionSpec as P

LAYERS = 2
EPSILON = 1e-05
CHUNK = 2048
BIAS_ROWS = 16
GRANT = 60 << 20
F32 = jnp.float32
BF16 = jnp.bfloat16


def layer_norm(values, gain_row, shift_row):
    average = jnp.mean(values, axis=-1, keepdims=True)
    centered = values - average
    variance = jnp.mean(centered * centered, axis=-1, keepdims=True)
    return centered * lax.rsqrt(variance + EPSILON) * gain_row + shift_row


def silu(values):
    return 0.5 * values * (1.0 + jnp.tanh(0.5 * values))


def dot(a, b):
    return jnp.dot(a, b, preferred_element_type=F32)


def kernel_call(body, out_shape, operands, spaces, scratch=(), outs=None, flops=0, vmem=24 << 20):
    if outs is None:
        outs = jax.tree.map(lambda _: pltpu.VMEM, out_shape)
    return pl.pallas_call(
        body,
        out_shape=out_shape,
        in_specs=[pl.BlockSpec(memory_space=space) for space in spaces],
        out_specs=jax.tree.map(lambda space: pl.BlockSpec(memory_space=space), outs),
        scratch_shapes=list(scratch),
        compiler_params=pltpu.CompilerParams(vmem_limit_bytes=vmem),
        cost_estimate=pl.CostEstimate(flops=flops, bytes_accessed=4 << 20, transcendentals=0),
    )(*operands)


def started(pairs, sem):
    copies = [pltpu.make_async_copy(src, dst, sem.at[i]) for i, (src, dst) in enumerate(pairs)]
    for copy in copies:
        copy.start()
    return copies


def wait_all(copies):
    for copy in copies:
        copy.wait()


def embed_hidden(order, section_id, place_ref, x_hbm, w_hbm, out_hbm, bias_ref, own_out, *refs):
    sends = refs[:-3]
    x_ref, w_ref, sem = refs[-3:]
    latent = out_hbm.shape[2]
    width = w_ref.shape[1]
    rows = own_out.shape[0]
    pairs = [(x_hbm, x_ref), (w_hbm, w_ref)]
    for out in sends:
        for b in range(0, latent, width):
            pairs.append((out_hbm.at[section_id, :, pl.ds(b, width)], out.at[pl.ds(b, width)]))
    copies = started(pairs, sem)
    wait_all(copies[:2])
    me = place_ref[0]
    bias = bias_ref[section_id : section_id + 1, :]
    first, second = sends
    _, across, core, diagonal = order
    for other, out, begin in (
        (across, first, latent + rows),
        (diagonal, first, latent),
        (core, second, latent),
        (0, own_out, 0),
    ):
        source = pl.multiple_of((me ^ other) * rows, rows)
        product = lax.dot_general(
            x_ref[:, pl.ds(source, rows)], w_ref[...], (((0,), (0,)), ((), ())), preferred_element_type=F32
        )
        out[pl.ds(begin, rows), :] = silu(product + bias).astype(BF16)
    wait_all(copies[2:])


def embed_finish(section_id, own_ref, out_ref, across, core, diagonal, gain, shift, out):
    rows, latent = out.shape
    width = own_ref.shape[1]
    hidden = [own_ref[...], across[pl.ds(latent + rows, rows), :]]
    hidden += [ref[pl.ds(latent, rows), :] for ref in (core, diagonal)]
    weights = [
        jnp.concatenate([ref[pl.ds(b, width), :] for b in range(0, latent, width)], axis=1)
        for ref in (out_ref, across, core, diagonal)
    ]
    product = dot(jnp.concatenate(hidden, axis=1), jnp.concatenate(weights, axis=0))
    row = slice(section_id, section_id + 1)
    out[...] = layer_norm(product, gain[row, :], shift[row, :]).astype(BF16)


def pack(place_ref, in_hbm, out_ref, bias_ref, *refs):
    packed, *crossing, sem = refs
    part = place_ref[2]
    inner, width = in_hbm.shape[1:]
    latent = out_ref.shape[2]
    targets = []
    pairs = []
    for i in range(packed.shape[0]):
        section_id = (i - i % 2) + (part if i % 2 == 0 else 1 - part)
        outs = [packed.at[i]] + ([crossing[i // 2]] if i % 2 == 0 else [])
        targets.append((section_id, outs))
        pairs += [(in_hbm.at[section_id], out.at[pl.ds(0, inner)]) for out in targets[-1][1]]
    copies = started(pairs, sem)
    for section_id, outs in targets:
        rest = bias_ref[pl.ds(section_id, 1), :]
        index = lax.broadcasted_iota(jnp.int32, (BIAS_ROWS, width), 0)
        value = jnp.zeros((BIAS_ROWS, width), F32)
        for term in range(3):
            head = rest.astype(BF16).astype(F32)
            value = jnp.where(index == term, head, value)
            rest = rest - head
        second = out_ref[section_id]
        for out in outs:
            out[pl.ds(inner + latent, BIAS_ROWS), :] = value.astype(BF16)
            for b in range(0, latent, width):
                out[pl.ds(inner + b, width), :] = second[:, b : b + width]
    wait_all(copies)


def route(bits, direct, bands, caps, counts, edges, place_ref, *refs):
    tables = refs[: bands if direct else 1]
    from_g, from_m, from_d, to_g, to_m, pos, pos_w, *outs = refs[len(tables) :]
    ids_g, ids_m, ids_d, col_g, col_m, row_g, row_m, mesh_out = outs
    me, band = place_ref[0], place_ref[1]

    def column(row):
        return jnp.broadcast_to(row, (8, row.shape[1])).T[:, :1].astype(jnp.int32)

    begin = 0
    for cap, count, size, senders, out in zip(caps, counts, edges, (from_g, from_m, from_d), (ids_g, ids_m, ids_d)):
        padded = -(-cap // 128) * 128
        names = senders[:, pl.ds(pl.multiple_of(me * size, size), size)]
        total = jnp.zeros((16, size), F32)
        for s in range(bands):
            if direct:
                value = tables[s][pl.ds(band, 1), begin : begin + padded]
                source = jnp.where(band >= s, band - s, band - s + bands)
            else:
                value = tables[0][s : s + 1, begin : begin + padded]
                source = s
            other = (value >> (count.bit_length() - 1)) ^ me
            slot = jnp.zeros_like(other)
            for i, bit in enumerate(bits):
                slot = slot + jnp.where((other & bit) != 0, 1 << i, 0)
            value = (slot * bands + s) * count + (value & (count - 1))
            index = lax.broadcasted_iota(jnp.int32, (16, padded), 0)
            high = jnp.broadcast_to((value >> 7).astype(F32), index.shape)
            low = jnp.broadcast_to((value & 127).astype(F32), index.shape)
            digits = jnp.where(index == 0, high, jnp.where(index == 1, low, 0.0)).astype(BF16)
            slots = lax.broadcasted_iota(jnp.int32, (padded, size), 0)
            hot = jnp.where((slots + source * cap == names) & (slots < cap), 1.0, 0.0).astype(BF16)
            total = total + dot(digits, hot)
        out[...] = column(total[0:1] * 128.0 + total[1:2])
        begin += padded
    for size, rows, to, col, row in ((edges[0], mesh_out.shape[0], to_g, col_g, row_g), (edges[1], mesh_out.shape[0], to_m, col_m, row_m)):
        mine = to[:, pl.ds(pl.multiple_of(me * size, size), size)] - me * rows
        row[...] = mine
        col[...] = column(mine.astype(F32))
    rows = mesh_out.shape[0]
    mine = pos[:, pl.ds(pl.multiple_of(me * rows, rows), rows)]
    index = lax.broadcasted_iota(jnp.int32, (8, rows), 0)
    stacked = jnp.zeros((8, rows), F32)
    for t in range(3):
        stacked = jnp.where(index == t, mine[t : t + 1, :], stacked)
    turned = stacked.T
    mesh = turned[:, 0:1] * pos_w[0:1, :] + turned[:, 1:2] * pos_w[1:2, :]
    mesh_out[...] = (mesh + turned[:, 2:3] * pos_w[2:3, :]).astype(BF16)


def stage(begin, last, *refs):
    place_ref, mine_hbm, other_hbm, *across, own_ref = refs[:8]
    rest = refs[8:]
    if not last:
        recv_col, *rest = rest
    w_send, w_out, w_agg, w_out2, recv_pre, node_pre, mine, other, sem = rest
    copies = started([(ref.at[pl.ds(begin, 2)], out) for ref, out in ((mine_hbm, mine), (other_hbm, other))], sem)
    x_first, y_second, cx_first, cy_second = across
    kinds = (
        [mine.at[0], x_first, other.at[0], cx_first],
        [mine.at[1], y_second, other.at[1], cy_second],
    )
    own = own_ref[...]
    rows, latent = own.shape
    width = mine.shape[2]
    edges = recv_pre.shape[0]
    if last:
        degree = edges // rows
        edge = lax.broadcasted_iota(jnp.int32, (edges, rows), 0)
        node = lax.broadcasted_iota(jnp.int32, (edges, rows), 1) * degree
        spread = (edge >= node) & (edge < node + degree)
    else:
        spread = recv_col[...] == lax.broadcasted_iota(jnp.int32, (edges, rows), 1)
    received = dot(spread.astype(BF16), own).astype(BF16)

    def bias(refs):
        terms = [ref[pl.ds(3 * latent, BIAS_ROWS), :].astype(F32) for ref in refs]
        return jnp.concatenate([(t[0:1] + t[1:2]) + t[2:3] for t in terms], axis=1)

    def fill(target, out, begin, refs):
        for slot, ref in enumerate(refs):
            columns = pl.ds(slot * width, width)
            target[:, columns] = ref[pl.ds(begin, latent), :]
            for b in range(0, latent, width):
                out[columns, pl.ds(b, width)] = ref[pl.ds(2 * latent + b, width), :]

    wait_all(copies)

    def emit(edge_kind):
        first, second = kinds[edge_kind], kinds[1 - edge_kind]
        fill(w_send, w_out, 0, first)
        fill(w_agg, w_out2, latent, second)
        weights = jnp.concatenate([ref[pl.ds(latent, latent), :] for ref in first], axis=1)
        recv_pre[...] = dot(received, weights) + bias(first)
        weights = jnp.concatenate([ref[pl.ds(0, latent), :] for ref in second], axis=1)
        node_pre[...] = dot(own, weights) + bias(second)

    part = place_ref[2]
    pl.when(part == 0)(functools.partial(emit, 0))
    pl.when(part == 1)(functools.partial(emit, 1))


def stack(*refs):
    begin = 0
    for ref in refs[:-1]:
        refs[-1][pl.ds(begin, ref.shape[0]), :] = ref[...]
        begin += ref.shape[0]


def phase(section_id, tables, segments, last, *refs):
    table_refs = refs[:tables]
    ids, own_ref, w_send, w_out, w_agg, w_out2, recv_pre, node_pre, gain, shift, extra, out = refs[tables:]
    rows, latent = own_ref.shape
    edges = ids.shape[0]
    chunks = [[]]
    held = 0
    for which, first, count in segments:
        size = min(count, CHUNK)
        for begin in range(first, first + count, size):
            if held + size > CHUNK:
                chunks.append([])
                held = 0
            chunks[-1].append(table_refs[which][pl.ds(begin, size), :])
            held += size
    preact = recv_pre[...]
    sent = None
    start = 0
    for chunk in chunks:
        chunk = jnp.concatenate(chunk, axis=0) if len(chunk) > 1 else chunk[0]
        hot = ids[...] == lax.broadcasted_iota(jnp.int32, (edges, chunk.shape[0]), 1) + start
        term = dot(hot.astype(BF16), chunk)
        sent = term if sent is None else sent + term
        start += chunk.shape[0]
    preact = preact + dot(sent.astype(BF16), w_send[...])

    def finish(t, preact, weights):
        row = slice(section_id + t, section_id + t + 1)
        return layer_norm(dot(silu(preact).astype(BF16), weights[...]), gain[row, :], shift[row, :])

    messages = finish(0, preact, w_out).astype(BF16)
    if last:
        degree = edges // rows
        edge = lax.broadcasted_iota(jnp.int32, (rows, edges), 1)
        node = lax.broadcasted_iota(jnp.int32, (rows, edges), 0) * degree
        collect = (edge >= node) & (edge < node + degree)
    else:
        collect = lax.broadcasted_iota(jnp.int32, (rows, edges), 0) == extra[...]
    aggregate = dot(collect.astype(BF16), messages).astype(BF16)
    update = finish(1, node_pre[...] + dot(aggregate, w_agg[...]), w_out2)
    updated = (own_ref[...].astype(F32) + update).astype(BF16)
    if last:
        out[...] = lax.dot_general(
            extra[...], updated, (((1,), (1,)), ((), ())), preferred_element_type=F32
        )
    else:
        out[...] = updated


def local(
    x_grid,
    mesh_pos,
    pos_weight,
    embed_in,
    pair_in,
    pair_out,
    hidden_bias,
    norm_gain,
    norm_shift,
    head,
    g2m_take,
    g2m_from,
    g2m_to,
    m2m_take,
    m2m_from,
    m2m_to,
    m2g_take,
    m2g_from,
):
    quarters = lax.axis_size("feat")
    bands = lax.axis_size("band")
    feat_index = lax.axis_index("feat")
    band_index = lax.axis_index("band")
    latent = norm_gain.shape[1]
    width = hidden_bias.shape[1]
    embed_id = pair_out.shape[0] - 1
    band_mesh = mesh_pos.shape[1]
    band_grid = x_grid.shape[0]
    mesh_rows = band_mesh // quarters
    grid_rows = band_grid // quarters
    direct = bands <= 4
    part_index = lax.axis_index("parts")
    vmem, hbm, scalar = pltpu.VMEM, pltpu.HBM, pltpu.SMEM
    place = jnp.stack([feat_index, band_index, part_index]).astype(jnp.int32)

    bits = [1 << b for b in reversed(range(quarters.bit_length() - 1))]
    order = [0]
    for bit in bits:
        order = order + [other ^ bit for other in order]

    def swap(value, bit):
        return lax.ppermute(value, "feat", [(f, f ^ bit) for f in range(quarters)])

    def shift(value, step):
        return lax.ppermute(value, "band", [(b, (b + step) % bands) for b in range(bands)])

    def pieces(value):
        parts = [value]
        for bit in bits:
            parts = parts + [swap(part, bit) for part in parts]
        return parts

    def spread(rows, opening, second, next_id):
        if direct:
            near = [rows] + [shift(rows, step) for step in range(1, bands)]
            far = [opening]
            following = cross(next_id, far[0]) if 2 * next_id < sections else None
            far.append(swap(near[1], bits[0]))
            late, _ = lax.optimization_barrier((near[2:], (second, following)))
            return near + far + [swap(part, bits[0]) for part in late], following
        parts = [rows, swap(rows, bits[0])]
        following = cross(next_id, rows) if 2 * next_id < sections else None
        return [lax.all_gather(part, "band", axis=0, tiled=True) for part in parts], following

    def stacked(parts):
        rows = sum(part.shape[0] for part in parts)
        return kernel_call(
            stack,
            jax.ShapeDtypeStruct((rows, latent), BF16),
            parts,
            (vmem,) * len(parts),
            vmem=8 << 20,
        )

    def complete(parts, staged):
        if not direct:
            table = parts + [swap(part, bits[1]) for part in parts]
            return table, [(i, 0, part.shape[0]) for i, part in enumerate(table)]
        near, far = parts[:bands], parts[bands:]
        far, _ = lax.optimization_barrier((far, staged))
        table = parts + [swap(stacked(near), bits[1]), swap(stacked(far), bits[1])]
        return table, [(i, 0, part.shape[0]) for i, part in enumerate(table)]

    caps = [take.shape[2] for take in (g2m_take, m2m_take, m2g_take)]
    direct = direct and all(cap % 128 == 0 for cap in caps)
    takes = [take[0] for take in (g2m_take, m2m_take, m2g_take)]
    if not direct:
        takes = [jnp.pad(take, ((0, 0), (0, -take.shape[1] % 128))) for take in takes]
    whole = jnp.concatenate(takes, axis=1)
    names = [v[None, :] for v in (g2m_from, m2m_from, m2g_from, g2m_to, m2m_to)]
    names, whole, place = lax.optimization_barrier((names, whole, place))
    hidden, *sends = kernel_call(
        functools.partial(embed_hidden, order, embed_id),
        [jax.ShapeDtypeStruct((n, width), BF16) for n in (grid_rows, latent + 2 * grid_rows, latent + grid_rows)],
        (place, x_grid.T, embed_in, pair_out, hidden_bias),
        (scalar, hbm, hbm, hbm, vmem),
        scratch=(
            pltpu.VMEM(x_grid.shape[::-1], BF16),
            pltpu.VMEM(embed_in.shape, BF16),
            pltpu.SemaphoreType.DMA((2 + 2 * latent // width,)),
        ),
        vmem=GRANT,
    )
    met = swap(sends[0], bits[0])
    received = [met, swap(sends[1], bits[1]), swap(met, bits[1])]
    place_after, _ = lax.optimization_barrier((place, received[1]))
    nearby = received[1]

    sections = embed_id
    piece = (3 * latent + BIAS_ROWS, width)
    packed, *crossing = kernel_call(
        pack,
        [jax.ShapeDtypeStruct((sections, *piece), BF16)]
        + [jax.ShapeDtypeStruct(piece, BF16)] * (sections // 2),
        (place_after, pair_in, pair_out, hidden_bias),
        (scalar, hbm, vmem, vmem),
        scratch=(pltpu.SemaphoreType.DMA((sections + sections // 2,)),),
        vmem=GRANT,
    )
    edges = [v.shape[0] // quarters for v in (g2m_from, m2m_from, m2g_from)]
    columns = [jax.ShapeDtypeStruct((n, 1), jnp.int32) for n in edges + edges[:2]]
    lines = [jax.ShapeDtypeStruct((1, n), jnp.int32) for n in edges[:2]]
    shape = jax.ShapeDtypeStruct((mesh_rows, latent), BF16)

    def held(value, after):
        return lax.optimization_barrier((value, after))[0]

    def cross(group_id, after):
        first = crossing[group_id]
        if after is not None:
            first, _ = lax.optimization_barrier((first, after))
        return swap(first, bits[0])

    first = cross(0, nearby)
    swapped = swap(held(packed, met), bits[1])
    received, first = lax.optimization_barrier((received, first))
    grid = kernel_call(
        functools.partial(embed_finish, embed_id),
        jax.ShapeDtypeStruct((grid_rows, latent), BF16),
        (hidden, sends[0], *received, norm_gain, norm_shift),
        (vmem,) * 7,
    )
    def over(first, after):
        first, _ = lax.optimization_barrier((first, after))
        return lax.ppermute(first, "parts", [(0, 1), (1, 0)])

    def share(first, second, after):
        first, second, _ = lax.optimization_barrier((first, second, after))
        return [first, second, swap(first, bits[1]), swap(second, bits[1])]

    def run(section_id, parts, swapped, across, ids, own_latent, column, extra, last=False):
        edges = ids.shape[0]
        square = jax.ShapeDtypeStruct((latent, latent), BF16)
        columns = () if last else (column,)
        staged = kernel_call(
            functools.partial(stage, section_id, last),
            [square] * 4
            + [jax.ShapeDtypeStruct((n, latent), F32) for n in (edges, own_latent.shape[0])],
            (place, packed, swapped, *across, own_latent, *columns),
            (scalar, hbm, hbm) + (vmem,) * (5 + len(columns)),
            scratch=[pltpu.VMEM((2, *piece), BF16)] * 2 + [pltpu.SemaphoreType.DMA((2,))],
            flops=4 * edges * latent * latent,
            vmem=20 << 20,
        )
        table, segments = complete(parts, staged)
        rows = sum(part.shape[0] for part in table)
        out_shape = jax.ShapeDtypeStruct(own_latent.shape, BF16)
        if last:
            out_shape = jax.ShapeDtypeStruct((head.shape[1], own_latent.shape[0]), F32)
        return kernel_call(
            functools.partial(phase, section_id, len(table), segments, last),
            out_shape,
            (*table, ids, own_latent, *staged, norm_gain, norm_shift, extra),
            (vmem,) * (len(table) + 11),
            flops=2 * edges * latent * (rows + 3 * latent),
            vmem=(20 << 20) + rows * latent * 2,
        )

    def window(group_id, rows, first):
        opening = swap(rows, bits[0]) if direct else rows
        second = over(first, rows)
        parts, following = spread(rows, opening, second, group_id + 1)
        near = tuple(parts[: len(parts) // 2])
        after = near if following is not None else (near, opening)
        return parts, share(first, second, after), following

    parts, across, first = window(0, grid, first)
    if direct:
        whole = held(whole, tuple(parts[:bands]))
        tables = [whole] + [shift(whole, step) for step in range(1, bands)]
    else:
        tables = [lax.all_to_all(whole, "band", split_axis=0, concat_axis=0, tiled=True)]
    routed = kernel_call(
        functools.partial(route, bits, direct, bands, caps, (grid_rows, mesh_rows, mesh_rows), edges),
        [*columns, *lines, shape],
        (place, *tables, *names, mesh_pos, pos_weight),
        (scalar,) + (vmem,) * (len(tables) + 7),
        vmem=24 << 20,
    )
    ids_g, ids_m, ids_d, col_g, col_m, row_g, row_m, mesh = routed
    mesh = run(0, parts, swapped, across, ids_g, mesh, col_g, row_g)
    for layer_id in range(LAYERS):
        parts, across, first = window(1 + layer_id, mesh, first)
        mesh = run(2 + 2 * layer_id, parts, swapped, across, ids_m, mesh, col_m, row_m)
    parts, across, _ = window(LAYERS + 1, mesh, first)
    return run(2 * LAYERS + 2, parts, swapped, across, ids_d, grid, None, head.T, True).T


def solution(mesh):
    return jax.shard_map(
        local,
        mesh=mesh,
        in_specs=(
            P(("parts", "band"), None),
            P(None, "band"),
            P(),
            P(None, "feat"),
            P(None, None, "feat"),
            P(None, "feat", None),
            P(None, "feat"),
            P(),
            P(),
            P(),
            P("band", None, None),
            P("band"),
            P("band"),
            P("band", None, None),
            P("band"),
            P("band"),
            P("band", None, None),
            P("band"),
        ),
        out_specs=P(("parts", "band", "feat"), None),
        check_vma=False,
    )
```

```python
import functools

import jax
import jax.numpy as jnp
from jax import lax
from jax.experimental import pallas as pl
from jax.experimental.pallas import tpu as pltpu
from jax.sharding import PartitionSpec as P

LAYERS = 2
EPSILON = 1e-05
CHUNK = 2048
BIAS_ROWS = 16
GRANT = 60 << 20
F32 = jnp.float32
BF16 = jnp.bfloat16


def layer_norm(values, gain_row, shift_row):
    average = jnp.mean(values, axis=-1, keepdims=True)
    centered = values - average
    variance = jnp.mean(centered * centered, axis=-1, keepdims=True)
    return centered * lax.rsqrt(variance + EPSILON) * gain_row + shift_row


def silu(values):
    return 0.5 * values * (1.0 + jnp.tanh(0.5 * values))


def dot(a, b):
    return jnp.dot(a, b, preferred_element_type=F32)


def kernel_call(body, out_shape, operands, spaces, scratch=(), outs=None, flops=0, vmem=24 << 20):
    if outs is None:
        outs = jax.tree.map(lambda _: pltpu.VMEM, out_shape)
    return pl.pallas_call(
        body,
        out_shape=out_shape,
        in_specs=[pl.BlockSpec(memory_space=space) for space in spaces],
        out_specs=jax.tree.map(lambda space: pl.BlockSpec(memory_space=space), outs),
        scratch_shapes=list(scratch),
        compiler_params=pltpu.CompilerParams(vmem_limit_bytes=vmem),
        cost_estimate=pl.CostEstimate(flops=flops, bytes_accessed=4 << 20, transcendentals=0),
    )(*operands)


def started(pairs, sem):
    copies = [pltpu.make_async_copy(src, dst, sem.at[i]) for i, (src, dst) in enumerate(pairs)]
    for copy in copies:
        copy.start()
    return copies


def wait_all(copies):
    for copy in copies:
        copy.wait()


def embed_hidden(order, section_id, place_ref, x_hbm, w_hbm, out_hbm, bias_ref, own_out, *refs):
    sends = refs[:-3]
    x_ref, w_ref, sem = refs[-3:]
    latent = out_hbm.shape[2]
    width = w_ref.shape[1]
    rows = own_out.shape[0]
    pairs = [(x_hbm, x_ref), (w_hbm, w_ref)]
    for out in sends:
        for b in range(0, latent, width):
            pairs.append((out_hbm.at[section_id, :, pl.ds(b, width)], out.at[pl.ds(b, width)]))
    copies = started(pairs, sem)
    wait_all(copies[:2])
    me = place_ref[0]
    bias = bias_ref[section_id : section_id + 1, :]
    first, second = sends
    _, across, core, diagonal = order
    for other, out, begin in (
        (across, first, latent + rows),
        (diagonal, first, latent),
        (core, second, latent),
        (0, own_out, 0),
    ):
        source = pl.multiple_of((me ^ other) * rows, rows)
        product = lax.dot_general(
            x_ref[:, pl.ds(source, rows)], w_ref[...], (((0,), (0,)), ((), ())), preferred_element_type=F32
        )
        out[pl.ds(begin, rows), :] = silu(product + bias).astype(BF16)
    wait_all(copies[2:])


def embed_finish(section_id, own_ref, out_ref, across, core, diagonal, gain, shift, out):
    rows, latent = out.shape
    width = own_ref.shape[1]
    hidden = [own_ref[...], across[pl.ds(latent + rows, rows), :]]
    hidden += [ref[pl.ds(latent, rows), :] for ref in (core, diagonal)]
    weights = [
        jnp.concatenate([ref[pl.ds(b, width), :] for b in range(0, latent, width)], axis=1)
        for ref in (out_ref, across, core, diagonal)
    ]
    product = dot(jnp.concatenate(hidden, axis=1), jnp.concatenate(weights, axis=0))
    row = slice(section_id, section_id + 1)
    out[...] = layer_norm(product, gain[row, :], shift[row, :]).astype(BF16)


def pack(place_ref, in_hbm, out_ref, bias_ref, *refs):
    packed, *crossing, sem = refs
    part = place_ref[2]
    inner, width = in_hbm.shape[1:]
    latent = out_ref.shape[2]
    targets = []
    pairs = []
    for i in range(packed.shape[0]):
        section_id = (i - i % 2) + (part if i % 2 == 0 else 1 - part)
        outs = [packed.at[i]] + ([crossing[i // 2]] if i % 2 == 0 else [])
        targets.append((section_id, outs))
        pairs += [(in_hbm.at[section_id], out.at[pl.ds(0, inner)]) for out in targets[-1][1]]
    copies = started(pairs, sem)
    for section_id, outs in targets:
        rest = bias_ref[pl.ds(section_id, 1), :]
        index = lax.broadcasted_iota(jnp.int32, (BIAS_ROWS, width), 0)
        value = jnp.zeros((BIAS_ROWS, width), F32)
        for term in range(3):
            head = rest.astype(BF16).astype(F32)
            value = jnp.where(index == term, head, value)
            rest = rest - head
        second = out_ref[section_id]
        for out in outs:
            out[pl.ds(inner + latent, BIAS_ROWS), :] = value.astype(BF16)
            for b in range(0, latent, width):
                out[pl.ds(inner + b, width), :] = second[:, b : b + width]
    wait_all(copies)


def route(bits, direct, bands, caps, counts, edges, place_ref, *refs):
    tables = refs[: bands if direct else 1]
    from_g, from_m, from_d, to_g, to_m, pos, pos_w, *outs = refs[len(tables) :]
    ids_g, ids_m, ids_d, col_g, col_m, row_g, row_m, mesh_out = outs
    me, band = place_ref[0], place_ref[1]

    def column(row):
        return jnp.broadcast_to(row, (8, row.shape[1])).T[:, :1].astype(jnp.int32)

    begin = 0
    for cap, count, size, senders, out in zip(caps, counts, edges, (from_g, from_m, from_d), (ids_g, ids_m, ids_d)):
        padded = -(-cap // 128) * 128
        names = senders[:, pl.ds(pl.multiple_of(me * size, size), size)]
        total = jnp.zeros((16, size), F32)
        for s in range(bands):
            if direct:
                value = tables[s][pl.ds(band, 1), begin : begin + padded]
                source = jnp.where(band >= s, band - s, band - s + bands)
            else:
                value = tables[0][s : s + 1, begin : begin + padded]
                source = s
            other = (value >> (count.bit_length() - 1)) ^ me
            slot = jnp.zeros_like(other)
            for i, bit in enumerate(bits):
                slot = slot + jnp.where((other & bit) != 0, 1 << i, 0)
            value = (slot * bands + s) * count + (value & (count - 1))
            index = lax.broadcasted_iota(jnp.int32, (16, padded), 0)
            high = jnp.broadcast_to((value >> 7).astype(F32), index.shape)
            low = jnp.broadcast_to((value & 127).astype(F32), index.shape)
            digits = jnp.where(index == 0, high, jnp.where(index == 1, low, 0.0)).astype(BF16)
            slots = lax.broadcasted_iota(jnp.int32, (padded, size), 0)
            hot = jnp.where((slots + source * cap == names) & (slots < cap), 1.0, 0.0).astype(BF16)
            total = total + dot(digits, hot)
        out[...] = column(total[0:1] * 128.0 + total[1:2])
        begin += padded
    for size, rows, to, col, row in ((edges[0], mesh_out.shape[0], to_g, col_g, row_g), (edges[1], mesh_out.shape[0], to_m, col_m, row_m)):
        mine = to[:, pl.ds(pl.multiple_of(me * size, size), size)] - me * rows
        row[...] = mine
        col[...] = column(mine.astype(F32))
    rows = mesh_out.shape[0]
    mine = pos[:, pl.ds(pl.multiple_of(me * rows, rows), rows)]
    index = lax.broadcasted_iota(jnp.int32, (8, rows), 0)
    stacked = jnp.zeros((8, rows), F32)
    for t in range(3):
        stacked = jnp.where(index == t, mine[t : t + 1, :], stacked)
    turned = stacked.T
    mesh = turned[:, 0:1] * pos_w[0:1, :] + turned[:, 1:2] * pos_w[1:2, :]
    mesh_out[...] = (mesh + turned[:, 2:3] * pos_w[2:3, :]).astype(BF16)


def stage(begin, last, *refs):
    place_ref, mine_hbm, other_hbm, *across, own_ref = refs[:8]
    rest = refs[8:]
    if not last:
        recv_col, *rest = rest
    w_send, w_out, w_agg, w_out2, recv_pre, node_pre, mine, other, sem = rest
    copies = started([(ref.at[pl.ds(begin, 2)], out) for ref, out in ((mine_hbm, mine), (other_hbm, other))], sem)
    x_first, y_second, cx_first, cy_second = across
    kinds = (
        [mine.at[0], x_first, other.at[0], cx_first],
        [mine.at[1], y_second, other.at[1], cy_second],
    )
    own = own_ref[...]
    rows, latent = own.shape
    width = mine.shape[2]
    edges = recv_pre.shape[0]
    if last:
        degree = edges // rows
        edge = lax.broadcasted_iota(jnp.int32, (edges, rows), 0)
        node = lax.broadcasted_iota(jnp.int32, (edges, rows), 1) * degree
        spread = (edge >= node) & (edge < node + degree)
    else:
        spread = recv_col[...] == lax.broadcasted_iota(jnp.int32, (edges, rows), 1)
    received = dot(spread.astype(BF16), own).astype(BF16)

    def bias(refs):
        terms = [ref[pl.ds(3 * latent, BIAS_ROWS), :].astype(F32) for ref in refs]
        return jnp.concatenate([(t[0:1] + t[1:2]) + t[2:3] for t in terms], axis=1)

    def fill(target, out, begin, refs):
        for slot, ref in enumerate(refs):
            columns = pl.ds(slot * width, width)
            target[:, columns] = ref[pl.ds(begin, latent), :]
            for b in range(0, latent, width):
                out[columns, pl.ds(b, width)] = ref[pl.ds(2 * latent + b, width), :]

    wait_all(copies)

    def emit(edge_kind):
        first, second = kinds[edge_kind], kinds[1 - edge_kind]
        fill(w_send, w_out, 0, first)
        fill(w_agg, w_out2, latent, second)
        weights = jnp.concatenate([ref[pl.ds(latent, latent), :] for ref in first], axis=1)
        recv_pre[...] = dot(received, weights) + bias(first)
        weights = jnp.concatenate([ref[pl.ds(0, latent), :] for ref in second], axis=1)
        node_pre[...] = dot(own, weights) + bias(second)

    part = place_ref[2]
    pl.when(part == 0)(functools.partial(emit, 0))
    pl.when(part == 1)(functools.partial(emit, 1))


def stack(*refs):
    begin = 0
    for ref in refs[:-1]:
        refs[-1][pl.ds(begin, ref.shape[0]), :] = ref[...]
        begin += ref.shape[0]


def phase(section_id, tables, segments, last, *refs):
    table_refs = refs[:tables]
    ids, own_ref, w_send, w_out, w_agg, w_out2, recv_pre, node_pre, gain, shift, extra, out = refs[tables:]
    rows, latent = own_ref.shape
    edges = ids.shape[0]
    chunks = [[]]
    held = 0
    for which, first, count in segments:
        size = min(count, CHUNK)
        for begin in range(first, first + count, size):
            if held + size > CHUNK:
                chunks.append([])
                held = 0
            chunks[-1].append(table_refs[which][pl.ds(begin, size), :])
            held += size
    preact = recv_pre[...]
    sent = None
    start = 0
    for chunk in chunks:
        chunk = jnp.concatenate(chunk, axis=0) if len(chunk) > 1 else chunk[0]
        hot = ids[...] == lax.broadcasted_iota(jnp.int32, (edges, chunk.shape[0]), 1) + start
        term = dot(hot.astype(BF16), chunk)
        sent = term if sent is None else sent + term
        start += chunk.shape[0]
    preact = preact + dot(sent.astype(BF16), w_send[...])

    def finish(t, preact, weights):
        row = slice(section_id + t, section_id + t + 1)
        return layer_norm(dot(silu(preact).astype(BF16), weights[...]), gain[row, :], shift[row, :])

    messages = finish(0, preact, w_out).astype(BF16)
    if last:
        degree = edges // rows
        edge = lax.broadcasted_iota(jnp.int32, (rows, edges), 1)
        node = lax.broadcasted_iota(jnp.int32, (rows, edges), 0) * degree
        collect = (edge >= node) & (edge < node + degree)
    else:
        collect = lax.broadcasted_iota(jnp.int32, (rows, edges), 0) == extra[...]
    aggregate = dot(collect.astype(BF16), messages).astype(BF16)
    update = finish(1, node_pre[...] + dot(aggregate, w_agg[...]), w_out2)
    updated = (own_ref[...].astype(F32) + update).astype(BF16)
    if last:
        out[...] = lax.dot_general(
            extra[...], updated, (((1,), (1,)), ((), ())), preferred_element_type=F32
        )
    else:
        out[...] = updated


def local(
    x_grid,
    mesh_pos,
    pos_weight,
    embed_in,
    pair_in,
    pair_out,
    hidden_bias,
    norm_gain,
    norm_shift,
    head,
    g2m_take,
    g2m_from,
    g2m_to,
    m2m_take,
    m2m_from,
    m2m_to,
    m2g_take,
    m2g_from,
):
    quarters = lax.axis_size("feat")
    bands = lax.axis_size("band")
    feat_index = lax.axis_index("feat")
    band_index = lax.axis_index("band")
    latent = norm_gain.shape[1]
    width = hidden_bias.shape[1]
    embed_id = pair_out.shape[0] - 1
    band_mesh = mesh_pos.shape[1]
    band_grid = x_grid.shape[0]
    mesh_rows = band_mesh // quarters
    grid_rows = band_grid // quarters
    direct = bands <= 4
    part_index = lax.axis_index("parts")
    vmem, hbm, scalar = pltpu.VMEM, pltpu.HBM, pltpu.SMEM
    place = jnp.stack([feat_index, band_index, part_index]).astype(jnp.int32)

    bits = [1 << b for b in reversed(range(quarters.bit_length() - 1))]
    order = [0]
    for bit in bits:
        order = order + [other ^ bit for other in order]

    def swap(value, bit):
        return lax.ppermute(value, "feat", [(f, f ^ bit) for f in range(quarters)])

    def shift(value, step):
        return lax.ppermute(value, "band", [(b, (b + step) % bands) for b in range(bands)])

    def pieces(value):
        parts = [value]
        for bit in bits:
            parts = parts + [swap(part, bit) for part in parts]
        return parts

    def spread(rows, opening, second, next_id):
        if direct:
            near = [rows] + [shift(rows, step) for step in range(1, bands)]
            far = [opening]
            following = cross(next_id, far[0]) if 2 * next_id < sections else None
            far.append(swap(near[1], bits[0]))
            late, _ = lax.optimization_barrier((near[2:], (second, following)))
            return near + far + [swap(part, bits[0]) for part in late], following
        parts = [rows, swap(rows, bits[0])]
        following = cross(next_id, rows) if 2 * next_id < sections else None
        return [lax.all_gather(part, "band", axis=0, tiled=True) for part in parts], following

    def stacked(parts):
        rows = sum(part.shape[0] for part in parts)
        return kernel_call(
            stack,
            jax.ShapeDtypeStruct((rows, latent), BF16),
            parts,
            (vmem,) * len(parts),
            vmem=8 << 20,
        )

    def complete(parts, staged):
        if not direct:
            table = parts + [swap(part, bits[1]) for part in parts]
            return table, [(i, 0, part.shape[0]) for i, part in enumerate(table)]
        near, far = parts[:bands], parts[bands:]
        far, _ = lax.optimization_barrier((far, staged))
        table = parts + [swap(stacked(near), bits[1]), swap(stacked(far), bits[1])]
        return table, [(i, 0, part.shape[0]) for i, part in enumerate(table)]

    caps = [take.shape[2] for take in (g2m_take, m2m_take, m2g_take)]
    direct = direct and all(cap % 128 == 0 for cap in caps)
    takes = [take[0] for take in (g2m_take, m2m_take, m2g_take)]
    if not direct:
        takes = [jnp.pad(take, ((0, 0), (0, -take.shape[1] % 128))) for take in takes]
    whole = jnp.concatenate(takes, axis=1)
    names = [v[None, :] for v in (g2m_from, m2m_from, m2g_from, g2m_to, m2m_to)]
    names, whole, place = lax.optimization_barrier((names, whole, place))
    hidden, *sends = kernel_call(
        functools.partial(embed_hidden, order, embed_id),
        [jax.ShapeDtypeStruct((n, width), BF16) for n in (grid_rows, latent + 2 * grid_rows, latent + grid_rows)],
        (place, x_grid.T, embed_in, pair_out, hidden_bias),
        (scalar, hbm, hbm, hbm, vmem),
        scratch=(
            pltpu.VMEM(x_grid.shape[::-1], BF16),
            pltpu.VMEM(embed_in.shape, BF16),
            pltpu.SemaphoreType.DMA((2 + 2 * latent // width,)),
        ),
        vmem=GRANT,
    )
    met = swap(sends[0], bits[0])
    received = [met, swap(sends[1], bits[1]), swap(met, bits[1])]
    place_after, _ = lax.optimization_barrier((place, received[1]))
    nearby = received[1]

    sections = embed_id
    piece = (3 * latent + BIAS_ROWS, width)
    packed, *crossing = kernel_call(
        pack,
        [jax.ShapeDtypeStruct((sections, *piece), BF16)]
        + [jax.ShapeDtypeStruct(piece, BF16)] * (sections // 2),
        (place_after, pair_in, pair_out, hidden_bias),
        (scalar, hbm, vmem, vmem),
        scratch=(pltpu.SemaphoreType.DMA((sections + sections // 2,)),),
        vmem=GRANT,
    )
    edges = [v.shape[0] // quarters for v in (g2m_from, m2m_from, m2g_from)]
    columns = [jax.ShapeDtypeStruct((n, 1), jnp.int32) for n in edges + edges[:2]]
    lines = [jax.ShapeDtypeStruct((1, n), jnp.int32) for n in edges[:2]]
    shape = jax.ShapeDtypeStruct((mesh_rows, latent), BF16)

    def held(value, after):
        return lax.optimization_barrier((value, after))[0]

    def cross(group_id, after):
        first = crossing[group_id]
        if after is not None:
            first, _ = lax.optimization_barrier((first, after))
        return swap(first, bits[0])

    first = cross(0, nearby)
    received, _ = lax.optimization_barrier((received, place_after))
    grid = kernel_call(
        functools.partial(embed_finish, embed_id),
        jax.ShapeDtypeStruct((grid_rows, latent), BF16),
        (hidden, sends[0], *received, norm_gain, norm_shift),
        (vmem,) * 7,
    )
    def over(first, after):
        first, _ = lax.optimization_barrier((first, after))
        return lax.ppermute(first, "parts", [(0, 1), (1, 0)])

    swapped = swap(held(packed, grid), bits[1])

    def share(first, second, after):
        first, second, _ = lax.optimization_barrier((first, second, after))
        return [first, second, swap(first, bits[1]), swap(second, bits[1])]

    def run(section_id, parts, swapped, across, ids, own_latent, column, extra, last=False):
        edges = ids.shape[0]
        square = jax.ShapeDtypeStruct((latent, latent), BF16)
        columns = () if last else (column,)
        staged = kernel_call(
            functools.partial(stage, section_id, last),
            [square] * 4
            + [jax.ShapeDtypeStruct((n, latent), F32) for n in (edges, own_latent.shape[0])],
            (place, packed, swapped, *across, own_latent, *columns),
            (scalar, hbm, hbm) + (vmem,) * (5 + len(columns)),
            scratch=[pltpu.VMEM((2, *piece), BF16)] * 2 + [pltpu.SemaphoreType.DMA((2,))],
            flops=4 * edges * latent * latent,
            vmem=20 << 20,
        )
        table, segments = complete(parts, staged)
        rows = sum(part.shape[0] for part in table)
        out_shape = jax.ShapeDtypeStruct(own_latent.shape, BF16)
        if last:
            out_shape = jax.ShapeDtypeStruct((head.shape[1], own_latent.shape[0]), F32)
        return kernel_call(
            functools.partial(phase, section_id, len(table), segments, last),
            out_shape,
            (*table, ids, own_latent, *staged, norm_gain, norm_shift, extra),
            (vmem,) * (len(table) + 11),
            flops=2 * edges * latent * (rows + 3 * latent),
            vmem=(20 << 20) + rows * latent * 2,
        )

    def window(group_id, rows, first):
        opening = swap(rows, bits[0]) if direct else rows
        second = over(first, rows) if group_id > 0 else None
        parts, following = spread(rows, opening, second, group_id + 1)
        if second is None:
            second = over(first, tuple(parts[: len(parts) // 2]))
        near = tuple(parts[: len(parts) // 2])
        after = near if following is not None else (near, opening)
        return parts, share(first, second, after), following

    parts, across, first = window(0, grid, first)
    if direct:
        whole = held(whole, tuple(parts[:bands]))
        tables = [whole] + [shift(whole, step) for step in range(1, bands)]
    else:
        tables = [lax.all_to_all(whole, "band", split_axis=0, concat_axis=0, tiled=True)]
    routed = kernel_call(
        functools.partial(route, bits, direct, bands, caps, (grid_rows, mesh_rows, mesh_rows), edges),
        [*columns, *lines, shape],
        (place, *tables, *names, mesh_pos, pos_weight),
        (scalar,) + (vmem,) * (len(tables) + 7),
        vmem=24 << 20,
    )
    ids_g, ids_m, ids_d, col_g, col_m, row_g, row_m, mesh = routed
    mesh = run(0, parts, swapped, across, ids_g, mesh, col_g, row_g)
    for layer_id in range(LAYERS):
        parts, across, first = window(1 + layer_id, mesh, first)
        mesh = run(2 + 2 * layer_id, parts, swapped, across, ids_m, mesh, col_m, row_m)
    parts, across, _ = window(LAYERS + 1, mesh, first)
    return run(2 * LAYERS + 2, parts, swapped, across, ids_d, grid, None, head.T, True).T


def solution(mesh):
    return jax.shard_map(
        local,
        mesh=mesh,
        in_specs=(
            P(("parts", "band"), None),
            P(None, "band"),
            P(),
            P(None, "feat"),
            P(None, None, "feat"),
            P(None, "feat", None),
            P(None, "feat"),
            P(),
            P(),
            P(),
            P("band", None, None),
            P("band"),
            P("band"),
            P("band", None, None),
            P("band"),
            P("band"),
            P("band", None, None),
            P("band"),
        ),
        out_specs=P(("parts", "band", "feat"), None),
        check_vma=False,
    )
```
